128 devices in a mesh: section: 2 (over core), dp: 64 (over z, x, y).
Axes of the slice: x: 4, y: 4, z: 4, core: 2. Of those that a mesh axis runs over, the one named last changes fastest.
Arguments:
- ends_in: bfloat16 [2, 16384, 1536], P('section', 'dp'), may hold values from -6 to 6
- seg_ids: int32 [128, 128], P('dp'), may hold values from 0 to 2, never falling along the last dimension, each value on 1 to 96 neighbouring positions
- block_counts: int32 [128], P('dp'), may hold values from 64 to 128, as said below
- in_weight: bfloat16 [2, 1536, 6448], P('section', 'dp'), may hold values from -0.15625 to 0.15625
- conv_weight: bfloat16 [2, 4, 3328], P('section', None, 'dp'), may hold values from -3 to 3
- conv_bias: bfloat16 [2, 3328], P('section', 'dp'), may hold values from -1.5 to 1.5
- pre_gain: bfloat16 [2, 1536], P('section', 'dp'), may hold values from 0.5 to 1.5
- gate_gain: bfloat16 [2, 3072], P('section', 'dp'), may hold values from 0.5 to 1.5
- out_weight: bfloat16 [2, 3072, 1536], P('section', 'dp'), may hold values from -0.109375 to 0.109375
- dt_bias: bfloat16 [2, 48], P('section'), may hold values from -6.5 to -2.5
- a_log: bfloat16 [2, 48], P('section'), may hold values from 0 to 2.765625
- skip: bfloat16 [2, 48], P('section'), may hold values from 0.5 to 1.5
Outputs:
- ends_out: bfloat16 [2, 16384, 1536], P('section', 'dp')
- d_in_weight: float32 [2, 1536, 6448], P('section', 'dp')
- d_conv_weight: float32 [2, 4, 3328], P('section', None, 'dp')
- d_conv_bias: float32 [2, 3328], P('section', 'dp')
- d_pre_gain: float32 [2, 1536], P('section', 'dp')
- d_gate_gain: float32 [2, 3072], P('section', 'dp')
- d_out_weight: float32 [2, 3072, 1536], P('section', 'dp')
- d_dt_bias: float32 [2, 48], P('section')
- d_a_log: float32 [2, 48], P('section')
- d_skip: float32 [2, 48], P('section')
The draws below stay inside these ranges and needn't reach their ends.
Inputs may be any that keep to these rules, and one draw needn't show every extreme that they name: The first block_counts[b] slots of block b hold tokens, the rest are padding; some block is full and some holds 64. `seg_ids`: within a block the numbers never fall; one number is one packed sequence of at most 96 slots.
All inputs are finite; a program needn't handle non-finite values.
Results may differ from the reference program's by a relative error of at most 0.013.
Values may be sent and summed in bfloat16 or wider, within the bound.
A program may use at most 256 MiB of HBM per device.

```python
import math
import jax
import jax.numpy as jnp
import numpy as np
from jax import lax

D = 1536
DI = 3072
N = 128
HEAD_DIM = 64
KC = 4
MB_TOK = 128
H = 48
CC = 3328
E_IN = 6448
NBLK = 128
TOKENS = 16384


def draw_block_counts(key, part):
    key = jax.random.fold_in(key, 17)
    first_key, second_key = jax.random.split(key)
    counts = jax.random.randint(first_key, (NBLK,), MB_TOK // 2, MB_TOK + 1, dtype=jnp.int32)
    shuffled = jax.random.permutation(second_key, NBLK)
    counts = counts.at[shuffled[0]].set(MB_TOK)
    counts = counts.at[shuffled[1]].set(MB_TOK // 2)
    return counts.astype(jnp.int32)


def block_scale(own_key, dims, cuts, low, high):
    loudness = 1.0
    for position, parts in cuts:
        draws = jax.random.uniform(jax.random.fold_in(jax.random.fold_in(own_key, 6), position), (parts,), jnp.float32, low / len(cuts), high / len(cuts))
        loudness = loudness * jnp.repeat(jnp.exp(draws), dims[position] // parts).reshape((-1,) + (1,) * (len(dims) - 1 - position))
    return loudness


def split_up(count, total, most, lean):
    weights = [(1 << 20) // math.isqrt(standing ** lean) + 1 for standing in range(2, count + 1)]
    surplus, given = total - most - (count - 1), [1] * (count - 1)
    while surplus > 0:
        movable = [i for i in range(count - 1) if given[i] < most]
        pool, budget = sum([weights[i] for i in movable]), surplus
        for i in movable:
            addition = min(most - given[i], max(1, budget * weights[i] // pool), surplus)
            given[i] = given[i] + addition
            surplus = surplus - addition
    return np.array([most] + given)


def uneven_parts(stream_key, amount, total, limit, slope):
    if amount == 2:
        one = jax.random.randint(stream_key, (), max(1, total - limit), min(limit, total - 1) + 1)
        return jnp.stack([one, total - one])
    tallies = jnp.asarray(split_up(amount, total, limit, slope), jnp.int32)
    twos = (amount - 1) // 2
    donor, taker = tallies[1:1 + 2 * twos:2], tallies[2:2 + 2 * twos:2]
    room = jnp.minimum(donor - 1, limit - taker)
    moved = jax.random.randint(jax.random.fold_in(stream_key, 1), (twos,), 0, 1 << 20) % (room + 1)
    tallies = tallies.at[1:1 + 2 * twos:2].set(donor - moved).at[2:2 + 2 * twos:2].set(taker + moved)
    return tallies[jax.random.permutation(jax.random.fold_in(stream_key, 2), amount)]


def scatter_about(rng, dims, scale, bound, cuts=(), kind=jnp.bfloat16):
    level = block_scale(rng, dims, cuts, -0.22, 0.18) if cuts else 1.0
    drawn = jax.random.normal(rng, dims, jnp.float32) * scale * level
    return jnp.minimum(jnp.maximum(drawn, -bound), bound).astype(kind)


def setup_inputs(seed: int = 0) -> dict:
    splits = jax.random.split(jax.random.key(seed), 13)
    ends_in = scatter_about(splits[0], (2, TOKENS, D), 1.0, 6.0, ((0, 2), (1, 64)))
    seg_ids = jax.vmap(lambda own: jnp.searchsorted(jnp.cumsum(uneven_parts(own, 3, MB_TOK, MB_TOK * 3 // 4, 0)), jnp.arange(MB_TOK), side="right"))(jax.random.split(splits[1], NBLK)).reshape((NBLK, MB_TOK)).astype(jnp.int32)
    block_counts = draw_block_counts(jax.random.fold_in(splits[12], 71), 0)
    in_weight = scatter_about(splits[3], (2, D, E_IN), D ** -0.5, 0.15625, ((0, 2), (1, 64)))
    conv_weight = scatter_about(splits[4], (2, KC, CC), KC ** -0.5, 3.0, ((0, 2), (2, 64)))
    conv_bias = scatter_about(splits[5], (2, CC), 0.3, 1.5, ((0, 2), (1, 64)))
    pre_gain = jnp.clip(1.0 + 0.1 * jax.random.normal(splits[6], (2, D), jnp.float32), 0.5, 1.5).astype(jnp.bfloat16)
    gate_gain = jnp.clip(1.0 + 0.1 * jax.random.normal(splits[7], (2, DI), jnp.float32), 0.5, 1.5).astype(jnp.bfloat16)
    out_weight = scatter_about(splits[8], (2, DI, D), DI ** -0.5, 0.109375, ((0, 2), (1, 64)))
    dt_bias = jnp.clip(-6.5 + 4.0 * jax.random.uniform(splits[9], (2, H), jnp.float32) ** block_scale(splits[9], (2, H), ((0, 2),), -0.2, 0.2), -6.5, -2.5).astype(jnp.bfloat16)
    a_log = jnp.clip(2.765625 * jax.random.uniform(splits[10], (2, H), jnp.float32) ** block_scale(splits[10], (2, H), ((0, 2),), -0.2, 0.2), 0.0, 2.765625).astype(jnp.bfloat16)
    skip = jnp.clip(1.0 + 0.1 * jax.random.normal(splits[11], (2, H), jnp.float32), 0.5, 1.5).astype(jnp.bfloat16)
    return {"ends_in": ends_in, "seg_ids": seg_ids, "block_counts": block_counts, "in_weight": in_weight, "conv_weight": conv_weight, "conv_bias": conv_bias, "pre_gain": pre_gain, "gate_gain": gate_gain, "out_weight": out_weight, "dt_bias": dt_bias, "a_log": a_log, "skip": skip}


EPSILON = 1e-05
HIGHEST = lax.Precision.HIGHEST

@jax.custom_vjp
def low(v):
    return lax.optimization_barrier(v.astype(jnp.bfloat16)).astype(jnp.float32)

@jax.custom_vjp
def low_back(v):
    return v

def low_keep(v):
    return (low(v), None)

def low_pass(kept, grad):
    return (grad,)

def back_keep(v):
    return (v, None)

def back_low(kept, grad):
    return (low(grad),)
low.defvjp(low_keep, low_pass)
low_back.defvjp(back_keep, back_low)

def norm_piece(hidden, gain_in, valid_rows):
    return hidden * lax.rsqrt(lax.optimization_barrier(jnp.mean(hidden * hidden, axis=-1, keepdims=True)) + EPSILON) * gain_in * valid_rows[:, None]

def mix_piece(projected, kernel_taps, kernel_bias, rate_bias, decay_log, segment):
    length = projected.shape[0]
    gate_z = projected[:, :DI]
    channels = projected[:, DI:DI + CC]
    rate_raw = projected[:, DI + CC:]
    padded = jnp.concatenate([jnp.zeros((KC - 1, CC), jnp.float32), channels], axis=0)
    seg_pad = jnp.concatenate([jnp.full((KC - 1,), -1, jnp.int32), segment.astype(jnp.int32)], axis=0)
    convolved = jnp.zeros_like(channels) + kernel_bias[None, :]
    for offset in range(KC):
        same_segment = (seg_pad[offset:offset + length] == segment).astype(jnp.float32)
        convolved = convolved + kernel_taps[offset][None, :] * padded[offset:offset + length] * same_segment[:, None]
    activated = jax.nn.silu(convolved)
    heads_x = activated[:, :DI].reshape(length, DI // HEAD_DIM, HEAD_DIM)
    in_state = activated[:, DI:DI + N]
    out_state = activated[:, DI + N:]
    step_size = jax.nn.softplus(rate_raw + rate_bias[None, :])
    cumulative = jnp.cumsum(step_size * (-jnp.exp(decay_log))[None, :], axis=0)
    return (gate_z, heads_x, in_state, out_state, step_size, cumulative)

def weight_piece(scores, cumulative, step_size, segment):
    length = scores.shape[0]
    positions = jnp.arange(length, dtype=jnp.int32)
    allowed = (positions[:, None] >= positions[None, :]) & (segment[:, None] == segment[None, :])
    across = cumulative.T
    gaps = across[:, :, None] - across[:, None, :]
    decay = jnp.exp(jnp.where(allowed[None, :, :], gaps, 0.0)) * allowed[None, :, :].astype(jnp.float32)
    return scores[None, :, :] * decay * step_size.T[:, None, :]

def gate_piece(ssd_out, gate_z, gain_out):
    gated = ssd_out * jax.nn.silu(gate_z)
    return gated * lax.rsqrt(lax.optimization_barrier(jnp.mean(gated * gated, axis=-1, keepdims=True)) + EPSILON) * gain_out

def mixer_layer(hidden, valid_rows, segment, weights):
    proj_in, kernel_taps, kernel_bias, gain_in, gain_out, proj_out, rate_bias, decay_log, skip_gain = weights
    length = hidden.shape[0]
    normed_in = norm_piece(hidden, gain_in, valid_rows)
    projected = low_back(jnp.dot(low(normed_in), proj_in, precision=HIGHEST))
    gate_z, heads_x, in_state, out_state, step_size, cumulative = mix_piece(projected, kernel_taps, kernel_bias, rate_bias, decay_log, segment)
    scores = low_back(jnp.dot(low(out_state), low(in_state).T, precision=HIGHEST))
    mix_weights = low(weight_piece(scores, cumulative, step_size, segment))
    ssd_out = jnp.einsum('hts,shp->thp', mix_weights, low(heads_x), precision=HIGHEST) + skip_gain[None, :, None] * heads_x
    ssd_out = low_back(ssd_out.reshape(length, DI))
    normed = gate_piece(ssd_out, gate_z, gain_out)
    return hidden + low_back(jnp.dot(low(normed), proj_out, precision=HIGHEST))

def widen(value):
    return value.astype(jnp.float32)

def reference(ends_in, seg_ids, block_counts, in_weight, conv_weight, conv_bias, pre_gain, gate_gain, out_weight, dt_bias, a_log, skip):
    blocks_all = seg_ids.shape[0]
    length = seg_ids.shape[1]
    group_size = math.gcd(blocks_all, max(1, 4096 // length))
    groups = blocks_all // group_size
    inputs = widen(ends_in[0]).reshape(groups, group_size, length, D)
    cotangent = widen(ends_in[1]).reshape(groups, group_size, length, D)
    segments = seg_ids.astype(jnp.int32).reshape(groups, group_size, length)
    valid_all = (jnp.arange(length, dtype=jnp.int32)[None, :] < block_counts.astype(jnp.int32)[:, None]).astype(jnp.float32)
    valid_all = valid_all.reshape(groups, group_size, length)
    params = [widen(value) for value in (in_weight, conv_weight, conv_bias, pre_gain, gate_gain, out_weight, dt_bias, a_log, skip)]

    def run(inputs, params):
        first_layer = [value[0] for value in params]
        second_layer = [value[1] for value in params]

        def one_group(pieces):
            hidden, segment, valid_rows = pieces
            middle = jax.vmap(lambda a, b, c: mixer_layer(a, b, c, first_layer))(hidden, valid_rows, segment)
            middle = low(low_back(middle))
            return jax.vmap(lambda a, b, c: mixer_layer(a, b, c, second_layer))(middle, valid_rows, segment)
        return lax.map(jax.checkpoint(one_group), (inputs, segments, valid_all))
    result, pullback = jax.vjp(run, inputs, params)
    d_inputs, d_params = pullback(cotangent)
    ends_out = jnp.stack([d_inputs.reshape(blocks_all * length, D), result.reshape(blocks_all * length, D)]).astype(jnp.bfloat16)
    return (ends_out, d_params[0], d_params[1], d_params[2], d_params[3], d_params[4], d_params[5], d_params[6], d_params[7], d_params[8])
```

```python
import jax
import jax.numpy as jnp
from jax import lax
from jax.experimental import pallas as pl
from jax.experimental.pallas import tpu as pltpu
from jax.sharding import PartitionSpec as P

D = 1536
DI = 3072
N = 128
HEAD_DIM = 64
H = 48
KC = 4
CC = 3328
EPSILON = 1e-05
F32 = jnp.float32
BF = jnp.bfloat16


def to_panels(w):
    rows = w.shape[0]
    z, x = w[:, :DI], w[:, DI : 2 * DI]
    rates = jnp.pad(w[:, 2 * DI + 2 * N :], ((0, 0), (0, N - H)))
    extras = (w[:, 2 * DI : 2 * DI + N], w[:, 2 * DI + N : 2 * DI + 2 * N], rates)
    panels = []
    for j in range(3):
        pieces = []
        for g in (2 * j, 2 * j + 1):
            pieces += [z[:, 512 * g : 512 * g + 512], x[:, 512 * g : 512 * g + 512]]
        panels.append(jnp.concatenate(pieces + [extras[j]], axis=1))
    return panels


def from_panels(p):
    z = [p[g // 2][:, 1024 * (g % 2) : 1024 * (g % 2) + 512] for g in range(6)]
    x = [p[g // 2][:, 1024 * (g % 2) + 512 : 1024 * (g % 2) + 1024] for g in range(6)]
    extras = [p[0][:, 2048:], p[1][:, 2048:], p[2][:, 2048 : 2048 + H]]
    return jnp.concatenate(z + x + extras, axis=1)


def pack_small(taps, bias, gain_in, gain_out, heads):
    lead = taps.shape[:-2]
    wide = lambda v: jnp.pad(v, [(0, 0)] * (v.ndim - 1) + [(0, 128 - v.shape[-1])])
    pair = lambda a, b: jnp.concatenate([jnp.pad(a, [(0, 0)] * (a.ndim - 1) + [(0, 64 - a.shape[-1])]), jnp.pad(b, [(0, 0)] * (b.ndim - 1) + [(0, 64 - b.shape[-1])])], axis=-1)
    spread = [jnp.broadcast_to(h, lead + (H,)) for h in heads]
    rows = [wide(taps), wide(bias)[..., None, :], pair(gain_in, spread[1])[..., None, :], pair(gain_out, spread[2])[..., None, :], wide(spread[0])[..., None, :]]
    return jnp.concatenate(rows, axis=-2)


def unpack_small(s):
    taps = jnp.transpose(s[:, 0:4, 0:52], (1, 0, 2)).reshape(4, CC)
    return taps, s[:, 4, 0:52].reshape(CC), s[:, 5, 0:24].reshape(D), s[:, 6, 0:48].reshape(DI), (s[0, 7, 0:48], s[0, 5, 64:112], s[0, 6, 64:112])


MESH = pl.DeviceIdType.MESH
ORDERS = ((2, 1, 0), (1, 0, 2), (0, 2, 1))


def device(section, pos):
    return {"section": section, "dp": pos[0] * 16 + pos[1] * 4 + pos[2]}


def moved(pos, axis, by):
    out = list(pos)
    out[axis] = lax.rem(pos[axis] + by, 4)
    return tuple(out)


def block_index(order, phase, pos, half):
    index = [pos[0], pos[1], pos[2]]
    for a in order[:phase]:
        index[a] = slice(None)
    if phase > 0 and half is not None:
        a = min(order[:phase])
        index[a] = pl.ds(2 * half, 2)
    return tuple(index)


def gather_kernel(in_ref, out_ref, small_ref, gin, gout, gsmall, send, recv, local, dsend, drecv):
    section = lax.axis_index("section")
    dp = lax.axis_index("dp")
    pos = (lax.div(dp, 16), lax.rem(lax.div(dp, 4), 4), lax.rem(dp, 4))
    other = 1 - section

    barrier = pltpu.get_barrier_semaphore()
    for axis in range(3):
        for by in (1, 3):
            pl.semaphore_signal(barrier, inc=1, device_id=device(section, moved(pos, axis, by)), device_id_type=MESH)
    pl.semaphore_signal(barrier, inc=1, device_id=device(other, pos), device_id_type=MESH)
    pl.semaphore_wait(barrier, 7)

    streams = []
    for j in range(3):
        streams.append((in_ref.at[j], gin.at[section, j], ORDERS[j], 0))
        streams.append((out_ref.at[j], gout.at[section, j], ORDERS[j], 1))
    streams.append((small_ref, gsmall.at[section], ORDERS[0], 0))

    own = []
    for n, (src, dst, order, turn) in enumerate(streams):
        copy = pltpu.make_async_copy(src, dst.at[pos], local.at[n])
        copy.start()
        own.append(copy)

    sib = []

    def to_sibling(n, index, tag):
        dst = streams[n][1].at[index]
        copy = pltpu.make_async_remote_copy(dst, dst, dsend.at[n, tag], drecv.at[n, tag], device_id=device(other, pos), device_id_type=MESH)
        copy.start()
        sib.append((n, index, tag))

    def remote(n, phase, k, src, dst, to):
        return pltpu.make_async_remote_copy(src, dst, send.at[n, phase, k], recv.at[n, phase, k], device_id=device(section, to), device_id_type=MESH)

    def halves(n, phase, at):
        order, turn = streams[n][2], streams[n][3]
        if phase == 0:
            whole = block_index(order, 0, at, None)
            return (whole, None) if turn == 0 else (None, whole)
        return tuple(block_index(order, phase, at, h) for h in (0, 1))

    N = len(streams)
    for phase in range(3):
        started = []
        for n, (src, dst, order, turn) in enumerate(streams):
            axis = order[phase]
            right, left = moved(pos, axis, 1), moved(pos, axis, 3)
            mine = halves(n, phase, pos)
            for k, (h, to) in enumerate(((0, right), (1, left), (1, right), (0, left))):
                if mine[h] is None:
                    continue
                source = src if phase == 0 else dst.at[mine[h]]
                c = remote(n, phase, k, source, dst.at[mine[h]], to)
                c.start()
                started.append(c)
        if phase == 0:
            for c in own:
                c.wait()
        for n, (src, dst, order, turn) in enumerate(streams):
            axis = order[phase]
            right, left = moved(pos, axis, 1), moved(pos, axis, 3)
            for k, h, frm, to in ((0, 0, left, right), (1, 1, right, left)):
                got = halves(n, phase, frm)[h]
                if got is None:
                    continue
                remote(n, phase, k, dst.at[got], dst.at[got], to).wait_recv()
                c = remote(n, phase, 4 + k, dst.at[got], dst.at[got], to)
                c.start()
                started.append(c)
                if phase == 2:
                    to_sibling(n, got, 2 * k)
        for n, (src, dst, order, turn) in enumerate(streams):
            axis = order[phase]
            right, left = moved(pos, axis, 1), moved(pos, axis, 3)
            for k, h, frm in ((2, 1, left), (3, 0, right)):
                got = halves(n, phase, frm)[h]
                if got is None:
                    continue
                remote(n, phase, k, dst.at[got], dst.at[got], frm).wait_recv()
                if phase == 2:
                    to_sibling(n, got, 2 * (k - 2) + 1)
        if phase == 2:
            for n, (src, dst, order, turn) in enumerate(streams):
                to_sibling(n, block_index(order, 2, pos, None), 4)
        for n, (src, dst, order, turn) in enumerate(streams):
            axis = order[phase]
            far = moved(pos, axis, 2)
            for k, h in ((0, 0), (1, 1)):
                got = halves(n, phase, far)[h]
                if got is None:
                    continue
                remote(n, phase, 4 + k, dst.at[got], dst.at[got], far).wait_recv()
                if phase == 2:
                    to_sibling(n, got, 5 + k)
        for c in started:
            c.wait_send()
    theirs = [gin.at[other, 0], gout.at[other, 0], gin.at[other, 1], gout.at[other, 1], gin.at[other, 2], gout.at[other, 2], gsmall.at[other]]
    for n, index, tag in sib:
        mine = streams[n][1].at[index]
        pltpu.make_async_remote_copy(mine, theirs[n].at[index], dsend.at[n, tag], drecv.at[n, tag], device_id=device(other, pos), device_id_type=MESH).wait()


def gather(a_in, a_out, a_small):
    any_ = pl.BlockSpec(memory_space=pl.ANY)
    return pl.pallas_call(
        gather_kernel,
        out_shape=(
            jax.ShapeDtypeStruct((2, 3, 4, 4, 4) + a_in.shape[1:], a_in.dtype),
            jax.ShapeDtypeStruct((2, 3, 4, 4, 4) + a_out.shape[1:], a_out.dtype),
            jax.ShapeDtypeStruct((2, 4, 4, 4) + a_small.shape, a_small.dtype),
        ),
        in_specs=[any_] * 3,
        out_specs=(any_,) * 3,
        scratch_shapes=[
            pltpu.SemaphoreType.DMA((7, 3, 6)),
            pltpu.SemaphoreType.DMA((7, 3, 6)),
            pltpu.SemaphoreType.DMA((7,)),
            pltpu.SemaphoreType.DMA((7, 7)),
            pltpu.SemaphoreType.DMA((7, 7)),
        ],
        compiler_params=pltpu.CompilerParams(collective_id=0, has_side_effects=True),
        name="gather_weights",
    )(a_in, a_out, a_small)


def lead(n):
    return {2: 16, 1: 4, 0: 1}[n]


def scatter_kernel(win, wout, small, oin, oout, osmall, *scratch):
    got = {}
    it = iter(scratch)
    for phase in (2, 1, 0):
        for kind in (0, 1):
            got[phase, kind] = next(it)
    acc = {}
    for phase in (2, 1):
        for kind in (0, 1):
            acc[phase, kind] = next(it)
    mine = {kind: next(it) for kind in (0, 1)}
    sgot = {phase: next(it) for phase in (2, 1, 0)}
    sacc = {phase: next(it) for phase in (3, 2, 1)}
    send, recv, ssend, srecv, lsem, ssem = it

    section = lax.axis_index("section")
    dp = lax.axis_index("dp")
    pos = (lax.div(dp, 16), lax.rem(lax.div(dp, 4), 4), lax.rem(dp, 4))

    barrier = pltpu.get_barrier_semaphore()
    for axis in range(3):
        for by in (1, 2, 3):
            pl.semaphore_signal(barrier, inc=1, device_id=device(section, moved(pos, axis, by)), device_id_type=MESH)
    first = pltpu.make_async_copy(small, sacc[3], ssem.at[0])
    first.start()
    pl.semaphore_wait(barrier, 9)

    def small_phase(phase):
        axis = ORDERS[0][phase]
        here = pos[axis]
        cur = sacc[phase + 1]
        if phase == 2:
            first.wait()
        sends = []
        for by in (1, 2, 3):
            to = moved(pos, axis, by)
            c = pltpu.make_async_remote_copy(cur.at[to[axis]], sgot[phase].at[by - 1], ssend.at[phase, by - 1], srecv.at[phase, by - 1], device_id=device(section, to), device_id_type=MESH)
            c.start()
            sends.append(c)
        def finish():
            for c in sends:
                c.wait()
            total = cur[here] + sgot[phase][0] + sgot[phase][1] + sgot[phase][2]
            if phase == 0:
                osmall[...] = total
            else:
                sacc[phase][...] = total
        return finish

    def add_into(dst, parts, slices):
        def one(i, carry):
            dst(i, [p[i].astype(F32) for p in parts])
            return carry
        lax.fori_loop(0, slices, one, 0)

    refs = (win, wout)
    for phase in (2, 1, 0):
        half = {2: 8, 1: 2, 0: 1}[phase]
        streams = [(j, kind) for j in range(3) for kind in (0, 1)]

        def own(j, kind, k, h):
            order = ORDERS[j]
            axis = order[phase]
            if phase == 2:
                at = list(pos)
                at[axis] = k
                return refs[kind].at[(j,) + block_index(order, 2, tuple(at), h)]
            return acc[phase + 1, kind].at[j, k, pl.ds(half * h, half)] if phase == 1 else acc[1, kind].at[j, k]

        def have(kind, h):
            return phase != 0 or h == kind

        def slot_ref(j, kind, slot):
            return got[phase, kind].at[(j, slot, 0) if phase == 0 else (j, slot)]

        def copy(n, slot, src, to):
            j, kind = streams[n]
            return pltpu.make_async_remote_copy(src, slot_ref(j, kind, slot), send.at[phase, n, slot], recv.at[phase, n, slot], device_id=device(section, to), device_id_type=MESH)

        finish_small = small_phase(phase)
        started = []
        loads = []
        for n, (j, kind) in enumerate(streams):
            axis = ORDERS[j][phase]
            left, right, far = (moved(pos, axis, by)[axis] for by in (3, 1, 2))
            to_left, to_right = moved(pos, axis, 3), moved(pos, axis, 1)
            for slot, k, h, to in ((0, far, 0, to_left), (1, far, 1, to_right), (2, left, 1, to_left), (3, right, 0, to_right)):
                if have(kind, h):
                    c = copy(n, slot, own(j, kind, k, h), to)
                    c.start()
                    started.append(c)
            if phase == 2:
                for i, (k, h) in enumerate(((left, 0), (right, 1))):
                    c = pltpu.make_async_copy(own(j, kind, k, h), mine[kind].at[j, i], lsem.at[n, i])
                    c.start()
                    loads.append(c)
        for n, (j, kind) in enumerate(streams):
            axis = ORDERS[j][phase]
            left, right = (moved(pos, axis, by)[axis] for by in (3, 1))
            to_left, to_right = moved(pos, axis, 3), moved(pos, axis, 1)
            for i, (slot, k, h, to) in enumerate(((0, left, 0, to_left), (1, right, 1, to_right))):
                if not have(kind, h):
                    continue
                copy(n, slot, slot_ref(j, kind, slot), to).wait_recv()
                if phase == 2:
                    loads[2 * n + i].wait()
                    part = mine[kind].at[j, i]
                else:
                    part = own(j, kind, k, h)
                buf = slot_ref(j, kind, slot)
                sum_refs(buf, [part], buf, BF, phase)
                c = copy(n, 4 + i, buf, to)
                c.start()
                started.append(c)
                if phase == 2:
                    c = pltpu.make_async_copy(own(j, kind, pos[axis], h), mine[kind].at[j, i], lsem.at[n, i])
                    c.start()
                    loads[2 * n + i] = c
        finish_small()
        for n, (j, kind) in enumerate(streams):
            axis = ORDERS[j][phase]
            to_left = moved(pos, axis, 3)
            for h, slots in ((0, (3, 4)), (1, (2, 5))):
                if not have(kind, h):
                    continue
                for slot in slots:
                    copy(n, slot, slot_ref(j, kind, slot), to_left).wait_recv()
                if phase == 2:
                    loads[2 * n + h].wait()
                    part = mine[kind].at[j, h]
                else:
                    part = own(j, kind, pos[axis], h)
                a, b = (slot_ref(j, kind, s) for s in slots)
                if phase == 0:
                    out = (oin, oout)[kind].at[j]
                    out[...] = part[...].astype(F32) + a[...].astype(F32) + b[...].astype(F32)
                else:
                    final_sum(j, kind, phase, h, part, a, b, acc[phase, kind])
        for c in started:
            c.wait_send()


def sum_refs(a, others, dst, dtype, phase):
    shape = a.shape
    if len(shape) == 2:
        dst[...] = (a[...].astype(F32) + others[0][...].astype(F32)).astype(dtype)
        return
    if len(shape) == 3:
        def one(i, c):
            o = others[0][i] if len(others[0].shape) == 3 else others[0][...]
            dst[i] = (a[i].astype(F32) + o.astype(F32)).astype(dtype)
            return c
        lax.fori_loop(0, shape[0], one, 0)
        return
    def one(i, c):
        for q in range(shape[1]):
            dst[i, q] = (a[i, q].astype(F32) + others[0][i, q].astype(F32)).astype(dtype)
        return c
    lax.fori_loop(0, shape[0], one, 0)


def final_sum(j, kind, phase, h, part, a, b, acc):
    order = ORDERS[j]
    if phase == 1:
        def one(i, c):
            acc[j, 2 * h + i] = (part[i].astype(F32) + a[i].astype(F32) + b[i].astype(F32)).astype(BF)
            return c
        lax.fori_loop(0, 2, one, 0)
        return
    low = min(order[:2])
    def one(i, c):
        for q in range(4):
            first, second = 2 * h + i, q
            at = (first, second) if order[1] == low else (second, first)
            acc[j, at[0], at[1]] = (part[i, q].astype(F32) + a[i, q].astype(F32) + b[i, q].astype(F32)).astype(BF)
        return c
    lax.fori_loop(0, 2, one, 0)


def scatter(win, wout, small):
    any_ = pl.BlockSpec(memory_space=pl.ANY)
    vm = pl.BlockSpec(memory_space=pltpu.VMEM)
    ri, ci = win.shape[-2:]
    ro, co = wout.shape[-2:]
    dims = {0: (ri, ci), 1: (ro, co)}
    scratch = []
    for phase in (2, 1, 0):
        for kind in (0, 1):
            n = {2: (2, 4), 1: (2,), 0: (1,)}[phase]
            scratch.append(pltpu.VMEM((3, 6) + n + dims[kind], BF))
    for phase in (2, 1):
        for kind in (0, 1):
            n = {2: (4, 4), 1: (4,)}[phase]
            scratch.append(pltpu.VMEM((3,) + n + dims[kind], BF))
    for kind in (0, 1):
        scratch.append(pltpu.VMEM((3, 2, 2, 4) + dims[kind], BF))
    for n in ((4, 4), (4,), ()):
        scratch.append(pltpu.VMEM((3,) + n + (8, 128), F32))
    for n in ((4, 4, 4), (4, 4), (4,)):
        scratch.append(pltpu.VMEM(n + (8, 128), F32))
    scratch += [pltpu.SemaphoreType.DMA((3, 6, 6)), pltpu.SemaphoreType.DMA((3, 6, 6)), pltpu.SemaphoreType.DMA((3, 3)), pltpu.SemaphoreType.DMA((3, 3)), pltpu.SemaphoreType.DMA((6, 2)), pltpu.SemaphoreType.DMA((1,))]
    return pl.pallas_call(
        scatter_kernel,
        out_shape=(jax.ShapeDtypeStruct((3, ri, ci), F32), jax.ShapeDtypeStruct((3, ro, co), F32), jax.ShapeDtypeStruct((8, 128), F32)),
        in_specs=[any_] * 3,
        out_specs=(vm,) * 3,
        scratch_shapes=scratch,
        compiler_params=pltpu.CompilerParams(collective_id=1, has_side_effects=True, vmem_limit_bytes=62 * 1024 * 1024),
        name="scatter_grads",
    )(win, wout, small)


def norm_piece(hidden, gain_in, valid_rows):
    return (
        hidden
        * lax.rsqrt(jnp.mean(hidden * hidden, axis=-1, keepdims=True) + EPSILON)
        * gain_in
        * valid_rows[:, None]
    )


def mix_piece(projected, kernel_taps, kernel_bias, rate_bias, decay_log, segment):
    length = projected.shape[0]
    gate_z = projected[:, :DI]
    channels = projected[:, DI : DI + CC]
    rate_raw = projected[:, DI + CC :]
    padded = jnp.concatenate([jnp.zeros((KC - 1, CC), jnp.float32), channels], axis=0)
    seg_pad = jnp.concatenate([jnp.full((KC - 1,), -1, jnp.int32), segment], axis=0)
    convolved = jnp.zeros_like(channels) + kernel_bias[None, :]
    for offset in range(KC):
        same_segment = (seg_pad[offset : offset + length] == segment).astype(jnp.float32)
        convolved = (
            convolved
            + kernel_taps[offset][None, :]
            * padded[offset : offset + length]
            * same_segment[:, None]
        )
    activated = jax.nn.silu(convolved)
    heads_x = activated[:, :DI].reshape(length, DI // HEAD_DIM, HEAD_DIM)
    in_state = activated[:, DI : DI + N]
    out_state = activated[:, DI + N :]
    step_size = jax.nn.softplus(rate_raw + rate_bias[None, :])
    cumulative = jnp.cumsum(step_size * (-jnp.exp(decay_log))[None, :], axis=0)
    return (gate_z, heads_x, in_state, out_state, step_size, cumulative)


def weight_piece(scores, cumulative, step_size, segment):
    length = scores.shape[0]
    positions = jnp.arange(length, dtype=jnp.int32)
    allowed = (positions[:, None] >= positions[None, :]) & (segment[:, None] == segment[None, :])
    across = cumulative.T
    gaps = across[:, :, None] - across[:, None, :]
    decay = jnp.exp(jnp.where(allowed[None, :, :], gaps, 0.0)) * allowed[None, :, :].astype(
        jnp.float32
    )
    return scores[None, :, :] * decay * step_size.T[:, None, :]


def gate_piece(ssd_out, gate_z, gain_out):
    gated = ssd_out * jax.nn.silu(gate_z)
    return gated * lax.rsqrt(jnp.mean(gated * gated, axis=-1, keepdims=True) + EPSILON) * gain_out


def layer_parts(hidden, segment, valid_rows, weights, heads):
    proj_in, proj_out, kernel_taps, kernel_bias, gain_in, gain_out = weights
    rate_bias, decay_log, skip_gain = heads
    length = hidden.shape[0]
    normed_in, norm_pull = jax.vjp(
        lambda a, b: norm_piece(a, b, valid_rows), hidden, gain_in.astype(jnp.float32)
    )
    input_low = normed_in.astype(jnp.bfloat16)
    projected = from_panels([jnp.dot(input_low, w, preferred_element_type=jnp.float32) for w in proj_in])
    mixed, mix_pull = jax.vjp(
        lambda a, b, c, d, e: mix_piece(a, b, c, d, e, segment),
        projected,
        kernel_taps.astype(jnp.float32),
        kernel_bias.astype(jnp.float32),
        rate_bias,
        decay_log,
    )
    gate_z, heads_x, in_state, out_state, step_size, cumulative = mixed
    x_low = heads_x.astype(jnp.bfloat16)
    state_in_low = in_state.astype(jnp.bfloat16)
    state_out_low = out_state.astype(jnp.bfloat16)
    scores = jnp.dot(state_out_low, state_in_low.T, preferred_element_type=jnp.float32)
    mix_weights, weight_pull = jax.vjp(
        lambda a, b, c: weight_piece(a, b, c, segment), scores, cumulative, step_size
    )
    mix_low = mix_weights.astype(jnp.bfloat16)
    ssd_out = (
        jnp.einsum("hts,shp->thp", mix_low, x_low, preferred_element_type=jnp.float32)
        + skip_gain[None, :, None] * heads_x
    )
    ssd_out = ssd_out.reshape(length, DI)
    normed, gate_pull = jax.vjp(gate_piece, ssd_out, gate_z, gain_out.astype(jnp.float32))
    normed_low = normed.astype(jnp.bfloat16)
    return (
        input_low,
        norm_pull,
        mix_pull,
        heads_x,
        x_low,
        state_in_low,
        state_out_low,
        weight_pull,
        mix_low,
        gate_pull,
        normed_low,
    )


def out_product(low, panels):
    return jnp.concatenate([jnp.dot(low, w, preferred_element_type=jnp.float32) for w in panels], axis=1)


def layer_forward(hidden, segment, valid_rows, weights, heads):
    parts = layer_parts(hidden, segment, valid_rows, weights, heads)
    return hidden + out_product(parts[10], weights[1]), parts


def layer_backward(parts, upstream, weights, heads):
    proj_in, proj_out = (weights[0], weights[1])
    skip_gain = heads[2]
    length = upstream.shape[0]
    (
        input_low,
        norm_pull,
        mix_pull,
        heads_x,
        x_low,
        state_in_low,
        state_out_low,
        weight_pull,
        mix_low,
        gate_pull,
        normed_low,
    ) = parts
    upstream_low = upstream.astype(jnp.bfloat16)
    d_normed = sum(jnp.dot(upstream_low[:, 512 * j : 512 * j + 512], w.T, preferred_element_type=jnp.float32) for j, w in enumerate(proj_out))
    d_ssd, d_gate_z, d_gain_out = gate_pull(d_normed)
    d_ssd_low = d_ssd.astype(jnp.bfloat16).reshape(length, DI // HEAD_DIM, HEAD_DIM)
    d_ssd_wide = d_ssd_low.astype(jnp.float32)
    d_mix = jnp.einsum("thp,shp->hts", d_ssd_low, x_low, preferred_element_type=jnp.float32)
    d_heads_x = jnp.einsum("hts,thp->shp", mix_low, d_ssd_low, preferred_element_type=jnp.float32)
    d_heads_x = d_heads_x + skip_gain[None, :, None] * d_ssd_wide
    d_skip = jnp.sum(d_ssd_wide * heads_x, axis=(0, 2))
    d_scores, d_cumulative, d_step = weight_pull(d_mix)
    d_scores_low = d_scores.astype(jnp.bfloat16)
    d_out_state = jnp.dot(d_scores_low, state_in_low, preferred_element_type=jnp.float32)
    d_in_state = jnp.dot(d_scores_low.T, state_out_low, preferred_element_type=jnp.float32)
    d_projected, d_taps, d_kernel_bias, d_rate_bias, d_decay_log = mix_pull(
        (d_gate_z, d_heads_x, d_in_state, d_out_state, d_step, d_cumulative)
    )
    d_projected_low = d_projected.astype(jnp.bfloat16)
    d_panels = to_panels(d_projected_low)
    d_normed_in = sum(jnp.dot(d, w.T, preferred_element_type=jnp.float32) for d, w in zip(d_panels, proj_in))
    d_hidden, d_gain_in = norm_pull(d_normed_in)
    return (
        upstream + d_hidden,
        jnp.concatenate([input_low, normed_low, upstream_low] + d_panels, axis=1),
        (d_taps, d_kernel_bias, d_gain_in, d_gain_out, (d_rate_bias, d_decay_log, d_skip)),
    )


def spread_small(grads):
    taps, bias, gain_in, gain_out, heads = grads
    return pack_small(
        jnp.transpose(taps.reshape(4, 64, 52), (1, 0, 2)),
        bias.reshape(64, 52),
        gain_in.reshape(64, 24),
        gain_out.reshape(64, 48),
        heads,
    )


def body(
    ends_in,
    seg_ids,
    block_counts,
    in_weight,
    conv_weight,
    conv_bias,
    pre_gain,
    gate_gain,
    out_weight,
    dt_bias,
    a_log,
    skip,
):
    section = lax.axis_index("section")
    length = seg_ids.shape[1]
    wide = lambda v: v[0].astype(F32)
    small = pack_small(wide(conv_weight), wide(conv_bias), wide(pre_gain), wide(gate_gain), (wide(dt_bias), wide(a_log), wide(skip)))
    own_in = jnp.stack(to_panels(in_weight[0]))
    own_out = jnp.stack([out_weight[0][:, 512 * j : 512 * j + 512] for j in range(3)])
    all_in, all_out, all_small = gather(own_in, own_out, small)
    weights, heads = [], []
    for l in range(2):
        taps, bias, gain_in, gain_out, head = unpack_small(all_small[l].reshape(64, 8, 128))
        panels_in = [all_in[l, j].reshape(D, 2176) for j in range(3)]
        panels_out = [all_out[l, j].reshape(DI, 512) for j in range(3)]
        weights.append((panels_in, panels_out, taps, bias, gain_in, gain_out))
        heads.append(head)
    mine = lax.dynamic_index_in_dim(ends_in[0].reshape(2, length, D), section, 0, keepdims=False)
    theirs = lax.dynamic_index_in_dim(ends_in[0].reshape(2, length, D), 1 - section, 0, keepdims=False)
    swap = [(0, 1), (1, 0)]
    got = lax.ppermute(theirs, "section", swap)
    block_in = jnp.where(section == 0, mine, got).astype(F32)
    cotangent = jnp.where(section == 0, got, mine).astype(F32)
    segment = lax.dynamic_index_in_dim(seg_ids, section, 0, keepdims=False)
    count = lax.dynamic_index_in_dim(block_counts, section, 0, keepdims=False)
    valid_rows = (jnp.arange(length, dtype=jnp.int32) < count).astype(F32)

    first, first_parts = layer_forward(block_in, segment, valid_rows, weights[0], heads[0])
    middle = first.astype(BF).astype(F32)
    second, second_parts = layer_forward(middle, segment, valid_rows, weights[1], heads[1])
    d_middle, second_terms, second_small = layer_backward(second_parts, cotangent, weights[1], heads[1])
    d_middle = d_middle.astype(BF).astype(F32)
    d_first, first_terms, first_small = layer_backward(first_parts, d_middle, weights[0], heads[0])

    leading = section == 0
    keep = jnp.where(leading, first_terms, second_terms)
    got_terms = lax.ppermute(jnp.where(leading, second_terms, first_terms), "section", swap)
    terms = jnp.concatenate([keep, got_terms], axis=0)
    spread = [spread_small(first_small), spread_small(second_small)]
    small_sum = jnp.where(leading, spread[0], spread[1]) + lax.ppermute(jnp.where(leading, spread[1], spread[0]), "section", swap)
    d_first, second = d_first.astype(BF), second.astype(BF)
    end_got = lax.ppermute(jnp.where(leading, second, d_first), "section", swap)
    ends_out = jnp.where(leading, jnp.stack([d_first, end_got]), jnp.stack([end_got, second])).reshape(1, 2 * length, D)

    u, o, dv = terms[:, :D], terms[:, D : D + DI], terms[:, D + DI : 2 * D + DI]
    dp = terms[:, 2 * D + DI :]
    d_in = jnp.stack([jnp.dot(u.T, dp[:, 2176 * j : 2176 * j + 2176], preferred_element_type=F32).astype(BF) for j in range(3)]).reshape(3, 4, 4, 4, 24, 2176)
    d_out = jnp.stack([jnp.dot(o.T, dv[:, 512 * j : 512 * j + 512], preferred_element_type=F32).astype(BF) for j in range(3)]).reshape(3, 4, 4, 4, 48, 512)
    sum_in, sum_out, sums = scatter(d_in, d_out, small_sum.reshape(4, 4, 4, 8, 128))
    d_in_weight = from_panels([sum_in[j] for j in range(3)])
    d_out_weight = jnp.concatenate([sum_out[j] for j in range(3)], axis=1)
    return (
        ends_out,
        d_in_weight[None],
        sums[None, 0:4, 0:52],
        sums[None, 4, 0:52],
        sums[None, 5, 0:24],
        sums[None, 6, 0:48],
        d_out_weight[None],
        sums[None, 7, 0:48],
        sums[None, 5, 64:112],
        sums[None, 6, 64:112],
    )


def solution(mesh):
    placed = (
        P("section", "dp", None),
        P("dp", None),
        P("dp"),
        P("section", "dp", None),
        P("section", None, "dp"),
        P("section", "dp"),
        P("section", "dp"),
        P("section", "dp"),
        P("section", "dp", None),
        P("section", None),
        P("section", None),
        P("section", None),
    )
    return jax.shard_map(
        body,
        mesh=mesh,
        in_specs=placed,
        out_specs=(
            P("section", "dp", None),
            P("section", "dp", None),
            P("section", None, "dp"),
            P("section", "dp"),
            P("section", "dp"),
            P("section", "dp"),
            P("section", "dp", None),
            P("section", None),
            P("section", None),
            P("section", None),
        ),
        check_vma=False,
    )
```

```python
import jax
import jax.numpy as jnp
from jax import lax
from jax.experimental import pallas as pl
from jax.experimental.pallas import tpu as pltpu
from jax.sharding import PartitionSpec as P

D = 1536
DI = 3072
N = 128
HEAD_DIM = 64
H = 48
CC = 3328
EPSILON = 1e-05
F32 = jnp.float32
BF = jnp.bfloat16


def to_panels(w):
    rows = w.shape[0]
    z, x = w[:, :DI], w[:, DI : 2 * DI]
    rates = jnp.pad(w[:, 2 * DI + 2 * N :], ((0, 0), (0, N - H)))
    extras = (w[:, 2 * DI : 2 * DI + N], w[:, 2 * DI + N : 2 * DI + 2 * N], rates)
    panels = []
    for j in range(3):
        pieces = []
        for g in (2 * j, 2 * j + 1):
            pieces += [z[:, 512 * g : 512 * g + 512], x[:, 512 * g : 512 * g + 512]]
        panels.append(jnp.concatenate(pieces + [extras[j]], axis=1))
    return panels


def from_panels(p):
    z = [p[g // 2][:, 1024 * (g % 2) : 1024 * (g % 2) + 512] for g in range(6)]
    x = [p[g // 2][:, 1024 * (g % 2) + 512 : 1024 * (g % 2) + 1024] for g in range(6)]
    extras = [p[0][:, 2048:], p[1][:, 2048:], p[2][:, 2048 : 2048 + H]]
    return jnp.concatenate(z + x + extras, axis=1)


def pack_small(taps, bias, gain_in, gain_out, heads):
    lead = taps.shape[:-2]
    wide = lambda v: jnp.pad(v, [(0, 0)] * (v.ndim - 1) + [(0, 128 - v.shape[-1])])
    pair = lambda a, b: jnp.concatenate([jnp.pad(a, [(0, 0)] * (a.ndim - 1) + [(0, 64 - a.shape[-1])]), jnp.pad(b, [(0, 0)] * (b.ndim - 1) + [(0, 64 - b.shape[-1])])], axis=-1)
    spread = [jnp.broadcast_to(h, lead + (H,)) for h in heads]
    rows = [wide(taps), wide(bias)[..., None, :], pair(gain_in, spread[1])[..., None, :], pair(gain_out, spread[2])[..., None, :], wide(spread[0])[..., None, :]]
    return jnp.concatenate(rows, axis=-2)


def layer_params(s):
    rows = jnp.transpose(s[:, :, 0:5, 0:52], (0, 2, 1, 3)).reshape(2, 5, CC)
    gain_in, gain_out = s[:, :, 5, 0:24].reshape(2, 1, D), s[:, :, 6, 0:48].reshape(2, 6, 1, 512)
    rate_bias, decay_log, skip = s[:, 0, 7, 0:48], s[:, 0, 5, 64:112], s[:, 0, 6, 64:112]
    skip = jnp.repeat(skip, HEAD_DIM, axis=1).reshape(2, 6, 1, 512)
    x_rows = jnp.transpose(rows[:, :, :DI].reshape(2, 5, 6, 512), (0, 2, 1, 3))
    pg = jnp.concatenate([x_rows, gain_out, skip, jnp.zeros_like(skip)], axis=2)
    pe = jnp.pad(jnp.transpose(rows[:, :, DI:].reshape(2, 5, 2, N), (0, 2, 1, 3)), ((0, 0), (0, 0), (0, 3), (0, 0)))
    ph = jnp.pad(jnp.stack([rate_bias, decay_log], axis=1), ((0, 0), (0, 6), (0, N - H)))
    pn = jnp.pad(gain_in, ((0, 0), (0, 7), (0, 0)))
    return pg, pe, ph, pn


def small_grads(sg, se, sh, sn):
    rows = jnp.concatenate([jnp.transpose(sg[:, :, 0:5], (0, 2, 1, 3)).reshape(2, 5, DI), jnp.transpose(se[:, :, 0:5], (0, 2, 1, 3)).reshape(2, 5, 2 * N)], axis=2)
    rows = jnp.transpose(rows.reshape(2, 5, 64, 52), (0, 2, 1, 3))
    gain_in, gain_out = sn[:, 0].reshape(2, 64, 24), sg[:, :, 5].reshape(2, 64, 48)
    skip = jnp.sum(sg[:, :, 6].reshape(2, H, HEAD_DIM), axis=2)
    heads = [v[:, None] for v in (sh[:, 0, :H], sh[:, 1, :H], skip)]
    return pack_small(rows[:, :, 0:4], rows[:, :, 4], gain_in, gain_out, heads)


MESH = pl.DeviceIdType.MESH
ORDERS = ((2, 1, 0), (1, 0, 2), (0, 2, 1))


def device(section, pos):
    return {"section": section, "dp": pos[0] * 16 + pos[1] * 4 + pos[2]}


def moved(pos, axis, by):
    out = list(pos)
    out[axis] = lax.rem(pos[axis] + by, 4)
    return tuple(out)


def block_index(order, phase, pos, half):
    index = [pos[0], pos[1], pos[2]]
    for a in order[:phase]:
        index[a] = slice(None)
    if phase > 0 and half is not None:
        a = min(order[:phase])
        index[a] = pl.ds(2 * half, 2)
    return tuple(index)


def gather_kernel(in_ref, out_ref, small_ref, gin, gout, gsmall, send, recv, local, dsend, drecv):
    section = lax.axis_index("section")
    dp = lax.axis_index("dp")
    pos = (lax.div(dp, 16), lax.rem(lax.div(dp, 4), 4), lax.rem(dp, 4))
    other = 1 - section

    barrier = pltpu.get_barrier_semaphore()
    for axis in range(3):
        for by in (1, 3):
            pl.semaphore_signal(barrier, inc=1, device_id=device(section, moved(pos, axis, by)), device_id_type=MESH)
    pl.semaphore_signal(barrier, inc=1, device_id=device(other, pos), device_id_type=MESH)
    pl.semaphore_wait(barrier, 7)

    streams = []
    for j in range(3):
        streams.append((in_ref.at[j], gin.at[section, j], ORDERS[j], 0))
        streams.append((out_ref.at[j], gout.at[section, j], ORDERS[j], 1))
    streams.append((small_ref, gsmall.at[section], ORDERS[0], 0))

    own = []
    for n, (src, dst, order, turn) in enumerate(streams):
        copy = pltpu.make_async_copy(src, dst.at[pos], local.at[n])
        copy.start()
        own.append(copy)

    sib = []

    def to_sibling(n, index, tag):
        dst = streams[n][1].at[index]
        copy = pltpu.make_async_remote_copy(dst, dst, dsend.at[n, tag], drecv.at[n, tag], device_id=device(other, pos), device_id_type=MESH)
        copy.start()
        sib.append((n, index, tag))

    def remote(n, phase, k, src, dst, to):
        return pltpu.make_async_remote_copy(src, dst, send.at[n, phase, k], recv.at[n, phase, k], device_id=device(section, to), device_id_type=MESH)

    def halves(n, phase, at):
        order, turn = streams[n][2], streams[n][3]
        if phase == 0:
            whole = block_index(order, 0, at, None)
            return (whole, None) if turn == 0 else (None, whole)
        return tuple(block_index(order, phase, at, h) for h in (0, 1))

    N = len(streams)
    for phase in range(3):
        started = []
        for n, (src, dst, order, turn) in enumerate(streams):
            axis = order[phase]
            right, left = moved(pos, axis, 1), moved(pos, axis, 3)
            mine = halves(n, phase, pos)
            for k, (h, to) in enumerate(((0, right), (1, left), (1, right), (0, left))):
                if mine[h] is None:
                    continue
                source = src if phase == 0 else dst.at[mine[h]]
                c = remote(n, phase, k, source, dst.at[mine[h]], to)
                c.start()
                started.append(c)
        if phase == 0:
            for c in own:
                c.wait()
        for n, (src, dst, order, turn) in enumerate(streams):
            axis = order[phase]
            right, left = moved(pos, axis, 1), moved(pos, axis, 3)
            for k, h, frm, to in ((0, 0, left, right), (1, 1, right, left)):
                got = halves(n, phase, frm)[h]
                if got is None:
                    continue
                remote(n, phase, k, dst.at[got], dst.at[got], to).wait_recv()
                c = remote(n, phase, 4 + k, dst.at[got], dst.at[got], to)
                c.start()
                started.append(c)
                if phase == 2:
                    to_sibling(n, got, 2 * k)
        for n, (src, dst, order, turn) in enumerate(streams):
            axis = order[phase]
            right, left = moved(pos, axis, 1), moved(pos, axis, 3)
            for k, h, frm in ((2, 1, left), (3, 0, right)):
                got = halves(n, phase, frm)[h]
                if got is None:
                    continue
                remote(n, phase, k, dst.at[got], dst.at[got], frm).wait_recv()
                if phase == 2:
                    to_sibling(n, got, 2 * (k - 2) + 1)
        if phase == 2:
            for n, (src, dst, order, turn) in enumerate(streams):
                to_sibling(n, block_index(order, 2, pos, None), 4)
        for n, (src, dst, order, turn) in enumerate(streams):
            axis = order[phase]
            far = moved(pos, axis, 2)
            for k, h in ((0, 0), (1, 1)):
                got = halves(n, phase, far)[h]
                if got is None:
                    continue
                remote(n, phase, 4 + k, dst.at[got], dst.at[got], far).wait_recv()
                if phase == 2:
                    to_sibling(n, got, 5 + k)
        for c in started:
            c.wait_send()
    theirs = [gin.at[other, 0], gout.at[other, 0], gin.at[other, 1], gout.at[other, 1], gin.at[other, 2], gout.at[other, 2], gsmall.at[other]]
    for n, index, tag in sib:
        mine = streams[n][1].at[index]
        pltpu.make_async_remote_copy(mine, theirs[n].at[index], dsend.at[n, tag], drecv.at[n, tag], device_id=device(other, pos), device_id_type=MESH).wait()


def gather(a_in, a_out, a_small):
    any_ = pl.BlockSpec(memory_space=pl.ANY)
    return pl.pallas_call(
        gather_kernel,
        out_shape=(
            jax.ShapeDtypeStruct((2, 3, 4, 4, 4) + a_in.shape[1:], a_in.dtype),
            jax.ShapeDtypeStruct((2, 3, 4, 4, 4) + a_out.shape[1:], a_out.dtype),
            jax.ShapeDtypeStruct((2, 4, 4, 4) + a_small.shape, a_small.dtype),
        ),
        in_specs=[pl.BlockSpec(memory_space=pltpu.VMEM)] * 3,
        out_specs=(any_,) * 3,
        scratch_shapes=[
            pltpu.SemaphoreType.DMA((7, 3, 6)),
            pltpu.SemaphoreType.DMA((7, 3, 6)),
            pltpu.SemaphoreType.DMA((7,)),
            pltpu.SemaphoreType.DMA((7, 7)),
            pltpu.SemaphoreType.DMA((7, 7)),
        ],
        compiler_params=pltpu.CompilerParams(collective_id=0, has_side_effects=True),
        name="gather_weights",
    )(a_in, a_out, a_small)


def lead(n):
    return {2: 16, 1: 4, 0: 1}[n]


def scatter_kernel(win0, win1, win2, wout0, wout1, wout2, small, oin, oout, osmall, *scratch):
    got = {}
    it = iter(scratch)
    for phase in (2, 1, 0):
        for kind in (0, 1):
            got[phase, kind] = next(it)
    acc = {}
    for phase in (2, 1):
        for kind in (0, 1):
            acc[phase, kind] = next(it)
    mine = {kind: next(it) for kind in (0, 1)}
    sgot = {phase: next(it) for phase in (2, 1, 0)}
    sacc = {phase: next(it) for phase in (3, 2, 1)}
    send, recv, ssend, srecv, lsem, ssem = it

    section = lax.axis_index("section")
    dp = lax.axis_index("dp")
    pos = (lax.div(dp, 16), lax.rem(lax.div(dp, 4), 4), lax.rem(dp, 4))

    barrier = pltpu.get_barrier_semaphore()
    for axis in range(3):
        for by in (1, 2, 3):
            pl.semaphore_signal(barrier, inc=1, device_id=device(section, moved(pos, axis, by)), device_id_type=MESH)
    first = pltpu.make_async_copy(small, sacc[3], ssem.at[0])
    first.start()
    pl.semaphore_wait(barrier, 9)

    def small_phase(phase):
        axis = ORDERS[0][phase]
        here = pos[axis]
        cur = sacc[phase + 1]
        if phase == 2:
            first.wait()
        sends = []
        for by in (1, 2, 3):
            to = moved(pos, axis, by)
            c = pltpu.make_async_remote_copy(cur.at[to[axis]], sgot[phase].at[by - 1], ssend.at[phase, by - 1], srecv.at[phase, by - 1], device_id=device(section, to), device_id_type=MESH)
            c.start()
            sends.append(c)
        def finish():
            for c in sends:
                c.wait()
            total = cur[here] + sgot[phase][0] + sgot[phase][1] + sgot[phase][2]
            if phase == 0:
                osmall[...] = total
            else:
                sacc[phase][...] = total
        return finish

    def add_into(dst, parts, slices):
        def one(i, carry):
            dst(i, [p[i].astype(F32) for p in parts])
            return carry
        lax.fori_loop(0, slices, one, 0)

    refs = ((win0, win1, win2), (wout0, wout1, wout2))
    for phase in (2, 1, 0):
        half = {2: 8, 1: 2, 0: 1}[phase]
        streams = [(j, kind) for j in range(3) for kind in (0, 1)]

        def own(j, kind, k, h):
            order = ORDERS[j]
            axis = order[phase]
            if phase == 2:
                at = list(pos)
                at[axis] = k
                return refs[kind][j].at[block_index(order, 2, tuple(at), h)]
            return acc[phase + 1, kind].at[j, k, pl.ds(half * h, half)] if phase == 1 else acc[1, kind].at[j, k]

        def have(kind, h):
            return phase != 0 or h == kind

        def slot_ref(j, kind, slot):
            return got[phase, kind].at[(j, slot, 0) if phase == 0 else (j, slot)]

        def copy(n, slot, src, to):
            j, kind = streams[n]
            return pltpu.make_async_remote_copy(src, slot_ref(j, kind, slot), send.at[phase, n, slot], recv.at[phase, n, slot], device_id=device(section, to), device_id_type=MESH)

        finish_small = small_phase(phase)
        started = []
        loads = []
        for n, (j, kind) in enumerate(streams):
            axis = ORDERS[j][phase]
            left, right, far = (moved(pos, axis, by)[axis] for by in (3, 1, 2))
            to_left, to_right = moved(pos, axis, 3), moved(pos, axis, 1)
            for slot, k, h, to in ((0, far, 0, to_left), (1, far, 1, to_right), (2, left, 1, to_left), (3, right, 0, to_right)):
                if have(kind, h):
                    c = copy(n, slot, own(j, kind, k, h), to)
                    c.start()
                    started.append(c)
            if phase == 2:
                for i, (k, h) in enumerate(((left, 0), (right, 1))):
                    c = pltpu.make_async_copy(own(j, kind, k, h), mine[kind].at[j, i], lsem.at[n, i])
                    c.start()
                    loads.append(c)
        for n, (j, kind) in enumerate(streams):
            axis = ORDERS[j][phase]
            left, right = (moved(pos, axis, by)[axis] for by in (3, 1))
            to_left, to_right = moved(pos, axis, 3), moved(pos, axis, 1)
            for i, (slot, k, h, to) in enumerate(((0, left, 0, to_left), (1, right, 1, to_right))):
                if not have(kind, h):
                    continue
                copy(n, slot, slot_ref(j, kind, slot), to).wait_recv()
                if phase == 2:
                    loads[2 * n + i].wait()
                    part = mine[kind].at[j, i]
                else:
                    part = own(j, kind, k, h)
                buf = slot_ref(j, kind, slot)
                sum_refs(buf, [part], buf, BF, phase)
                c = copy(n, 4 + i, buf, to)
                c.start()
                started.append(c)
                if phase == 2:
                    c = pltpu.make_async_copy(own(j, kind, pos[axis], h), mine[kind].at[j, i], lsem.at[n, i])
                    c.start()
                    loads[2 * n + i] = c
        finish_small()
        for n, (j, kind) in enumerate(streams):
            axis = ORDERS[j][phase]
            to_left = moved(pos, axis, 3)
            for h, slots in ((0, (3, 4)), (1, (2, 5))):
                if not have(kind, h):
                    continue
                for slot in slots:
                    copy(n, slot, slot_ref(j, kind, slot), to_left).wait_recv()
                if phase == 2:
                    loads[2 * n + h].wait()
                    part = mine[kind].at[j, h]
                else:
                    part = own(j, kind, pos[axis], h)
                a, b = (slot_ref(j, kind, s) for s in slots)
                if phase == 0:
                    out = (oin, oout)[kind].at[j]
                    out[...] = part[...].astype(F32) + a[...].astype(F32) + b[...].astype(F32)
                else:
                    final_sum(j, kind, phase, h, part, a, b, acc[phase, kind])
        for c in started:
            c.wait_send()


def sum_refs(a, others, dst, dtype, phase):
    shape = a.shape
    if len(shape) == 2:
        dst[...] = (a[...].astype(F32) + others[0][...].astype(F32)).astype(dtype)
        return
    if len(shape) == 3:
        def one(i, c):
            o = others[0][i] if len(others[0].shape) == 3 else others[0][...]
            dst[i] = (a[i].astype(F32) + o.astype(F32)).astype(dtype)
            return c
        lax.fori_loop(0, shape[0], one, 0)
        return
    def one(i, c):
        for q in range(shape[1]):
            dst[i, q] = (a[i, q].astype(F32) + others[0][i, q].astype(F32)).astype(dtype)
        return c
    lax.fori_loop(0, shape[0], one, 0)


def final_sum(j, kind, phase, h, part, a, b, acc):
    order = ORDERS[j]
    if phase == 1:
        def one(i, c):
            acc[j, 2 * h + i] = (part[i].astype(F32) + a[i].astype(F32) + b[i].astype(F32)).astype(BF)
            return c
        lax.fori_loop(0, 2, one, 0)
        return
    low = min(order[:2])
    def one(i, c):
        for q in range(4):
            first, second = 2 * h + i, q
            at = (first, second) if order[1] == low else (second, first)
            acc[j, at[0], at[1]] = (part[i, q].astype(F32) + a[i, q].astype(F32) + b[i, q].astype(F32)).astype(BF)
        return c
    lax.fori_loop(0, 2, one, 0)


def scatter(win, wout, small):
    any_ = pl.BlockSpec(memory_space=pl.ANY)
    vm = pl.BlockSpec(memory_space=pltpu.VMEM)
    ri, ci = win[0].shape[-2:]
    ro, co = wout[0].shape[-2:]
    dims = {0: (ri, ci), 1: (ro, co)}
    scratch = []
    for phase in (2, 1, 0):
        for kind in (0, 1):
            n = {2: (2, 4), 1: (2,), 0: (1,)}[phase]
            scratch.append(pltpu.VMEM((3, 6) + n + dims[kind], BF))
    for phase in (2, 1):
        for kind in (0, 1):
            n = {2: (4, 4), 1: (4,)}[phase]
            scratch.append(pltpu.VMEM((3,) + n + dims[kind], BF))
    for kind in (0, 1):
        scratch.append(pltpu.VMEM((3, 2, 2, 4) + dims[kind], BF))
    for n in ((4, 4), (4,), ()):
        scratch.append(pltpu.VMEM((3,) + n + (8, 128), F32))
    for n in ((4, 4, 4), (4, 4), (4,)):
        scratch.append(pltpu.VMEM(n + (8, 128), F32))
    scratch += [pltpu.SemaphoreType.DMA((3, 6, 6)), pltpu.SemaphoreType.DMA((3, 6, 6)), pltpu.SemaphoreType.DMA((3, 3)), pltpu.SemaphoreType.DMA((3, 3)), pltpu.SemaphoreType.DMA((6, 2)), pltpu.SemaphoreType.DMA((1,))]
    return pl.pallas_call(
        scatter_kernel,
        out_shape=(jax.ShapeDtypeStruct((3, ri, ci), F32), jax.ShapeDtypeStruct((3, ro, co), F32), jax.ShapeDtypeStruct((8, 128), F32)),
        in_specs=[any_] * 7,
        out_specs=(vm,) * 3,
        scratch_shapes=scratch,
        compiler_params=pltpu.CompilerParams(collective_id=1, has_side_effects=True, vmem_limit_bytes=62 * 1024 * 1024),
        name="scatter_grads",
    )(*win, *wout, small)


GROUPS = 6
LOG2E = 1.4426950408889634


def dot(a, b, dims=((1,), (0,)), precision=None):
    return lax.dot_general(a, b, (dims, ((), ())), preferred_element_type=F32, precision=precision)


def sigmoid(v):
    return 1.0 / (1.0 + jnp.exp(-v))


def split_dot(exact, wide, dims=((1,), (0,)), flip=False):
    total = None
    rest = wide
    for _ in range(3):
        term = rest.astype(BF)
        rest = rest - term.astype(F32)
        part = dot(term, exact, dims) if flip else dot(exact, term, dims)
        total = part if total is None else total + part
    return total


def compute_kernel(
    h_ref, ct_ref, info_ref, allowed_ref, pg_ref, pe_ref, ph_ref, pn_ref, win_ref, wout_ref,
    dfirst_ref, second_ref, u_ref, o_ref, dv_ref, dp_ref, sg_ref, se_ref, sh_ref, sn_ref,
    wbuf, ebuf, obuf, zbuf, xbuf, ybuf, tbuf, hbuf, pebuf, masks, tri, sel, qcol, qrow, dtrow, heads, smat, gbuf, dgacc, rowq, rowx, acc, rbuf,
    wsem, esem, osem,
):
    def copy_w(l, g):
        j, off = lax.div(g, 2), pl.multiple_of(lax.rem(g, 2) * 1024, 128)
        return pltpu.make_async_copy(win_ref.at[l, j, :, pl.ds(off, 1024)], wbuf.at[g], wsem.at[g])

    def copy_e(l, j):
        return pltpu.make_async_copy(win_ref.at[l, j, :, pl.ds(2048, 128)], ebuf.at[j], esem.at[j])

    def copy_o(l, j):
        return pltpu.make_async_copy(wout_ref.at[l, j], obuf.at[j], osem.at[j])

    for j in range(3):
        copy_e(0, j).start()
    for g in range(GROUPS):
        copy_w(0, jnp.int32(g)).start()
    for j in range(3):
        copy_o(0, j).start()

    info = info_ref[...]
    for d in range(3):
        masks[d] = jnp.broadcast_to(info[:, 2 + d : 3 + d], (128, 128))
    masks[3] = jnp.broadcast_to(info[:, 1:2], (128, 128))
    rows = lax.broadcasted_iota(jnp.int32, (128, 128), 0)
    cols = lax.broadcasted_iota(jnp.int32, (128, 128), 1)
    tri[...] = (rows >= cols).astype(F32).astype(BF)
    srow = lax.broadcasted_iota(jnp.int32, (512, 128), 0)
    scol = lax.broadcasted_iota(jnp.int32, (512, 128), 1)
    sel[...] = (lax.div(srow, 64) == scol).astype(F32).astype(BF)
    low_lanes = cols < 64

    def conv(px, taps, bias):
        s1 = pltpu.roll(px, 1, 0) * masks[0]
        s2 = pltpu.roll(px, 2, 0) * masks[1]
        s3 = pltpu.roll(px, 3, 0) * masks[2]
        c = bias + taps[3:4] * px + taps[2:3] * s1 + taps[1:2] * s2 + taps[0:1] * s3
        return c, (s3, s2, s1, px)

    def conv_back(dc, taps):
        out = taps[3:4] * dc
        out = out + taps[2:3] * pltpu.roll(dc * masks[0], 127, 0)
        out = out + taps[1:2] * pltpu.roll(dc * masks[1], 126, 0)
        return out + taps[0:1] * pltpu.roll(dc * masks[2], 125, 0)

    def total(v):
        return jnp.sum(v, axis=0, keepdims=True)

    def decay(g, hh):
        gap = jnp.broadcast_to(qcol[g][:, hh : hh + 1], (128, 128)) - qrow[g][hh : hh + 1, :]
        return jnp.exp2(jnp.minimum(gap, 0.0)) * dtrow[g][hh : hh + 1, :]

    def zero_lanes(v, keep):
        return jnp.where(keep, v, jnp.zeros_like(v))

    def forward(l, h):
        hbuf[l] = h.astype(BF)
        rs = lax.rsqrt(jnp.sum(h * h, axis=1, keepdims=True) * (1.0 / D) + EPSILON)
        rbuf[l, 0] = jnp.broadcast_to(rs, (128, 128))
        u_ref[l] = (h * rs * pn_ref[l, 0:1, :] * info_ref[:, 1:2]).astype(BF)
        for j in range(3):
            copy_e(l, j).wait()
            pebuf[l, j] = dot(u_ref[l], ebuf[j])
        if l == 0:
            for j in range(3):
                copy_e(1, j).start()
        for j in range(2):
            c, _ = conv(pebuf[l, j], pe_ref[l, j, 0:4], pe_ref[l, j, 4:5])
            smat[l, j] = (c * sigmoid(c)).astype(BF)
        v = pebuf[l, 2] + ph_ref[l, 0:1]
        dt = jnp.maximum(v, 0.0) + jnp.log1p(jnp.exp(-jnp.abs(v)))
        rate = -jnp.exp(ph_ref[l, 1:2])
        q = split_dot(tri[...], dt * rate) * LOG2E
        heads[l, 0] = dt
        heads[l, 1] = q
        gbuf[l] = dot(smat[l, 1], smat[l, 0], ((1,), (1,))) * allowed_ref[...]
        prepare(l)
        acc[:, 0:128] = jnp.zeros((128, 128), F32)

        def group(g, carry):
            copy_w(l, g).wait()
            p = dot(u_ref[l], wbuf[g])
            if l == 0:
                copy_w(1, g).start()
            zbuf[l, g] = p[:, 0:512]
            xbuf[l, g] = p[:, 512:1024]
            for k in range(4):
                at = slice(128 * k, 128 * k + 128)
                c, _ = conv(xbuf[l, g, :, at], pg_ref[l, g, 0:4, at], pg_ref[l, g, 4:5, at])
                x = c * sigmoid(c)
                xb = x.astype(BF)
                both = jnp.concatenate([zero_lanes(xb, low_lanes), zero_lanes(xb, ~low_lanes)], axis=0)
                w = jnp.concatenate([(gbuf[l] * decay(g, 2 * k + i)).astype(BF) for i in range(2)], axis=1)
                y = dot(w, both) + pg_ref[l, g, 6:7, at] * x
                ybuf[l, g, :, at] = y
                z = zbuf[l, g, :, at]
                e = y * (z * sigmoid(z))
                tbuf[g, :, at] = e
                acc[:, 0:128] += e * e
            return carry

        lax.fori_loop(0, GROUPS, group, 0)
        r = lax.rsqrt(jnp.sum(acc[:, 0:128], axis=1, keepdims=True) * (1.0 / DI) + EPSILON)
        rbuf[l, 1] = jnp.broadcast_to(r, (128, 128))
        for g in range(GROUPS):
            o_ref[l, :, 512 * g : 512 * g + 512] = (tbuf[g] * r * pg_ref[l, g, 5:6, :]).astype(BF)
        for j in range(3):
            copy_o(l, j).wait()
            acc[:, 512 * j : 512 * j + 512] = dot(o_ref[l], obuf[j])
            if l == 0:
                copy_o(1, j).start()
        return h + acc[...]

    def prepare(l):
        q = heads[l, 1]
        qt = jnp.transpose(q)
        dtt = jnp.transpose(heads[l, 0])
        for g in range(GROUPS):
            qcol[g] = q if g == 0 else pltpu.roll(q, 128 - 8 * g, 1)
            qrow[g] = qt[8 * g : 8 * g + 8, :]
            dtrow[g] = dtt[8 * g : 8 * g + 8, :]

    def backward(l, dh):
        dv_ref[l] = dh.astype(BF)
        if l == 0:
            for j in range(3):
                copy_o(0, j).wait()
        sumcol = jnp.zeros((128, 128), F32)
        acc[:, 0:128] = sumcol

        def first(g, carry):
            do = None
            for j in range(3):
                part = dot(dv_ref[l, :, 512 * j : 512 * j + 512], obuf[j, pl.ds(pl.multiple_of(512 * g, 512), 512), :], ((1,), (1,)))
                do = part if do is None else do + part
            tbuf[g] = do
            for k in range(4):
                at = slice(128 * k, 128 * k + 128)
                z = zbuf[l, g, :, at]
                e = ybuf[l, g, :, at] * (z * sigmoid(z))
                prod = tbuf[g, :, at] * e
                sg_ref[l, g, 5:6, at] = total(prod * rbuf[l, 1])
                acc[:, 0:128] += prod * pg_ref[l, g, 5:6, at]
            return carry

        lax.fori_loop(0, GROUPS, first, 0)
        if l == 1:
            for j in range(3):
                copy_o(0, j).start()
        r = rbuf[l, 1]
        coef = jnp.broadcast_to(jnp.sum(acc[:, 0:128], axis=1, keepdims=True) * (1.0 / DI), (128, 128)) * r * r * r
        masks[4] = coef
        prepare(l)
        dgacc[...] = jnp.zeros((128, 128), F32)
        rowq[...] = jnp.zeros((128, 128), F32)
        rowx[...] = jnp.zeros((128, 128), F32)
        acc[...] = jnp.zeros((128, D), F32)

        def second(g, carry):
            if l == 0:
                copy_w(0, g).wait()
            j, off = lax.div(g, 2), pl.multiple_of(lax.rem(g, 2) * 1024, 128)
            sums_q = None
            sums_x = None
            for k in range(4):
                at = slice(128 * k, 128 * k + 128)
                z = zbuf[l, g, :, at]
                y = ybuf[l, g, :, at]
                sz = sigmoid(z)
                silu = z * sz
                de = rbuf[l, 1] * (tbuf[g, :, at] * pg_ref[l, g, 5:6, at]) - (y * silu) * masks[4]
                dyb = (de * silu).astype(BF)
                dz = de * y * (sz + silu * (1.0 - sz))
                dp_ref[l, j, :, pl.ds(pl.multiple_of(off + 128 * k, 128), 128)] = dz.astype(BF)
                taps = pg_ref[l, g, 0:4, at]
                c, shifts = conv(xbuf[l, g, :, at], taps, pg_ref[l, g, 4:5, at])
                sc = sigmoid(c)
                x = c * sc
                xb = x.astype(BF)
                dyw = dyb.astype(F32)
                skip = pg_ref[l, g, 6:7, at]
                xt = jnp.concatenate([zero_lanes(xb, low_lanes), zero_lanes(xb, ~low_lanes)], axis=0)
                dyt = jnp.concatenate([zero_lanes(dyb, low_lanes), zero_lanes(dyb, ~low_lanes)], axis=0)
                dw = dot(dyb, xt, ((1,), (1,)))
                ws = []
                dg = None
                for i in range(2):
                    e = decay(g, 2 * k + i)
                    ws.append((gbuf[l] * e).astype(BF))
                    part = dw[:, 128 * i : 128 * i + 128] * e
                    dg = part if dg is None else dg + part
                dgacc[...] += dg
                dx0 = dot(jnp.concatenate(ws, axis=0), dyt, ((0,), (0,)))
                dx = dx0 + skip * dyw
                sg_ref[l, g, 6:7, at] = total(dyw * x)
                mq = dyw * (y - skip * x)
                mx = xb.astype(F32) * dx0
                one = sel[128 * k : 128 * k + 128, :]
                for m, name in ((mq, "q"), (mx, "x")):
                    hi = m.astype(BF)
                    lo = (m - hi.astype(F32)).astype(BF)
                    part = dot(hi, one) + dot(lo, one)
                    if name == "q":
                        sums_q = part if sums_q is None else sums_q + part
                    else:
                        sums_x = part if sums_x is None else sums_x + part
                dc = dx * (sc + x * (1.0 - sc))
                for t in range(4):
                    sg_ref[l, g, t : t + 1, at] = total(dc * shifts[t])
                sg_ref[l, g, 4:5, at] = total(dc)
                dp_ref[l, j, :, pl.ds(pl.multiple_of(off + 512 + 128 * k, 128), 128)] = conv_back(dc, taps).astype(BF)
            rowq[...] += pltpu.roll(sums_q, 8 * g, 1)
            rowx[...] += pltpu.roll(sums_x, 8 * g, 1)
            acc[...] += dot(dp_ref[l, j, :, pl.ds(off, 1024)], wbuf[g], ((1,), (1,)))
            if l == 1:
                copy_w(0, g).start()
            return carry

        lax.fori_loop(0, GROUPS, second, 0)
        dg = (dgacc[...] * allowed_ref[...]).astype(BF)
        d_states = (dot(dg, smat[l, 1], ((0,), (0,))), dot(dg, smat[l, 0]))
        for j in range(2):
            taps = pe_ref[l, j, 0:4]
            c, shifts = conv(pebuf[l, j], taps, pe_ref[l, j, 4:5])
            sc = sigmoid(c)
            dc = d_states[j] * (sc + c * sc * (1.0 - sc))
            for t in range(4):
                se_ref[l, j, t : t + 1] = total(dc * shifts[t])
            se_ref[l, j, 4:5] = total(dc)
            dp_ref[l, j, :, 2048:2176] = conv_back(dc, taps).astype(BF)
        v = pebuf[l, 2] + ph_ref[l, 0:1]
        sv = sigmoid(v)
        dt = heads[l, 0]
        rate = -jnp.exp(ph_ref[l, 1:2])
        back = split_dot(tri[...], rowq[...] - rowx[...], ((0,), (0,)))
        real = cols < H
        ratio = jnp.where(v < -15.0, 1.0, sv / jnp.maximum(dt, 1e-30))
        dr = jnp.where(real, rowx[...] * ratio + back * rate * sv, 0.0)
        sh_ref[l, 0:1] = total(dr)
        sh_ref[l, 1:2] = total(jnp.where(real, back * dt, 0.0)) * rate
        dp_ref[l, 2, :, 2048:2176] = dr.astype(BF)
        du = acc[...]
        for j in range(3):
            if l == 0:
                copy_e(0, j).wait()
            du = du + dot(dp_ref[l, j, :, 2048:2176], ebuf[j], ((1,), (1,)))
        if l == 1:
            for j in range(3):
                copy_e(0, j).start()
        h = hbuf[l].astype(F32)
        rs = rbuf[l, 0][:, 0:1]
        hn = h * rs
        du = du * info_ref[:, 1:2]
        sn_ref[l, 0:1, :] = total(du * hn)
        t = du * pn_ref[l, 0:1, :]
        s = jnp.sum(t * hn, axis=1, keepdims=True) * (1.0 / D)
        return dh + rs * (t - hn * s)

    middle = forward(0, h_ref[...].astype(F32)).astype(BF).astype(F32)
    second_ref[...] = forward(1, middle).astype(BF)
    d_middle = backward(1, ct_ref[...].astype(F32)).astype(BF).astype(F32)
    dfirst_ref[...] = backward(0, d_middle).astype(BF)


def compute(h, ct, info, allowed, pg, pe, ph, pn, win, wout):
    vm = pl.BlockSpec(memory_space=pltpu.VMEM)
    any_ = pl.BlockSpec(memory_space=pl.ANY)
    s = jax.ShapeDtypeStruct
    T = 128
    V = pltpu.VMEM
    return pl.pallas_call(
        compute_kernel,
        out_shape=(
            s((T, D), BF), s((T, D), BF), s((2, T, D), BF), s((2, T, DI), BF), s((2, T, D), BF),
            s((2, 3, T, 2176), BF), s((2, 6, 8, 512), F32), s((2, 2, 8, 128), F32), s((2, 8, 128), F32), s((2, 8, D), F32),
        ),
        in_specs=[vm] * 8 + [any_] * 2,
        out_specs=(vm,) * 10,
        scratch_shapes=[
            V((6, D, 1024), BF), V((3, D, 128), BF), V((3, DI, 512), BF),
            V((2, 6, T, 512), F32), V((2, 6, T, 512), F32), V((2, 6, T, 512), F32), V((6, T, 512), F32), V((2, T, D), BF),
            V((2, 3, T, 128), F32), V((5, T, 128), F32), V((128, 128), BF), V((512, 128), BF),
            V((6, 128, 128), F32), V((6, 8, 128), F32), V((6, 8, 128), F32), V((2, 2, 128, 128), F32), V((2, 2, 128, 128), BF),
            V((2, 128, 128), F32), V((128, 128), F32), V((128, 128), F32), V((128, 128), F32), V((T, D), F32), V((2, 2, 128, 128), F32),
            pltpu.SemaphoreType.DMA((6,)), pltpu.SemaphoreType.DMA((3,)), pltpu.SemaphoreType.DMA((3,)),
        ],
        compiler_params=pltpu.CompilerParams(vmem_limit_bytes=62 * 1024 * 1024),
        cost_estimate=pl.CostEstimate(flops=23_000_000_000, bytes_accessed=100_000_000, transcendentals=10_000_000),
        name="layers",
    )(h, ct, info, allowed, pg, pe, ph, pn, win, wout)


def block_info(segment, valid_rows):
    pos = jnp.arange(128, dtype=jnp.int32)
    col = jnp.arange(128, dtype=jnp.int32)[None, :]
    linked = []
    for d in (1, 2, 3):
        before = jnp.concatenate([jnp.full((d,), -1, jnp.int32), segment[: 128 - d]])
        linked.append((before == segment).astype(F32))
    out = jnp.zeros((128, 128), F32)
    for lane, v in enumerate([segment.astype(F32), valid_rows] + linked):
        out = jnp.where(col == lane, v[:, None], out)
    allowed = ((pos[:, None] >= pos[None, :]) & (segment[:, None] == segment[None, :])).astype(F32)
    return out, allowed


def body(
    ends_in,
    seg_ids,
    block_counts,
    in_weight,
    conv_weight,
    conv_bias,
    pre_gain,
    gate_gain,
    out_weight,
    dt_bias,
    a_log,
    skip,
):
    section = lax.axis_index("section")
    leading = section == 0
    length = seg_ids.shape[1]
    wide = lambda v: v[0].astype(F32)
    small = pack_small(wide(conv_weight), wide(conv_bias), wide(pre_gain), wide(gate_gain), (wide(dt_bias), wide(a_log), wide(skip)))
    own_in = jnp.stack(to_panels(in_weight[0]))
    own_out = jnp.stack([out_weight[0][:, 512 * j : 512 * j + 512] for j in range(3)])
    all_in, all_out, all_small = gather(own_in, own_out, small)
    params = layer_params(all_small.reshape(2, 64, 8, 128))
    swap = [(0, 1), (1, 0)]
    pick = lambda v, i: lax.dynamic_index_in_dim(v, i, 0, keepdims=False)
    ends = ends_in[0].reshape(2, length, D)
    mine, got = pick(ends, section), lax.ppermute(pick(ends, 1 - section), "section", swap)
    block_in, cotangent = jnp.where(leading, mine, got), jnp.where(leading, got, mine)
    segment = pick(seg_ids, section)
    valid_rows = (jnp.arange(length, dtype=jnp.int32) < pick(block_counts, section)).astype(F32)
    info, allowed = block_info(segment, valid_rows)

    d_first, second, u, o, dv, dp, sg, se, sh, sn = compute(
        block_in, cotangent, info, allowed, *params, all_in.reshape(2, 3, D, 2176), all_out.reshape(2, 3, DI, 512)
    )

    other = 1 - section
    both = lambda v: jnp.concatenate([pick(v, section), lax.ppermute(pick(v, other), "section", swap)], axis=-2)
    u, o, dv, dp = both(u), both(o), both(dv), both(dp)
    tiles = small_grads(sg, se, sh, sn)
    tiles = pick(tiles, section) + lax.ppermute(pick(tiles, other), "section", swap)
    end_got = lax.ppermute(jnp.where(leading, second, d_first), "section", swap)
    ends_out = jnp.where(leading, jnp.stack([d_first, end_got]), jnp.stack([end_got, second])).reshape(1, 2 * length, D)

    d_in = [jnp.dot(u.T, dp[j], preferred_element_type=F32).astype(BF).reshape(4, 4, 4, 24, 2176) for j in range(3)]
    d_out = [jnp.dot(o.T, dv[:, 512 * j : 512 * j + 512], preferred_element_type=F32).astype(BF).reshape(4, 4, 4, 48, 512) for j in range(3)]
    sum_in, sum_out, sums = scatter(d_in, d_out, tiles.reshape(4, 4, 4, 8, 128))
    d_in_weight = from_panels([sum_in[j] for j in range(3)])
    d_out_weight = jnp.concatenate([sum_out[j] for j in range(3)], axis=1)
    return (
        ends_out,
        d_in_weight[None],
        sums[None, 0:4, 0:52],
        sums[None, 4, 0:52],
        sums[None, 5, 0:24],
        sums[None, 6, 0:48],
        d_out_weight[None],
        sums[None, 7, 0:48],
        sums[None, 5, 64:112],
        sums[None, 6, 64:112],
    )


def solution(mesh):
    placed = (
        P("section", "dp", None),
        P("dp", None),
        P("dp"),
        P("section", "dp", None),
        P("section", None, "dp"),
        P("section", "dp"),
        P("section", "dp"),
        P("section", "dp"),
        P("section", "dp", None),
        P("section", None),
        P("section", None),
        P("section", None),
    )
    return jax.shard_map(
        body,
        mesh=mesh,
        in_specs=placed,
        out_specs=(
            P("section", "dp", None),
            P("section", "dp", None),
            P("section", None, "dp"),
            P("section", "dp"),
            P("section", "dp"),
            P("section", "dp"),
            P("section", "dp", None),
            P("section", None),
            P("section", None),
            P("section", None),
        ),
        check_vma=False,
    )
```

```python
import jax
import jax.numpy as jnp
from jax import lax
from jax.experimental import pallas as pl
from jax.experimental.pallas import tpu as pltpu
from jax.sharding import PartitionSpec as P

D = 1536
DI = 3072
N = 128
HEAD_DIM = 64
H = 48
CC = 3328
EPSILON = 1e-05
F32 = jnp.float32
BF = jnp.bfloat16


def to_panels(w):
    rows = w.shape[0]
    z, x = w[:, :DI], w[:, DI : 2 * DI]
    rates = jnp.pad(w[:, 2 * DI + 2 * N :], ((0, 0), (0, N - H)))
    extras = (w[:, 2 * DI : 2 * DI + N], w[:, 2 * DI + N : 2 * DI + 2 * N], rates)
    panels = []
    for j in range(3):
        pieces = []
        for g in (2 * j, 2 * j + 1):
            pieces += [z[:, 512 * g : 512 * g + 512], x[:, 512 * g : 512 * g + 512]]
        panels.append(jnp.concatenate(pieces + [extras[j]], axis=1))
    return panels


def from_panels(p):
    z = [p[g // 2][:, 1024 * (g % 2) : 1024 * (g % 2) + 512] for g in range(6)]
    x = [p[g // 2][:, 1024 * (g % 2) + 512 : 1024 * (g % 2) + 1024] for g in range(6)]
    extras = [p[0][:, 2048:], p[1][:, 2048:], p[2][:, 2048 : 2048 + H]]
    return jnp.concatenate(z + x + extras, axis=1)


def pack_small(taps, bias, gain_in, gain_out, heads):
    lead = taps.shape[:-2]
    wide = lambda v: jnp.pad(v, [(0, 0)] * (v.ndim - 1) + [(0, 128 - v.shape[-1])])
    pair = lambda a, b: jnp.concatenate([jnp.pad(a, [(0, 0)] * (a.ndim - 1) + [(0, 64 - a.shape[-1])]), jnp.pad(b, [(0, 0)] * (b.ndim - 1) + [(0, 64 - b.shape[-1])])], axis=-1)
    spread = [jnp.broadcast_to(h, lead + (H,)) for h in heads]
    rows = [wide(taps), wide(bias)[..., None, :], pair(gain_in, spread[1])[..., None, :], pair(gain_out, spread[2])[..., None, :], wide(spread[0])[..., None, :]]
    return jnp.concatenate(rows, axis=-2)


def layer_params(s):
    rows = jnp.transpose(s[:, :, 0:5, 0:52], (0, 2, 1, 3)).reshape(2, 5, CC)
    gain_in, gain_out = s[:, :, 5, 0:24].reshape(2, 1, D), s[:, :, 6, 0:48].reshape(2, 6, 1, 512)
    rate_bias, decay_log, skip = s[:, 0, 7, 0:48], s[:, 0, 5, 64:112], s[:, 0, 6, 64:112]
    skip = jnp.repeat(skip, HEAD_DIM, axis=1).reshape(2, 6, 1, 512)
    x_rows = jnp.transpose(rows[:, :, :DI].reshape(2, 5, 6, 512), (0, 2, 1, 3))
    pg = jnp.concatenate([x_rows, gain_out, skip, jnp.zeros_like(skip)], axis=2)
    pe = jnp.pad(jnp.transpose(rows[:, :, DI:].reshape(2, 5, 2, N), (0, 2, 1, 3)), ((0, 0), (0, 0), (0, 3), (0, 0)))
    ph = jnp.pad(jnp.stack([rate_bias, decay_log], axis=1), ((0, 0), (0, 6), (0, N - H)))
    pn = jnp.pad(gain_in, ((0, 0), (0, 7), (0, 0)))
    return pg, pe, ph, pn


def small_grads(sg, se, sh, sn):
    rows = jnp.concatenate([jnp.transpose(sg[:, :, 0:5], (0, 2, 1, 3)).reshape(2, 5, DI), jnp.transpose(se[:, :, 0:5], (0, 2, 1, 3)).reshape(2, 5, 2 * N)], axis=2)
    rows = jnp.transpose(rows.reshape(2, 5, 64, 52), (0, 2, 1, 3))
    gain_in, gain_out = sn[:, 0].reshape(2, 64, 24), sg[:, :, 5].reshape(2, 64, 48)
    skip = jnp.sum(sg[:, :, 6].reshape(2, H, HEAD_DIM), axis=2)
    heads = [v[:, None] for v in (sh[:, 0, :H], sh[:, 1, :H], skip)]
    return pack_small(rows[:, :, 0:4], rows[:, :, 4], gain_in, gain_out, heads)


MESH = pl.DeviceIdType.MESH
ORDERS = ((2, 1, 0), (1, 0, 2), (0, 2, 1))


def device(section, pos):
    return {"section": section, "dp": pos[0] * 16 + pos[1] * 4 + pos[2]}


def moved(pos, axis, by):
    out = list(pos)
    out[axis] = lax.rem(pos[axis] + by, 4)
    return tuple(out)


def block_index(order, phase, pos, half):
    index = [pos[0], pos[1], pos[2]]
    for a in order[:phase]:
        index[a] = slice(None)
    if phase > 0 and half is not None:
        a = min(order[:phase])
        index[a] = pl.ds(2 * half, 2)
    return tuple(index)


def gather_kernel(in_ref, out_ref, small_ref, gin, gout, gsmall, send, recv, local, dsend, drecv):
    section = lax.axis_index("section")
    dp = lax.axis_index("dp")
    pos = (lax.div(dp, 16), lax.rem(lax.div(dp, 4), 4), lax.rem(dp, 4))
    other = 1 - section

    barrier = pltpu.get_barrier_semaphore()
    for axis in range(3):
        for by in (1, 3):
            pl.semaphore_signal(barrier, inc=1, device_id=device(section, moved(pos, axis, by)), device_id_type=MESH)
    pl.semaphore_signal(barrier, inc=1, device_id=device(other, pos), device_id_type=MESH)
    pl.semaphore_wait(barrier, 7)

    streams = []
    for j in range(3):
        streams.append((in_ref.at[j], gin.at[section, j], ORDERS[j], 0))
        streams.append((out_ref.at[j], gout.at[section, j], ORDERS[j], 1))
    streams.append((small_ref, gsmall.at[section], ORDERS[0], 0))

    own = []
    for n, (src, dst, order, turn) in enumerate(streams):
        copy = pltpu.make_async_copy(src, dst.at[pos], local.at[n])
        copy.start()
        own.append(copy)

    sib = []

    def to_sibling(n, index, tag):
        dst = streams[n][1].at[index]
        copy = pltpu.make_async_remote_copy(dst, dst, dsend.at[n, tag], drecv.at[n, tag], device_id=device(other, pos), device_id_type=MESH)
        copy.start()
        sib.append((n, index, tag))

    def remote(n, phase, k, src, dst, to):
        return pltpu.make_async_remote_copy(src, dst, send.at[n, phase, k], recv.at[n, phase, k], device_id=device(section, to), device_id_type=MESH)

    def halves(n, phase, at):
        order, turn = streams[n][2], streams[n][3]
        if phase == 0:
            whole = block_index(order, 0, at, None)
            return (whole, None) if turn == 0 else (None, whole)
        return tuple(block_index(order, phase, at, h) for h in (0, 1))

    N = len(streams)
    for phase in range(3):
        started = []
        for n, (src, dst, order, turn) in enumerate(streams):
            axis = order[phase]
            right, left = moved(pos, axis, 1), moved(pos, axis, 3)
            mine = halves(n, phase, pos)
            for k, (h, to) in enumerate(((0, right), (1, left), (1, right), (0, left))):
                if mine[h] is None:
                    continue
                source = src if phase == 0 else dst.at[mine[h]]
                c = remote(n, phase, k, source, dst.at[mine[h]], to)
                c.start()
                started.append(c)
        if phase == 0:
            for c in own:
                c.wait()
        for n, (src, dst, order, turn) in enumerate(streams):
            axis = order[phase]
            right, left = moved(pos, axis, 1), moved(pos, axis, 3)
            for k, h, frm, to in ((0, 0, left, right), (1, 1, right, left)):
                got = halves(n, phase, frm)[h]
                if got is None:
                    continue
                remote(n, phase, k, dst.at[got], dst.at[got], to).wait_recv()
                c = remote(n, phase, 4 + k, dst.at[got], dst.at[got], to)
                c.start()
                started.append(c)
                if phase == 2:
                    to_sibling(n, got, 2 * k)
        for n, (src, dst, order, turn) in enumerate(streams):
            axis = order[phase]
            right, left = moved(pos, axis, 1), moved(pos, axis, 3)
            for k, h, frm in ((2, 1, left), (3, 0, right)):
                got = halves(n, phase, frm)[h]
                if got is None:
                    continue
                remote(n, phase, k, dst.at[got], dst.at[got], frm).wait_recv()
                if phase == 2:
                    to_sibling(n, got, 2 * (k - 2) + 1)
        if phase == 2:
            for n, (src, dst, order, turn) in enumerate(streams):
                to_sibling(n, block_index(order, 2, pos, None), 4)
        for n, (src, dst, order, turn) in enumerate(streams):
            axis = order[phase]
            far = moved(pos, axis, 2)
            for k, h in ((0, 0), (1, 1)):
                got = halves(n, phase, far)[h]
                if got is None:
                    continue
                remote(n, phase, 4 + k, dst.at[got], dst.at[got], far).wait_recv()
                if phase == 2:
                    to_sibling(n, got, 5 + k)
        for c in started:
            c.wait_send()
    theirs = [gin.at[other, 0], gout.at[other, 0], gin.at[other, 1], gout.at[other, 1], gin.at[other, 2], gout.at[other, 2], gsmall.at[other]]
    for n, index, tag in sib:
        mine = streams[n][1].at[index]
        pltpu.make_async_remote_copy(mine, theirs[n].at[index], dsend.at[n, tag], drecv.at[n, tag], device_id=device(other, pos), device_id_type=MESH).wait()


def gather(a_in, a_out, a_small):
    any_ = pl.BlockSpec(memory_space=pl.ANY)
    return pl.pallas_call(
        gather_kernel,
        out_shape=(
            jax.ShapeDtypeStruct((2, 3, 4, 4, 4) + a_in.shape[1:], a_in.dtype),
            jax.ShapeDtypeStruct((2, 3, 4, 4, 4) + a_out.shape[1:], a_out.dtype),
            jax.ShapeDtypeStruct((2, 4, 4, 4) + a_small.shape, a_small.dtype),
        ),
        in_specs=[pl.BlockSpec(memory_space=pltpu.VMEM)] * 3,
        out_specs=(any_,) * 3,
        scratch_shapes=[
            pltpu.SemaphoreType.DMA((7, 3, 6)),
            pltpu.SemaphoreType.DMA((7, 3, 6)),
            pltpu.SemaphoreType.DMA((7,)),
            pltpu.SemaphoreType.DMA((7, 7)),
            pltpu.SemaphoreType.DMA((7, 7)),
        ],
        compiler_params=pltpu.CompilerParams(collective_id=0, has_side_effects=True),
        name="gather_weights",
    )(a_in, a_out, a_small)


def lead(n):
    return {2: 16, 1: 4, 0: 1}[n]


def scatter_kernel(win0, win1, win2, wout0, wout1, wout2, small, oin, oout, osmall, *scratch):
    got = {}
    it = iter(scratch)
    for phase in (2, 1, 0):
        for kind in (0, 1):
            got[phase, kind] = next(it)
    acc = {}
    for phase in (2, 1):
        for kind in (0, 1):
            acc[phase, kind] = next(it)
    mine = {kind: next(it) for kind in (0, 1)}
    sgot = {phase: next(it) for phase in (2, 1, 0)}
    sacc = {phase: next(it) for phase in (3, 2, 1)}
    send, recv, ssend, srecv, lsem, ssem = it

    section = lax.axis_index("section")
    dp = lax.axis_index("dp")
    pos = (lax.div(dp, 16), lax.rem(lax.div(dp, 4), 4), lax.rem(dp, 4))

    barrier = pltpu.get_barrier_semaphore()
    for axis in range(3):
        for by in (1, 2, 3):
            pl.semaphore_signal(barrier, inc=1, device_id=device(section, moved(pos, axis, by)), device_id_type=MESH)
    first = pltpu.make_async_copy(small, sacc[3], ssem.at[0])
    first.start()
    pl.semaphore_wait(barrier, 9)

    def small_phase(phase):
        axis = ORDERS[0][phase]
        here = pos[axis]
        cur = sacc[phase + 1]
        if phase == 2:
            first.wait()
        sends = []
        for by in (1, 2, 3):
            to = moved(pos, axis, by)
            c = pltpu.make_async_remote_copy(cur.at[to[axis]], sgot[phase].at[by - 1], ssend.at[phase, by - 1], srecv.at[phase, by - 1], device_id=device(section, to), device_id_type=MESH)
            c.start()
            sends.append(c)
        def finish():
            for c in sends:
                c.wait()
            total = cur[here] + sgot[phase][0] + sgot[phase][1] + sgot[phase][2]
            if phase == 0:
                osmall[...] = total
            else:
                sacc[phase][...] = total
        return finish

    def add_into(dst, parts, slices):
        def one(i, carry):
            dst(i, [p[i].astype(F32) for p in parts])
            return carry
        lax.fori_loop(0, slices, one, 0)

    refs = ((win0, win1, win2), (wout0, wout1, wout2))
    for phase in (2, 1, 0):
        half = {2: 8, 1: 2, 0: 1}[phase]
        streams = [(j, kind) for j in range(3) for kind in (0, 1)]

        def own(j, kind, k, h):
            order = ORDERS[j]
            axis = order[phase]
            if phase == 2:
                at = list(pos)
                at[axis] = k
                return refs[kind][j].at[block_index(order, 2, tuple(at), h)]
            return acc[phase + 1, kind].at[j, k, pl.ds(half * h, half)] if phase == 1 else acc[1, kind].at[j, k]

        def have(kind, h):
            return phase != 0 or h == kind

        def slot_ref(j, kind, slot):
            return got[phase, kind].at[(j, slot, 0) if phase == 0 else (j, slot)]

        def copy(n, slot, src, to):
            j, kind = streams[n]
            return pltpu.make_async_remote_copy(src, slot_ref(j, kind, slot), send.at[phase, n, slot], recv.at[phase, n, slot], device_id=device(section, to), device_id_type=MESH)

        finish_small = small_phase(phase)
        started = []
        loads = []
        for n, (j, kind) in enumerate(streams):
            axis = ORDERS[j][phase]
            left, right, far = (moved(pos, axis, by)[axis] for by in (3, 1, 2))
            to_left, to_right = moved(pos, axis, 3), moved(pos, axis, 1)
            for slot, k, h, to in ((0, far, 0, to_left), (1, far, 1, to_right), (2, left, 1, to_left), (3, right, 0, to_right)):
                if have(kind, h):
                    c = copy(n, slot, own(j, kind, k, h), to)
                    c.start()
                    started.append(c)
            if phase == 2:
                for i, (k, h) in enumerate(((left, 0), (right, 1))):
                    c = pltpu.make_async_copy(own(j, kind, k, h), mine[kind].at[j, i], lsem.at[n, i])
                    c.start()
                    loads.append(c)
        for n, (j, kind) in enumerate(streams):
            axis = ORDERS[j][phase]
            left, right = (moved(pos, axis, by)[axis] for by in (3, 1))
            to_left, to_right = moved(pos, axis, 3), moved(pos, axis, 1)
            for i, (slot, k, h, to) in enumerate(((0, left, 0, to_left), (1, right, 1, to_right))):
                if not have(kind, h):
                    continue
                copy(n, slot, slot_ref(j, kind, slot), to).wait_recv()
                if phase == 2:
                    loads[2 * n + i].wait()
                    part = mine[kind].at[j, i]
                else:
                    part = own(j, kind, k, h)
                buf = slot_ref(j, kind, slot)
                sum_refs(buf, [part], buf, BF, phase)
                c = copy(n, 4 + i, buf, to)
                c.start()
                started.append(c)
                if phase == 2:
                    c = pltpu.make_async_copy(own(j, kind, pos[axis], h), mine[kind].at[j, i], lsem.at[n, i])
                    c.start()
                    loads[2 * n + i] = c
        finish_small()
        for n, (j, kind) in enumerate(streams):
            axis = ORDERS[j][phase]
            to_left = moved(pos, axis, 3)
            for h, slots in ((0, (3, 4)), (1, (2, 5))):
                if not have(kind, h):
                    continue
                for slot in slots:
                    copy(n, slot, slot_ref(j, kind, slot), to_left).wait_recv()
                if phase == 2:
                    loads[2 * n + h].wait()
                    part = mine[kind].at[j, h]
                else:
                    part = own(j, kind, pos[axis], h)
                a, b = (slot_ref(j, kind, s) for s in slots)
                if phase == 0:
                    out = (oin, oout)[kind].at[j]
                    out[...] = part[...].astype(F32) + a[...].astype(F32) + b[...].astype(F32)
                else:
                    final_sum(j, kind, phase, h, part, a, b, acc[phase, kind])
        for c in started:
            c.wait_send()


def sum_refs(a, others, dst, dtype, phase):
    shape = a.shape
    if len(shape) == 2:
        dst[...] = (a[...].astype(F32) + others[0][...].astype(F32)).astype(dtype)
        return
    if len(shape) == 3:
        def one(i, c):
            o = others[0][i] if len(others[0].shape) == 3 else others[0][...]
            dst[i] = (a[i].astype(F32) + o.astype(F32)).astype(dtype)
            return c
        lax.fori_loop(0, shape[0], one, 0)
        return
    def one(i, c):
        for q in range(shape[1]):
            dst[i, q] = (a[i, q].astype(F32) + others[0][i, q].astype(F32)).astype(dtype)
        return c
    lax.fori_loop(0, shape[0], one, 0)


def final_sum(j, kind, phase, h, part, a, b, acc):
    order = ORDERS[j]
    if phase == 1:
        def one(i, c):
            acc[j, 2 * h + i] = (part[i].astype(F32) + a[i].astype(F32) + b[i].astype(F32)).astype(BF)
            return c
        lax.fori_loop(0, 2, one, 0)
        return
    low = min(order[:2])
    def one(i, c):
        for q in range(4):
            first, second = 2 * h + i, q
            at = (first, second) if order[1] == low else (second, first)
            acc[j, at[0], at[1]] = (part[i, q].astype(F32) + a[i, q].astype(F32) + b[i, q].astype(F32)).astype(BF)
        return c
    lax.fori_loop(0, 2, one, 0)


def scatter(win, wout, small):
    any_ = pl.BlockSpec(memory_space=pl.ANY)
    vm = pl.BlockSpec(memory_space=pltpu.VMEM)
    ri, ci = win[0].shape[-2:]
    ro, co = wout[0].shape[-2:]
    dims = {0: (ri, ci), 1: (ro, co)}
    scratch = []
    for phase in (2, 1, 0):
        for kind in (0, 1):
            n = {2: (2, 4), 1: (2,), 0: (1,)}[phase]
            scratch.append(pltpu.VMEM((3, 6) + n + dims[kind], BF))
    for phase in (2, 1):
        for kind in (0, 1):
            n = {2: (4, 4), 1: (4,)}[phase]
            scratch.append(pltpu.VMEM((3,) + n + dims[kind], BF))
    for kind in (0, 1):
        scratch.append(pltpu.VMEM((3, 2, 2, 4) + dims[kind], BF))
    for n in ((4, 4), (4,), ()):
        scratch.append(pltpu.VMEM((3,) + n + (8, 128), F32))
    for n in ((4, 4, 4), (4, 4), (4,)):
        scratch.append(pltpu.VMEM(n + (8, 128), F32))
    scratch += [pltpu.SemaphoreType.DMA((3, 6, 6)), pltpu.SemaphoreType.DMA((3, 6, 6)), pltpu.SemaphoreType.DMA((3, 3)), pltpu.SemaphoreType.DMA((3, 3)), pltpu.SemaphoreType.DMA((6, 2)), pltpu.SemaphoreType.DMA((1,))]
    return pl.pallas_call(
        scatter_kernel,
        out_shape=(jax.ShapeDtypeStruct((3, ri, ci), F32), jax.ShapeDtypeStruct((3, ro, co), F32), jax.ShapeDtypeStruct((8, 128), F32)),
        in_specs=[any_] * 7,
        out_specs=(vm,) * 3,
        scratch_shapes=scratch,
        compiler_params=pltpu.CompilerParams(collective_id=1, has_side_effects=True, vmem_limit_bytes=62 * 1024 * 1024),
        name="scatter_grads",
    )(*win, *wout, small)


GROUPS = 6
LOG2E = 1.4426950408889634


def dot(a, b, dims=((1,), (0,)), precision=None):
    return lax.dot_general(a, b, (dims, ((), ())), preferred_element_type=F32, precision=precision)


def sigmoid(v):
    return 1.0 / (1.0 + jnp.exp(-v))


def split_dot(exact, wide, dims=((1,), (0,)), flip=False):
    total = None
    rest = wide
    for _ in range(3):
        term = rest.astype(BF)
        rest = rest - term.astype(F32)
        part = dot(term, exact, dims) if flip else dot(exact, term, dims)
        total = part if total is None else total + part
    return total


def compute_kernel(
    ends_ref, info_ref, allowed_ref, pg_ref, pe_ref, ph_ref, pn_ref, win_ref, wout_ref,
    ends_out, u_ref, o_ref, dv_ref, dp_ref, sg_ref, se_ref, sh_ref, sn_ref,
    swapped, leaving, send, recv, wbuf, ebuf, obuf, zbuf, xbuf, ybuf, tbuf, hbuf, pebuf, masks, tri, sel, qcol, qrow, dtrow, heads, smat, gbuf, dgacc, rowq, rowx, acc, rbuf,
    wsem, esem, osem,
):
    section = lax.axis_index("section")
    sibling = {"section": 1 - section}
    barrier = pltpu.get_barrier_semaphore()
    pl.semaphore_signal(barrier, inc=1, device_id=sibling, device_id_type=MESH)
    pl.semaphore_wait(barrier, 1)

    def across(n, src, dst):
        return pltpu.make_async_remote_copy(src, dst, send.at[n], recv.at[n], device_id=sibling, device_id_type=MESH)

    ends_copy = across(0, ends_ref.at[1 - section], swapped)
    ends_copy.start()

    def slot(l):
        return lax.select(section == l, 0, 2)

    def send_terms(l):
        @pl.when(section != l)
        def _():
            for n, ref in enumerate((u_ref, o_ref, dv_ref, dp_ref)):
                across(1 + n, ref.at[2], ref.at[1]).start()

    def copy_w(l, g):
        j, off = lax.div(g, 2), pl.multiple_of(lax.rem(g, 2) * 1024, 128)
        return pltpu.make_async_copy(win_ref.at[l, j, :, pl.ds(off, 1024)], wbuf.at[g], wsem.at[g])

    def copy_e(l, j):
        return pltpu.make_async_copy(win_ref.at[l, j, :, pl.ds(2048, 128)], ebuf.at[j], esem.at[j])

    def copy_o(l, j):
        return pltpu.make_async_copy(wout_ref.at[l, j], obuf.at[j], osem.at[j])

    for j in range(3):
        copy_e(0, j).start()
    for g in range(GROUPS):
        copy_w(0, jnp.int32(g)).start()
    for j in range(3):
        copy_o(0, j).start()

    info = info_ref[...]
    for d in range(3):
        masks[d] = jnp.broadcast_to(info[:, 2 + d : 3 + d], (128, 128))
    masks[3] = jnp.broadcast_to(info[:, 1:2], (128, 128))
    rows = lax.broadcasted_iota(jnp.int32, (128, 128), 0)
    cols = lax.broadcasted_iota(jnp.int32, (128, 128), 1)
    tri[...] = (rows >= cols).astype(F32).astype(BF)
    srow = lax.broadcasted_iota(jnp.int32, (512, 128), 0)
    scol = lax.broadcasted_iota(jnp.int32, (512, 128), 1)
    sel[...] = (lax.div(srow, 64) == scol).astype(F32).astype(BF)
    low_lanes = cols < 64

    def conv(px, taps, bias):
        s1 = pltpu.roll(px, 1, 0) * masks[0]
        s2 = pltpu.roll(px, 2, 0) * masks[1]
        s3 = pltpu.roll(px, 3, 0) * masks[2]
        c = bias + taps[3:4] * px + taps[2:3] * s1 + taps[1:2] * s2 + taps[0:1] * s3
        return c, (s3, s2, s1, px)

    def conv_back(dc, taps):
        out = taps[3:4] * dc
        out = out + taps[2:3] * pltpu.roll(dc * masks[0], 127, 0)
        out = out + taps[1:2] * pltpu.roll(dc * masks[1], 126, 0)
        return out + taps[0:1] * pltpu.roll(dc * masks[2], 125, 0)

    def total(v):
        return jnp.sum(v, axis=0, keepdims=True)

    def decay(g, hh):
        gap = jnp.broadcast_to(qcol[g][:, hh : hh + 1], (128, 128)) - qrow[g][hh : hh + 1, :]
        return jnp.exp2(jnp.minimum(gap, 0.0)) * dtrow[g][hh : hh + 1, :]

    def zero_lanes(v, keep):
        return jnp.where(keep, v, jnp.zeros_like(v))

    def forward(l, h):
        hbuf[l] = h.astype(BF)
        rs = lax.rsqrt(jnp.sum(h * h, axis=1, keepdims=True) * (1.0 / D) + EPSILON)
        rbuf[l, 0] = jnp.broadcast_to(rs, (128, 128))
        u_ref[slot(l)] = (h * rs * pn_ref[l, 0:1, :] * info_ref[:, 1:2]).astype(BF)
        for j in range(3):
            copy_e(l, j).wait()
            pebuf[l, j] = dot(u_ref[slot(l)], ebuf[j])
        if l == 0:
            for j in range(3):
                copy_e(1, j).start()
        for j in range(2):
            c, _ = conv(pebuf[l, j], pe_ref[l, j, 0:4], pe_ref[l, j, 4:5])
            smat[l, j] = (c * sigmoid(c)).astype(BF)
        v = pebuf[l, 2] + ph_ref[l, 0:1]
        dt = jnp.maximum(v, 0.0) + jnp.log1p(jnp.exp(-jnp.abs(v)))
        rate = -jnp.exp(ph_ref[l, 1:2])
        q = split_dot(tri[...], dt * rate) * LOG2E
        heads[l, 0] = dt
        heads[l, 1] = q
        gbuf[l] = dot(smat[l, 1], smat[l, 0], ((1,), (1,))) * allowed_ref[...]
        prepare(l)
        acc[:, 0:128] = jnp.zeros((128, 128), F32)

        def group(g, carry):
            copy_w(l, g).wait()
            p = dot(u_ref[slot(l)], wbuf[g])
            if l == 0:
                copy_w(1, g).start()
            zbuf[l, g] = p[:, 0:512]
            xbuf[l, g] = p[:, 512:1024]
            for k in range(4):
                at = slice(128 * k, 128 * k + 128)
                c, _ = conv(xbuf[l, g, :, at], pg_ref[l, g, 0:4, at], pg_ref[l, g, 4:5, at])
                x = c * sigmoid(c)
                xb = x.astype(BF)
                both = jnp.concatenate([zero_lanes(xb, low_lanes), zero_lanes(xb, ~low_lanes)], axis=0)
                w = jnp.concatenate([(gbuf[l] * decay(g, 2 * k + i)).astype(BF) for i in range(2)], axis=1)
                y = dot(w, both) + pg_ref[l, g, 6:7, at] * x
                ybuf[l, g, :, at] = y
                z = zbuf[l, g, :, at]
                e = y * (z * sigmoid(z))
                tbuf[g, :, at] = e
                acc[:, 0:128] += e * e
            return carry

        lax.fori_loop(0, GROUPS, group, 0)
        r = lax.rsqrt(jnp.sum(acc[:, 0:128], axis=1, keepdims=True) * (1.0 / DI) + EPSILON)
        rbuf[l, 1] = jnp.broadcast_to(r, (128, 128))
        for g in range(GROUPS):
            o_ref[slot(l), :, 512 * g : 512 * g + 512] = (tbuf[g] * r * pg_ref[l, g, 5:6, :]).astype(BF)
        for j in range(3):
            copy_o(l, j).wait()
            acc[:, 512 * j : 512 * j + 512] = dot(o_ref[slot(l)], obuf[j])
            if l == 0:
                copy_o(1, j).start()
        return h + acc[...]

    def prepare(l):
        q = heads[l, 1]
        qt = jnp.transpose(q)
        dtt = jnp.transpose(heads[l, 0])
        for g in range(GROUPS):
            qcol[g] = q if g == 0 else pltpu.roll(q, 128 - 8 * g, 1)
            qrow[g] = qt[8 * g : 8 * g + 8, :]
            dtrow[g] = dtt[8 * g : 8 * g + 8, :]

    def backward(l, dh):
        dv_ref[slot(l)] = dh.astype(BF)
        if l == 0:
            for j in range(3):
                copy_o(0, j).wait()
        sumcol = jnp.zeros((128, 128), F32)
        acc[:, 0:128] = sumcol

        def first(g, carry):
            do = None
            for j in range(3):
                part = dot(dv_ref[slot(l), :, 512 * j : 512 * j + 512], obuf[j, pl.ds(pl.multiple_of(512 * g, 512), 512), :], ((1,), (1,)))
                do = part if do is None else do + part
            tbuf[g] = do
            for k in range(4):
                at = slice(128 * k, 128 * k + 128)
                z = zbuf[l, g, :, at]
                e = ybuf[l, g, :, at] * (z * sigmoid(z))
                prod = tbuf[g, :, at] * e
                sg_ref[l, g, 5:6, at] = total(prod * rbuf[l, 1])
                acc[:, 0:128] += prod * pg_ref[l, g, 5:6, at]
            return carry

        lax.fori_loop(0, GROUPS, first, 0)
        if l == 1:
            for j in range(3):
                copy_o(0, j).start()
        r = rbuf[l, 1]
        coef = jnp.broadcast_to(jnp.sum(acc[:, 0:128], axis=1, keepdims=True) * (1.0 / DI), (128, 128)) * r * r * r
        masks[4] = coef
        prepare(l)
        dgacc[...] = jnp.zeros((128, 128), F32)
        rowq[...] = jnp.zeros((128, 128), F32)
        rowx[...] = jnp.zeros((128, 128), F32)
        acc[...] = jnp.zeros((128, D), F32)

        def second(g, carry):
            if l == 0:
                copy_w(0, g).wait()
            j, off = lax.div(g, 2), pl.multiple_of(lax.rem(g, 2) * 1024, 128)
            sums_q = None
            sums_x = None
            for k in range(4):
                at = slice(128 * k, 128 * k + 128)
                z = zbuf[l, g, :, at]
                y = ybuf[l, g, :, at]
                sz = sigmoid(z)
                silu = z * sz
                de = rbuf[l, 1] * (tbuf[g, :, at] * pg_ref[l, g, 5:6, at]) - (y * silu) * masks[4]
                dyb = (de * silu).astype(BF)
                dz = de * y * (sz + silu * (1.0 - sz))
                dp_ref[slot(l), j, :, pl.ds(pl.multiple_of(off + 128 * k, 128), 128)] = dz.astype(BF)
                taps = pg_ref[l, g, 0:4, at]
                c, shifts = conv(xbuf[l, g, :, at], taps, pg_ref[l, g, 4:5, at])
                sc = sigmoid(c)
                x = c * sc
                xb = x.astype(BF)
                dyw = dyb.astype(F32)
                skip = pg_ref[l, g, 6:7, at]
                xt = jnp.concatenate([zero_lanes(xb, low_lanes), zero_lanes(xb, ~low_lanes)], axis=0)
                dyt = jnp.concatenate([zero_lanes(dyb, low_lanes), zero_lanes(dyb, ~low_lanes)], axis=0)
                dw = dot(dyb, xt, ((1,), (1,)))
                ws = []
                dg = None
                for i in range(2):
                    e = decay(g, 2 * k + i)
                    ws.append((gbuf[l] * e).astype(BF))
                    part = dw[:, 128 * i : 128 * i + 128] * e
                    dg = part if dg is None else dg + part
                dgacc[...] += dg
                dx0 = dot(jnp.concatenate(ws, axis=0), dyt, ((0,), (0,)))
                dx = dx0 + skip * dyw
                sg_ref[l, g, 6:7, at] = total(dyw * x)
                mq = dyw * (y - skip * x)
                mx = xb.astype(F32) * dx0
                one = sel[128 * k : 128 * k + 128, :]
                for m, name in ((mq, "q"), (mx, "x")):
                    hi = m.astype(BF)
                    lo = (m - hi.astype(F32)).astype(BF)
                    part = dot(hi, one) + dot(lo, one)
                    if name == "q":
                        sums_q = part if sums_q is None else sums_q + part
                    else:
                        sums_x = part if sums_x is None else sums_x + part
                dc = dx * (sc + x * (1.0 - sc))
                for t in range(4):
                    sg_ref[l, g, t : t + 1, at] = total(dc * shifts[t])
                sg_ref[l, g, 4:5, at] = total(dc)
                dp_ref[slot(l), j, :, pl.ds(pl.multiple_of(off + 512 + 128 * k, 128), 128)] = conv_back(dc, taps).astype(BF)
            rowq[...] += pltpu.roll(sums_q, 8 * g, 1)
            rowx[...] += pltpu.roll(sums_x, 8 * g, 1)
            acc[...] += dot(dp_ref[slot(l), j, :, pl.ds(off, 1024)], wbuf[g], ((1,), (1,)))
            if l == 1:
                copy_w(0, g).start()
            return carry

        lax.fori_loop(0, GROUPS, second, 0)
        dg = (dgacc[...] * allowed_ref[...]).astype(BF)
        d_states = (dot(dg, smat[l, 1], ((0,), (0,))), dot(dg, smat[l, 0]))
        for j in range(2):
            taps = pe_ref[l, j, 0:4]
            c, shifts = conv(pebuf[l, j], taps, pe_ref[l, j, 4:5])
            sc = sigmoid(c)
            dc = d_states[j] * (sc + c * sc * (1.0 - sc))
            for t in range(4):
                se_ref[l, j, t : t + 1] = total(dc * shifts[t])
            se_ref[l, j, 4:5] = total(dc)
            dp_ref[slot(l), j, :, 2048:2176] = conv_back(dc, taps).astype(BF)
        v = pebuf[l, 2] + ph_ref[l, 0:1]
        sv = sigmoid(v)
        dt = heads[l, 0]
        rate = -jnp.exp(ph_ref[l, 1:2])
        back = split_dot(tri[...], rowq[...] - rowx[...], ((0,), (0,)))
        real = cols < H
        ratio = jnp.where(v < -15.0, 1.0, sv / jnp.maximum(dt, 1e-30))
        dr = jnp.where(real, rowx[...] * ratio + back * rate * sv, 0.0)
        sh_ref[l, 0:1] = total(dr)
        sh_ref[l, 1:2] = total(jnp.where(real, back * dt, 0.0)) * rate
        dp_ref[slot(l), 2, :, 2048:2176] = dr.astype(BF)
        du = acc[...]
        for j in range(3):
            if l == 0:
                copy_e(0, j).wait()
            du = du + dot(dp_ref[slot(l), j, :, 2048:2176], ebuf[j], ((1,), (1,)))
        if l == 1:
            for j in range(3):
                copy_e(0, j).start()
        h = hbuf[l].astype(F32)
        rs = rbuf[l, 0][:, 0:1]
        hn = h * rs
        du = du * info_ref[:, 1:2]
        sn_ref[l, 0:1, :] = total(du * hn)
        t = du * pn_ref[l, 0:1, :]
        s = jnp.sum(t * hn, axis=1, keepdims=True) * (1.0 / D)
        return dh + rs * (t - hn * s)

    ends_copy.wait()
    mine, theirs = ends_ref[section].astype(F32), swapped[...].astype(F32)
    leading = section == 0
    middle = forward(0, jnp.where(leading, mine, theirs)).astype(BF).astype(F32)
    out = forward(1, middle).astype(BF)

    end = across(5, leaving, ends_out.at[section])

    @pl.when(leading)
    def _():
        leaving[...] = out
        end.start()

    @pl.when(jnp.logical_not(leading))
    def _():
        ends_out[section] = out

    cotangent = jnp.where(leading, swapped[...].astype(F32), ends_ref[section].astype(F32))
    d_middle = backward(1, cotangent).astype(BF).astype(F32)
    send_terms(1)
    d_first = backward(0, d_middle).astype(BF)
    send_terms(0)

    @pl.when(leading)
    def _():
        ends_out[section] = d_first

    @pl.when(jnp.logical_not(leading))
    def _():
        leaving[...] = d_first
        end.start()

    for n, ref in enumerate((u_ref, o_ref, dv_ref, dp_ref)):
        across(1 + n, ref.at[2], ref.at[1]).wait()
    end.wait()


def compute(ends, info, allowed, pg, pe, ph, pn, win, wout):
    vm = pl.BlockSpec(memory_space=pltpu.VMEM)
    any_ = pl.BlockSpec(memory_space=pl.ANY)
    s = jax.ShapeDtypeStruct
    T = 128
    V = pltpu.VMEM
    return pl.pallas_call(
        compute_kernel,
        out_shape=(
            s((2, T, D), BF), s((3, T, D), BF), s((3, T, DI), BF), s((3, T, D), BF),
            s((3, 3, T, 2176), BF), s((2, 6, 8, 512), F32), s((2, 2, 8, 128), F32), s((2, 8, 128), F32), s((2, 8, D), F32),
        ),
        in_specs=[vm] * 7 + [any_] * 2,
        out_specs=(vm,) * 9,
        scratch_shapes=[
            V((T, D), BF), V((T, D), BF), pltpu.SemaphoreType.DMA((6,)), pltpu.SemaphoreType.DMA((6,)),
            V((6, D, 1024), BF), V((3, D, 128), BF), V((3, DI, 512), BF),
            V((2, 6, T, 512), F32), V((2, 6, T, 512), F32), V((2, 6, T, 512), F32), V((6, T, 512), F32), V((2, T, D), BF),
            V((2, 3, T, 128), F32), V((5, T, 128), F32), V((128, 128), BF), V((512, 128), BF),
            V((6, 128, 128), F32), V((6, 8, 128), F32), V((6, 8, 128), F32), V((2, 2, 128, 128), F32), V((2, 2, 128, 128), BF),
            V((2, 128, 128), F32), V((128, 128), F32), V((128, 128), F32), V((128, 128), F32), V((T, D), F32), V((2, 2, 128, 128), F32),
            pltpu.SemaphoreType.DMA((6,)), pltpu.SemaphoreType.DMA((3,)), pltpu.SemaphoreType.DMA((3,)),
        ],
        compiler_params=pltpu.CompilerParams(collective_id=2, has_side_effects=True, vmem_limit_bytes=62 * 1024 * 1024),
        cost_estimate=pl.CostEstimate(flops=23_000_000_000, bytes_accessed=100_000_000, transcendentals=10_000_000),
        name="layers",
    )(ends, info, allowed, pg, pe, ph, pn, win, wout)


def block_info(segment, valid_rows):
    pos = jnp.arange(128, dtype=jnp.int32)
    col = jnp.arange(128, dtype=jnp.int32)[None, :]
    linked = []
    for d in (1, 2, 3):
        before = jnp.concatenate([jnp.full((d,), -1, jnp.int32), segment[: 128 - d]])
        linked.append((before == segment).astype(F32))
    out = jnp.zeros((128, 128), F32)
    for lane, v in enumerate([segment.astype(F32), valid_rows] + linked):
        out = jnp.where(col == lane, v[:, None], out)
    allowed = ((pos[:, None] >= pos[None, :]) & (segment[:, None] == segment[None, :])).astype(F32)
    return out, allowed


def body(
    ends_in,
    seg_ids,
    block_counts,
    in_weight,
    conv_weight,
    conv_bias,
    pre_gain,
    gate_gain,
    out_weight,
    dt_bias,
    a_log,
    skip,
):
    section = lax.axis_index("section")
    length = seg_ids.shape[1]
    wide = lambda v: v[0].astype(F32)
    small = pack_small(wide(conv_weight), wide(conv_bias), wide(pre_gain), wide(gate_gain), (wide(dt_bias), wide(a_log), wide(skip)))
    own_in = jnp.stack(to_panels(in_weight[0]))
    own_out = jnp.stack([out_weight[0][:, 512 * j : 512 * j + 512] for j in range(3)])
    all_in, all_out, all_small = gather(own_in, own_out, small)
    params = layer_params(all_small.reshape(2, 64, 8, 128))
    pick = lambda v, i: lax.dynamic_index_in_dim(v, i, 0, keepdims=False)
    segment = pick(seg_ids, section)
    valid_rows = (jnp.arange(length, dtype=jnp.int32) < pick(block_counts, section)).astype(F32)
    info, allowed = block_info(segment, valid_rows)
    ends_out, u, o, dv, dp, sg, se, sh, sn = compute(
        ends_in[0].reshape(2, length, D), info, allowed, *params, all_in.reshape(2, 3, D, 2176), all_out.reshape(2, 3, DI, 512)
    )
    ends_out = ends_out.reshape(1, 2 * length, D)
    tiles = small_grads(sg, se, sh, sn)
    tiles = pick(tiles, section) + lax.ppermute(pick(tiles, 1 - section), "section", [(0, 1), (1, 0)])

    u, o, dv = (v[0:2].reshape(2 * length, -1) for v in (u, o, dv))
    dp = [jnp.concatenate([dp[0, j], dp[1, j]], axis=0) for j in range(3)]
    d_in = [jnp.dot(u.T, dp[j], preferred_element_type=F32).astype(BF).reshape(4, 4, 4, 24, 2176) for j in range(3)]
    d_out = [jnp.dot(o.T, dv[:, 512 * j : 512 * j + 512], preferred_element_type=F32).astype(BF).reshape(4, 4, 4, 48, 512) for j in range(3)]
    sum_in, sum_out, sums = scatter(d_in, d_out, tiles.reshape(4, 4, 4, 8, 128))
    d_in_weight = from_panels([sum_in[j] for j in range(3)])
    d_out_weight = jnp.concatenate([sum_out[j] for j in range(3)], axis=1)
    return (
        ends_out,
        d_in_weight[None],
        sums[None, 0:4, 0:52],
        sums[None, 4, 0:52],
        sums[None, 5, 0:24],
        sums[None, 6, 0:48],
        d_out_weight[None],
        sums[None, 7, 0:48],
        sums[None, 5, 64:112],
        sums[None, 6, 64:112],
    )


def solution(mesh):
    placed = (
        P("section", "dp", None),
        P("dp", None),
        P("dp"),
        P("section", "dp", None),
        P("section", None, "dp"),
        P("section", "dp"),
        P("section", "dp"),
        P("section", "dp"),
        P("section", "dp", None),
        P("section", None),
        P("section", None),
        P("section", None),
    )
    return jax.shard_map(
        body,
        mesh=mesh,
        in_specs=placed,
        out_specs=(
            P("section", "dp", None),
            P("section", "dp", None),
            P("section", None, "dp"),
            P("section", "dp"),
            P("section", "dp"),
            P("section", "dp"),
            P("section", "dp", None),
            P("section", None),
            P("section", None),
            P("section", None),
        ),
        check_vma=False,
    )
```

```python
import jax
import jax.numpy as jnp
from jax import lax
from jax.experimental import pallas as pl
from jax.experimental.pallas import tpu as pltpu
from jax.sharding import PartitionSpec as P

D = 1536
DI = 3072
N = 128
H = 48
CC = 3328
T = 128
EPSILON = 1e-05
F32 = jnp.float32
BF = jnp.bfloat16
GROUPS = 6
LOG2E = 1.4426950408889634
MESH = pl.DeviceIdType.MESH
KINDS = ((48, 1024), (48, 512), (16, 256))
ORDERS = ((2, 1, 0), (1, 0, 2), (0, 2, 1))
STREAMS = tuple((j, kind) for j in range(3) for kind in range(3))


def moved(pos, axis, by):
    out = list(pos)
    out[axis] = lax.rem(pos[axis] + by, 4)
    return tuple(out)


def block_index(order, phase, pos, half, sub=None):
    index = [pos[0], pos[1], pos[2]]
    for a in order[:phase]:
        index[a] = slice(None)
    if phase > 0 and half is not None:
        index[min(order[:phase])] = pl.ds(2 * half, 2) if sub is None else 2 * half + sub
    return tuple(index)


def has_half(kind, phase, half):
    return phase != 0 or half == (0 if kind == 0 else 1)


def dot(a, b, dims=((1,), (0,))):
    return lax.dot_general(a, b, (dims, ((), ())), preferred_element_type=F32)


def sigmoid(v):
    return 1.0 / (1.0 + jnp.exp(-v))


def total(v):
    return jnp.sum(v, axis=0, keepdims=True)


def exact_dot(zeros_ones, wide, dims=((1,), (0,)), flip=False, terms=3):
    out = None
    for _ in range(terms):
        term = wide.astype(BF)
        wide = wide - term.astype(F32)
        part = dot(term, zeros_ones, dims) if flip else dot(zeros_ones, term, dims)
        out = part if out is None else out + part
    return out


def keep_lanes(v, keep):
    return jnp.where(keep, v, jnp.zeros_like(v))


def step_kernel(*refs):
    it = iter(refs)
    take = lambda n: [next(it) for _ in range(n)]
    ends, segs, counts, win, taps_in, bias_in, pre_in, gate_in, wout, dtb_in, alog_in, skip_in = take(12)
    ends_out, d_win, d_taps, d_bias, d_pre, d_gate, d_wout, d_dtb, d_alog, d_skip = take(10)
    gath, grad, recv2, recv1, recv0 = take(3), take(3), take(3), take(3), take(3)
    wgot, egot, fgot, ggot, gs, par, hp, gr, tgot, sg2, sg1, sg0, swapped, leaving, us_, os_, dvs, dps, dpes = take(19)
    (s_misc, r_misc, s_ag, r_ag, s_small, r_small, s_sib, r_sib, s_rs, r_rs, s_terms, r_terms, own_sem, go_sem) = take(14)

    section = lax.axis_index("section")
    dp = lax.axis_index("dp")
    pos = (lax.div(dp, 16), lax.rem(lax.div(dp, 4), 4), lax.rem(dp, 4))
    parity = lax.rem(pos[2], 2)
    even = parity == 0
    partner = (pos[0], pos[1], pos[2] + 1 - 2 * parity)
    leading = section == 0

    def device(at, s=None):
        return {"section": section if s is None else s, "dp": at[0] * 16 + at[1] * 4 + at[2]}

    sibling = device(pos, 1 - section)

    def remote(src, dst, s, r, to):
        return pltpu.make_async_remote_copy(src, dst, s, r, device_id=to, device_id_type=MESH)

    def misc(n, src, dst, to):
        return remote(src, dst, s_misc.at[n], r_misc.at[n], to)

    barrier = pltpu.get_barrier_semaphore()
    for axis in range(3):
        for by in (1, 2, 3):
            pl.semaphore_signal(barrier, inc=1, device_id=device(moved(pos, axis, by)), device_id_type=MESH)
    pl.semaphore_signal(barrier, inc=1, device_id=sibling, device_id_type=MESH)

    def group_columns(g):
        return [pl.ds(pl.multiple_of(512 * g + first, 128), 512) for first in (0, DI)]

    def ag_copy(n, phase, slot, src, index, to):
        j, kind = STREAMS[n]
        return remote(src, gath[kind].at[section, j].at[index], s_ag.at[n, phase], r_ag.at[n, phase, slot], device(to))

    def ag_start(n, phase, unit=None):
        j, kind = STREAMS[n]
        order = ORDERS[j]
        right, left = moved(pos, order[phase], 1), moved(pos, order[phase], 3)
        for slot, (h, to) in enumerate(((0, right), (1, left), (1, right), (0, left))):
            if has_half(kind, phase, h):
                index = block_index(order, phase, pos, h)
                src = unit[kind].at[j] if phase == 0 else gath[kind].at[section, j].at[index]
                ag_copy(n, phase, slot, src, index, to).start()

    def ag_pieces(n, phase, at, h):
        order = ORDERS[STREAMS[n][0]]
        if phase < 2:
            return [block_index(order, phase, at, h)]
        return [block_index(order, phase, at, h, q) for q in range(2)]

    def to_sibling(n, index):
        j, kind = STREAMS[n]
        ref = gath[kind].at[section, j].at[index]
        remote(ref, ref, s_sib.at[n], r_sib.at[n], sibling).start()

    def ag_arrived(n, phase, slot, index):
        j, kind = STREAMS[n]
        ag_copy(n, phase, slot, gath[kind].at[section, j].at[index], index, moved(pos, 0, 1)).wait_recv()
        if phase == 2:
            to_sibling(n, index)

    def ag_forward(phase):
        for n, (j, kind) in enumerate(STREAMS):
            order = ORDERS[j]
            right, left = moved(pos, order[phase], 1), moved(pos, order[phase], 3)
            for slot, h, source, to in ((0, 0, left, right), (1, 1, right, left)):
                if has_half(kind, phase, h):
                    ag_arrived(n, phase, slot, block_index(order, phase, source, h))
                    for q, index in enumerate(ag_pieces(n, phase, source, h)):
                        ag_copy(n, phase, 4 + 2 * slot + q, gath[kind].at[section, j].at[index], index, to).start()

    def ag_rest(phase):
        for n, (j, kind) in enumerate(STREAMS):
            order = ORDERS[j]
            right, left = moved(pos, order[phase], 1), moved(pos, order[phase], 3)
            for slot, h, source in ((2, 1, left), (3, 0, right)):
                if has_half(kind, phase, h):
                    ag_arrived(n, phase, slot, block_index(order, phase, source, h))
        for q in range(2 if phase == 2 else 1):
            for n, (j, kind) in enumerate(STREAMS):
                far = moved(pos, ORDERS[j][phase], 2)
                for slot in (0, 1):
                    if has_half(kind, phase, slot):
                        ag_arrived(n, phase, 4 + 2 * slot + q, ag_pieces(n, phase, far, slot)[q])

    def ag_sent(phase):
        for n, (j, kind) in enumerate(STREAMS):
            index = {0: (0, 0, pl.ds(0, 3)), 1: (0, pl.ds(0, 3)), 2: (pl.ds(0, 3),)}[phase]
            ref = gath[kind].at[section, j].at[index]
            remote(ref, ref, s_ag.at[n, phase], r_ag.at[n, phase, 0], sibling).wait_send()

    def small_gather(phase):
        axis = (2, 1, 0)[phase]
        index = tuple(pos[: 3 - phase])
        sent = []
        for by in (1, 2, 3):
            ref = gs.at[section].at[index]
            c = remote(ref, ref, s_small.at[phase, by - 1], r_small.at[phase, by - 1], device(moved(pos, axis, by)))
            c.start()
            sent.append(c)
        return sent

    swap_ends = misc(2, ends.at[1 - section], swapped, sibling)

    def prologue(wsend, esend, uw, uo, ue, us):
        unit = (uw, uo, ue)
        bc = win[:, 2 * DI : 2 * DI + 2 * N].astype(F32)
        rz = jnp.concatenate([win[:, 2 * DI + 2 * N :].astype(F32), jnp.zeros((24, 2 * N - H), F32)], axis=1)
        for j in range(3):
            for i, at in enumerate(group_columns(2 * j + 1 - parity)):
                wsend[j, :, 512 * i : 512 * i + 512] = win[:, at]
        esend[...] = jnp.where(even, rz, bc).astype(BF)
        us[...] = jnp.zeros((8, 128), F32)
        us[0:4, 0:52] = taps_in[...].astype(F32)
        us[4:5, 0:52] = bias_in[...].astype(F32)
        us[5:6, 0:24] = pre_in[...].astype(F32)
        us[6:7, 0:48] = gate_in[...].astype(F32)
        us[7:8, 0:48] = dtb_in[...].astype(F32)
        us[5:6, 64:112] = alog_in[...].astype(F32)
        us[6:7, 64:112] = skip_in[...].astype(F32)
        gs[section, pos[0], pos[1], pos[2]] = us[...]
        for j in range(3):
            uo[j] = wout[:, 512 * j : 512 * j + 512]

        pl.semaphore_wait(barrier, 10)
        swap_w = misc(0, wsend, wgot, device(partner))
        swap_e = misc(1, esend, egot, device(partner))
        for c in (swap_w, swap_e, swap_ends):
            c.start()

        small = small_gather(0)
        swap_w.wait()
        swap_e.wait()
        for j in range(3):
            for i, at in enumerate(group_columns(2 * j + parity)):
                lanes = slice(512 * i, 512 * i + 512)
                mine, theirs = win[:, at].astype(F32), wgot[j, :, lanes].astype(F32)
                uw[j, :, lanes] = jnp.concatenate([jnp.where(even, mine, theirs), jnp.where(even, theirs, mine)], axis=0).astype(BF)
        mine, theirs = jnp.where(even, bc, rz), egot[...].astype(F32)
        both = jnp.concatenate([jnp.where(even, mine, theirs), jnp.where(even, theirs, mine)], axis=0).astype(BF)
        for j in range(3):
            ue[j] = both[16 * j : 16 * j + 16, :]
        own = []
        for n, (j, kind) in enumerate(STREAMS):
            ag_start(n, 0, unit)
            c = pltpu.make_async_copy(unit[kind].at[j], gath[kind].at[section, j].at[pos], own_sem.at[n])
            c.start()
            own.append(c)
        for c in small:
            c.wait()
        small = small_gather(1)
        ag_forward(0)
        for c in own:
            c.wait()
        ag_rest(0)
        for n in range(9):
            ag_start(n, 1)
        for c in small:
            c.wait()
        small = small_gather(2)
        ag_forward(1)
        ag_rest(1)
        for c in small:
            c.wait()
        ag_sent(0)

    pl.run_scoped(
        prologue,
        pltpu.VMEM((3, 24, 1024), BF), pltpu.VMEM((24, 256), BF), pltpu.VMEM((3, 48, 1024), BF), pltpu.VMEM((3, 48, 512), BF), pltpu.VMEM((3, 16, 256), BF), pltpu.VMEM((8, 128), F32),
    )
    small_across = misc(3, gs.at[section], gs.at[section], sibling)
    small_across.start()

    @pl.when(leading)
    def _():
        for n in range(9):
            ag_start(n, 2)
    for n, (j, kind) in enumerate(STREAMS):
        to_sibling(n, block_index(ORDERS[j], 2, pos, None))
    ag_sent(1)

    misc(3, gs.at[1 - section], gs.at[1 - section], sibling).wait()
    for l in range(2):
        hp[l] = gs[l, 0, 0, 0]
        for i in range(64):
            tile = gs.at[l, i // 16, i // 4 % 4, i % 4]
            par[l, 0:5, 52 * i : 52 * i + 52] = tile[0:5, 0:52]
            par[l, 7:8, 24 * i : 24 * i + 24] = tile[5:6, 0:24]
            par[l, 5:6, 48 * i : 48 * i + 48] = tile[6:7, 0:48]
    swap_ends.wait()

    @pl.when(leading)
    def _():
        ag_forward(2)
        ag_rest(2)
        ag_sent(2)
        pl.semaphore_signal(go_sem, inc=1, device_id=sibling, device_id_type=MESH)

    @pl.when(jnp.logical_not(leading))
    def _():
        pl.semaphore_wait(go_sem, 1)
        for n in range(9):
            ag_start(n, 2)

    def from_sibling(l):
        for n, (j, kind) in enumerate(STREAMS):
            ref = gath[kind].at[l, j]
            remote(ref, ref, s_sib.at[n], r_sib.at[n], sibling).wait_recv()

    @pl.when(jnp.logical_not(leading))
    def _():
        from_sibling(0)

    def rs_copy(n, phase, slot, src, to):
        j, kind = STREAMS[n]
        dst = (recv0, recv1, recv2)[phase][kind].at[j, slot]
        return remote(src, dst, s_rs.at[n, phase], r_rs.at[n, phase, slot], device(to))

    def rs_start(n, phase, part):
        j, kind = STREAMS[n]
        axis = ORDERS[j][phase]
        right, left, far = (moved(pos, axis, by) for by in (1, 3, 2))
        for slot, at, h, to in ((0, far, 0, left), (1, far, 1, right), (2, left, 1, left), (3, right, 0, right)):
            if has_half(kind, phase, h):
                rs_copy(n, phase, slot, part(n, at[axis], h), to).start()

    def grad_part(n, k, h):
        j, kind = STREAMS[n]
        at = list(pos)
        at[ORDERS[j][2]] = k
        return grad[kind].at[(j,) + block_index(ORDERS[j], 2, tuple(at), h)]

    def term(n, src, dst):
        return remote(src, dst, s_terms.at[n], r_terms.at[n], sibling)

    def dterm(g):
        return term(3 + g, dps.at[12 + lax.rem(g, 2)], dps.at[6 + g])

    def layers(wbuf, ebuf, obuf, zbuf, xbuf, ybuf, tbuf, hbuf, pebuf, masks, allowed, tri, sel, qcol, qrow, dtrow, heads, smat, gbuf, dgacc, rowq, rowx, acc, rbuf, wstage, ostage, estage, wsem, esem, osem, wssem, ossem, essem):
        def copy_w(l, g):
            j, p = lax.div(g, 2), lax.rem(g, 2)
            return [pltpu.make_async_copy(gath[0].at[l, j, :, :, 2 * m + p], wbuf.at[g, :, :, pl.ds(48 * m, 48)], wsem.at[g, m]) for m in range(2)]

        def copy_e(l):
            return [pltpu.make_async_copy(gath[2].at[l, j, :, :, 2 * m + p], ebuf.at[p, :, :, m, j], esem.at[p, m, j]) for p in range(2) for m in range(2) for j in range(3)]

        def copy_o(l, j):
            return [pltpu.make_async_copy(gath[1].at[l, j], obuf.at[j], osem.at[j])]

        def start(copies):
            for c in copies:
                c.start()

        def finish(copies):
            for c in copies:
                c.wait()

        def weights_e(p):
            return ebuf[p].reshape(D, 256)

        start(copy_e(0))
        for g in range(GROUPS):
            start(copy_w(0, jnp.int32(g)))
        for j in range(3):
            start(copy_o(0, j))

        rows = lax.broadcasted_iota(jnp.int32, (T, T), 0)
        cols = lax.broadcasted_iota(jnp.int32, (T, T), 1)
        seg = jnp.where(leading, segs[0:1, :], segs[1:2, :]).astype(F32)
        seg_s = jnp.broadcast_to(seg, (T, T))
        seg_t = jnp.transpose(seg_s)
        allowed[...] = jnp.where(rows >= cols, jnp.where(seg_t == seg_s, 1.0, 0.0), 0.0)
        for d in (1, 2, 3):
            masks[d - 1] = jnp.where(rows >= d, jnp.where(pltpu.roll(seg_t, d, 0) == seg_t, 1.0, 0.0), 0.0)
        masks[3] = jnp.where(rows < counts[section], 1.0, 0.0)
        tri[...] = jnp.where(rows >= cols, 1.0, 0.0).astype(BF)
        srow = lax.broadcasted_iota(jnp.int32, (512, T), 0)
        scol = lax.broadcasted_iota(jnp.int32, (512, T), 1)
        sel[...] = jnp.where(lax.div(srow, 64) == scol, 1.0, 0.0).astype(BF)
        low_lanes = cols < 64
        for l in range(2):
            skips = hp[l, 6:7, 64:112]
            skips = jnp.concatenate([skips, jnp.zeros((1, 80), F32)], axis=1)
            skips = jnp.broadcast_to(skips, (8, T))
            for g in range(GROUPS):
                mine = skips if g == 0 else pltpu.roll(skips, T - 8 * g, 1)
                mine = jnp.where(cols[0:8] < 8, mine, 0.0)
                par[l, 6:7, 512 * g : 512 * g + 512] = dot(mine.astype(BF), sel[...], ((1,), (1,)))[0:1]

        def conv(px, taps, bias):
            s1 = pltpu.roll(px, 1, 0) * masks[0]
            s2 = pltpu.roll(px, 2, 0) * masks[1]
            s3 = pltpu.roll(px, 3, 0) * masks[2]
            c = bias + taps[3:4] * px + taps[2:3] * s1 + taps[1:2] * s2 + taps[0:1] * s3
            return c, (s3, s2, s1, px)

        def conv_back(dc, taps):
            out = taps[3:4] * dc
            out = out + taps[2:3] * pltpu.roll(dc * masks[0], T - 1, 0)
            out = out + taps[1:2] * pltpu.roll(dc * masks[1], T - 2, 0)
            return out + taps[0:1] * pltpu.roll(dc * masks[2], T - 3, 0)

        def decay(g, hh):
            gap = jnp.broadcast_to(qcol[g][:, hh : hh + 1], (T, T)) - qrow[g][hh : hh + 1, :]
            return jnp.exp2(jnp.minimum(gap, 0.0)) * dtrow[g][hh : hh + 1, :]

        def rate_bias(l):
            return hp[l, 7:8, :]

        def rate(l):
            tile = pltpu.roll(hp[l], 64, 1)
            return -jnp.exp(jnp.where(cols[0:1] < H, tile[5:6, :], 0.0))

        def tile_at(g, k):
            return pl.ds(pl.multiple_of(512 * g + 128 * k, 128), 128)

        def prepare(l):
            q = heads[l, 1]
            qt = jnp.transpose(q)
            dtt = jnp.transpose(heads[l, 0])
            for g in range(GROUPS):
                qcol[g] = q if g == 0 else pltpu.roll(q, T - 8 * g, 1)
                qrow[g] = qt[8 * g : 8 * g + 8, :]
                dtrow[g] = dtt[8 * g : 8 * g + 8, :]

        def slot(l):
            return lax.select(section == l, 0, 2)

        def first_input():
            return jnp.where(leading, ends[section].astype(F32), swapped[...].astype(F32))

        def forward(l, h):
            if l == 1:
                hbuf[...] = h.astype(BF)
            rs = lax.rsqrt(jnp.sum(h * h, axis=1, keepdims=True) * (1.0 / D) + EPSILON)
            rbuf[l, 0] = jnp.broadcast_to(rs, (T, T))
            us_[slot(l)] = (h * rs * par[l, 7:8, 0:D] * masks[3][:, 0:1]).astype(BF)
            finish(copy_e(l))
            pebuf[l, :, 0:256] = dot(us_[slot(l)], weights_e(0))
            pebuf[l, :, 256:384] = dot(us_[slot(l)], weights_e(1))[:, 0:128]
            for j in range(2):
                at = slice(DI + 128 * j, DI + 128 * j + 128)
                c, _ = conv(pebuf[l, :, 128 * j : 128 * j + 128], par[l, 0:4, at], par[l, 4:5, at])
                smat[l, j] = (c * sigmoid(c)).astype(BF)
            v = pebuf[l, :, 256:384] + rate_bias(l)
            dt = jnp.maximum(v, 0.0) + jnp.log1p(jnp.exp(-jnp.abs(v)))
            heads[l, 0] = dt
            heads[l, 1] = exact_dot(tri[...], dt * rate(l)) * LOG2E
            gbuf[l] = dot(smat[l, 1], smat[l, 0], ((1,), (1,))) * allowed[...]
            prepare(l)
            acc[:, 0:128] = jnp.zeros((T, T), F32)

            def group(g, carry):
                finish(copy_w(l, g))
                p = dot(us_[slot(l)], wbuf[g].reshape(D, 1024))
                wide = pl.ds(pl.multiple_of(512 * g, 128), 512)
                zbuf[l, :, wide] = p[:, 0:512]
                xbuf[l, :, wide] = p[:, 512:1024]
                for k in range(4):
                    at = tile_at(g, k)
                    c, _ = conv(xbuf[l, :, at], par[l, 0:4, at], par[l, 4:5, at])
                    x = c * sigmoid(c)
                    xb = x.astype(BF)
                    both = jnp.concatenate([keep_lanes(xb, low_lanes), keep_lanes(xb, ~low_lanes)], axis=0)
                    w = jnp.concatenate([(gbuf[l] * decay(g, 2 * k + i)).astype(BF) for i in range(2)], axis=1)
                    y = dot(w, both) + par[l, 6:7, at] * x
                    ybuf[l, :, at] = y
                    z = zbuf[l, :, at]
                    e = y * (z * sigmoid(z))
                    tbuf[:, at] = e
                    acc[:, 0:128] += e * e
                return carry

            lax.fori_loop(0, GROUPS, group, 0)
            r = lax.rsqrt(jnp.sum(acc[:, 0:128], axis=1, keepdims=True) * (1.0 / DI) + EPSILON)
            rbuf[l, 1] = jnp.broadcast_to(r, (T, T))
            for g in range(GROUPS):
                at = slice(512 * g, 512 * g + 512)
                os_[slot(l), :, at] = (tbuf[:, at] * r * par[l, 5:6, at]).astype(BF)
            for j in range(3):
                finish(copy_o(l, j))
                acc[:, 512 * j : 512 * j + 512] = dot(os_[slot(l)], obuf[j].reshape(DI, 512))
            return h + acc[...]

        def backward(l, dh):
            dvs[slot(l)] = dh.astype(BF)

            @pl.when(section != l)
            def _():
                for n, ref in enumerate((us_, os_, dvs)):
                    term(n, ref.at[2], ref.at[1]).start()

            if l == 0:
                for j in range(3):
                    finish(copy_o(0, j))
            acc[:, 0:128] = jnp.zeros((T, T), F32)

            def first(zz, carry):
                wide = pl.ds(pl.multiple_of(768 * zz, 128), 768)
                do = None
                for j in range(3):
                    part = dot(dvs[slot(l), :, 512 * j : 512 * j + 512], obuf[j, zz].reshape(768, 512), ((1,), (1,)))
                    do = part if do is None else do + part
                tbuf[:, wide] = do
                for k in range(6):
                    at = pl.ds(pl.multiple_of(768 * zz + 128 * k, 128), 128)
                    z = zbuf[l, :, at]
                    e = ybuf[l, :, at] * (z * sigmoid(z))
                    prod = tbuf[:, at] * e
                    gr[l, 5:6, at] = total(prod * rbuf[l, 1])
                    acc[:, 0:128] += prod * par[l, 5:6, at]
                return carry

            lax.fori_loop(0, 4, first, 0)
            if l == 1:
                for j in range(3):
                    start(copy_o(0, j))
            r = rbuf[l, 1]
            masks[4] = jnp.broadcast_to(jnp.sum(acc[:, 0:128], axis=1, keepdims=True) * (1.0 / DI), (T, T)) * r * r * r
            prepare(l)
            dgacc[...] = jnp.zeros((T, T), F32)
            rowq[...] = jnp.zeros((T, T), F32)
            rowx[...] = jnp.zeros((T, T), F32)
            acc[...] = jnp.zeros((T, D), F32)

            def second(g, carry):
                if l == 0:
                    finish(copy_w(0, g))

                here = lax.select(section == l, g, 12 + lax.rem(g, 2))

                @pl.when(jnp.logical_and(section != l, g >= 2))
                def _():
                    dterm(g - 2).wait_send()

                sums_q, sums_x = None, None
                for k in range(4):
                    at = tile_at(g, k)
                    z = zbuf[l, :, at]
                    y = ybuf[l, :, at]
                    sz = sigmoid(z)
                    silu = z * sz
                    de = rbuf[l, 1] * (tbuf[:, at] * par[l, 5:6, at]) - (y * silu) * masks[4]
                    dyb = (de * silu).astype(BF)
                    dz = de * y * (sz + silu * (1.0 - sz))
                    dps[here, :, 128 * k : 128 * k + 128] = dz.astype(BF)
                    taps = par[l, 0:4, at]
                    c, shifts = conv(xbuf[l, :, at], taps, par[l, 4:5, at])
                    sc = sigmoid(c)
                    x = c * sc
                    xb = x.astype(BF)
                    dyw = dyb.astype(F32)
                    skip = par[l, 6:7, at]
                    xt = jnp.concatenate([keep_lanes(xb, low_lanes), keep_lanes(xb, ~low_lanes)], axis=0)
                    dyt = jnp.concatenate([keep_lanes(dyb, low_lanes), keep_lanes(dyb, ~low_lanes)], axis=0)
                    dw = dot(dyb, xt, ((1,), (1,)))
                    ws, dg = [], None
                    for i in range(2):
                        e = decay(g, 2 * k + i)
                        ws.append((gbuf[l] * e).astype(BF))
                        part = dw[:, 128 * i : 128 * i + 128] * e
                        dg = part if dg is None else dg + part
                    dgacc[...] += dg
                    dx0 = dot(jnp.concatenate(ws, axis=0), dyt, ((0,), (0,)))
                    dx = dx0 + skip * dyw
                    gr[l, 6:7, at] = total(dyw * x)
                    one = sel[128 * k : 128 * k + 128, :]
                    part = exact_dot(one, dyw * (y - skip * x), flip=True, terms=2)
                    sums_q = part if sums_q is None else sums_q + part
                    part = exact_dot(one, xb.astype(F32) * dx0, flip=True, terms=2)
                    sums_x = part if sums_x is None else sums_x + part
                    dc = dx * (sc + x * (1.0 - sc))
                    for t in range(4):
                        gr[l, t : t + 1, at] = total(dc * shifts[t])
                    gr[l, 4:5, at] = total(dc)
                    dps[here, :, 512 + 128 * k : 640 + 128 * k] = conv_back(dc, taps).astype(BF)
                rowq[...] += pltpu.roll(sums_q, 8 * g, 1)
                rowx[...] += pltpu.roll(sums_x, 8 * g, 1)

                @pl.when(section != l)
                def _():
                    dterm(g).start()

                acc[...] += dot(dps[here], wbuf[g].reshape(D, 1024), ((1,), (1,)))
                if l == 1:
                    start(copy_w(0, g))
                return carry

            lax.fori_loop(0, GROUPS, second, 0)
            dg = (dgacc[...] * allowed[...]).astype(BF)
            d_states = (dot(dg, smat[l, 1], ((0,), (0,))), dot(dg, smat[l, 0]))
            for j in range(2):
                at = slice(DI + 128 * j, DI + 128 * j + 128)
                taps = par[l, 0:4, at]
                c, shifts = conv(pebuf[l, :, 128 * j : 128 * j + 128], taps, par[l, 4:5, at])
                sc = sigmoid(c)
                dc = d_states[j] * (sc + c * sc * (1.0 - sc))
                for t in range(4):
                    gr[l, t : t + 1, at] = total(dc * shifts[t])
                gr[l, 4:5, at] = total(dc)
                dpes[slot(l), 0, :, 128 * j : 128 * j + 128] = conv_back(dc, taps).astype(BF)
            v = pebuf[l, :, 256:384] + rate_bias(l)
            sv = sigmoid(v)
            dt = heads[l, 0]
            back = exact_dot(tri[...], rowq[...] - rowx[...], ((0,), (0,)))
            ratio = jnp.where(v < -15.0, 1.0, sv / jnp.maximum(dt, 1e-30))
            dr = jnp.where(cols < H, rowx[...] * ratio + back * rate(l) * sv, 0.0)
            d_rate = total(jnp.where(cols < H, back * dt, 0.0)) * rate(l)
            dpes[slot(l), 1, :, 0:128] = dr.astype(BF)
            dpes[slot(l), 1, :, 128:256] = jnp.zeros((T, T), BF)

            @pl.when(section != l)
            def _():
                term(9, dpes.at[2], dpes.at[1]).start()

            if l == 0:
                finish(copy_e(0))
            du = acc[...]
            for p in range(2):
                du = du + dot(dpes[slot(l), p], weights_e(p), ((1,), (1,)))
            if l == 1:
                start(copy_e(0))
            h = hbuf[...].astype(F32) if l == 1 else first_input()
            hn = h * rbuf[l, 0][:, 0:1]
            du = du * masks[3][:, 0:1]
            gr[l, 7:8, 0:D] = total(du * hn)
            t = du * par[l, 7:8, 0:D]
            s = jnp.sum(t * hn, axis=1, keepdims=True) * (1.0 / D)
            dh_in = dh + rbuf[l, 0][:, 0:1] * (t - hn * s)
            skips = jnp.zeros((8, T), F32)
            for g in range(GROUPS):
                mine = exact_dot(sel[...], jnp.broadcast_to(gr[l, 6:7, 512 * g : 512 * g + 512], (8, 512)), flip=True)
                skips = skips + (mine if g == 0 else pltpu.roll(mine, 8 * g, 1))
            for i in range(64):
                tile = gs.at[l, i // 16, i // 4 % 4, i % 4]
                tile[0:5, 0:52] = gr[l, 0:5, 52 * i : 52 * i + 52]
                tile[5:6, 0:24] = gr[l, 7:8, 24 * i : 24 * i + 24]
                tile[6:7, 0:48] = gr[l, 5:6, 48 * i : 48 * i + 48]
                tile[7:8, 0:128] = total(dr)
                tile[5:6, 64:112] = d_rate[:, 0:48]
                tile[6:7, 64:112] = skips[0:1, 0:48]

            @pl.when(section != l)
            def _():
                term(10, gs.at[l], tgot).start()

            return dh_in

        def products(l):
            for n, ref in enumerate((us_, os_, dvs)):
                term(n, ref.at[2], ref.at[1]).wait_recv()
            for g in range(GROUPS):
                dterm(g).wait_recv()
            term(9, dpes.at[2], dpes.at[1]).wait_recv()

            def stacked(ref, *index):
                return jnp.concatenate([ref[(0,) + index], ref[(1,) + index]], axis=0)

            for p in range(2):
                de = dot(stacked(us_), stacked(dpes, p), ((0,), (0,))).astype(BF).reshape(4, 4, 2, 3, 16, 256)
                for j in range(3):
                    for m in range(2):
                        estage[j, m] = de[:, :, m, j]
                ecopies = [pltpu.make_async_copy(estage.at[j, m], grad[2].at[j, :, :, 2 * m + p], essem.at[j, m]) for j in range(3) for m in range(2)]
                start(ecopies)
                finish(ecopies)
            def w_at(i):
                return lax.div(i, 8), lax.rem(lax.div(i, 2), 4), lax.rem(i, 2), pl.multiple_of(512 * lax.rem(i, 2), 128)

            for j in range(3):
                def wcopy(i):
                    g, zz, b, wide = w_at(i)
                    return [pltpu.make_async_copy(wstage.at[b, :, pl.ds(48 * m, 48)], grad[0].at[j, zz, :, 2 * m + g, :, pl.ds(wide, 512)], wssem.at[b, m]) for m in range(2)]

                def wstep(i, carry):
                    @pl.when(i >= 2)
                    def _():
                        finish(wcopy(i - 2))
                    g, zz, b, wide = w_at(i)
                    u = stacked(us_, slice(None), pl.ds(pl.multiple_of(384 * zz, 128), 384))
                    at = pl.ds(wide, 512)
                    d = jnp.concatenate([dps[2 * j + g, :, at], dps[6 + 2 * j + g, :, at]], axis=0)
                    wstage[b] = dot(u, d, ((0,), (0,))).astype(BF).reshape(4, 96, 512)
                    start(wcopy(i))
                    return carry

                lax.fori_loop(0, 16, wstep, 0)
                for i in (14, 15):
                    finish(wcopy(jnp.int32(i)))
                rs_start(3 * j, 2, grad_part)

                def ocopy(i):
                    b = lax.rem(i, 2)
                    return [pltpu.make_async_copy(ostage.at[b], grad[1].at[j, lax.div(i, 4), pl.ds(2 * lax.rem(lax.div(i, 2), 2), 2), :, :, pl.ds(pl.multiple_of(256 * b, 128), 256)], ossem.at[b])]

                def ostep(i, carry):
                    @pl.when(i >= 2)
                    def _():
                        finish(ocopy(i - 2))
                    o = stacked(os_, slice(None), pl.ds(pl.multiple_of(384 * lax.div(i, 2), 128), 384))
                    b = lax.rem(i, 2)
                    ostage[b] = dot(o, stacked(dvs, slice(None), pl.ds(pl.multiple_of(512 * j + 256 * b, 128), 256)), ((0,), (0,))).astype(BF).reshape(2, 4, 48, 256)
                    start(ocopy(i))
                    return carry

                lax.fori_loop(0, 16, ostep, 0)
                for i in (14, 15):
                    finish(ocopy(jnp.int32(i)))
                rs_start(3 * j + 1, 2, grad_part)
                rs_start(3 * j + 2, 2, grad_part)

        middle = forward(0, first_input()).astype(BF).astype(F32)

        @pl.when(jnp.logical_not(leading))
        def _():
            ag_forward(2)
            ag_rest(2)

        @pl.when(leading)
        def _():
            from_sibling(1)

        start(copy_e(1))
        for g in range(GROUPS):
            start(copy_w(1, jnp.int32(g)))
        for j in range(3):
            start(copy_o(1, j))
        out = forward(1, middle).astype(BF)

        @pl.when(leading)
        def _():
            leaving[...] = out

        @pl.when(jnp.logical_not(leading))
        def _():
            ends_out[section] = out

        cotangent = jnp.where(leading, swapped[...].astype(F32), ends[section].astype(F32))
        d_middle = backward(1, cotangent).astype(BF).astype(F32)

        @pl.when(jnp.logical_not(leading))
        def _():
            products(1)

        d_first = backward(0, d_middle).astype(BF)

        @pl.when(leading)
        def _():
            ends_out[section] = d_first
            products(0)

        @pl.when(jnp.logical_not(leading))
        def _():
            leaving[...] = d_first

    V = pltpu.VMEM
    pl.run_scoped(
        layers,
        V((6, 4, 4, 96, 1024), BF), V((2, 4, 4, 2, 3, 16, 256), BF), V((3, 4, 4, 4, 48, 512), BF),
        V((2, T, DI), F32), V((2, T, DI), F32), V((2, T, DI), F32), V((T, DI), F32), V((T, D), BF), V((2, T, 384), F32),
        V((5, T, T), F32), V((T, T), F32), V((T, T), BF), V((512, T), BF), V((6, T, T), F32), V((6, 8, T), F32), V((6, 8, T), F32),
        V((2, 2, T, T), F32), V((2, 2, T, T), BF), V((2, T, T), F32), V((T, T), F32), V((T, T), F32), V((T, T), F32), V((T, D), F32), V((2, 2, T, T), F32),
        V((2, 4, 96, 512), BF), V((2, 2, 4, 48, 256), BF), V((3, 2, 4, 4, 16, 256), BF),
        pltpu.SemaphoreType.DMA((6, 2)), pltpu.SemaphoreType.DMA((2, 2, 3)), pltpu.SemaphoreType.DMA((3,)), pltpu.SemaphoreType.DMA((2, 2)), pltpu.SemaphoreType.DMA((2,)), pltpu.SemaphoreType.DMA((3, 2)),
    )

    end = misc(4, leaving, ends_out.at[section], sibling)
    end.start()

    def sums(*bufs):
        it = iter(bufs)
        take = lambda n: [next(it) for _ in range(n)]
        ab, ob, db, eb, acc2, acc1, b1, b0, fin = (take(3) for _ in range(9))
        fsend, gsend, sa2, sa1, lsem = it

        def load(n, h, which, src, dst):
            return pltpu.make_async_copy(src, dst, lsem.at[n, h, which])

        def add(dst, parts, dims, dtype, place=None):
            if not dims:
                out = parts[0][...].astype(F32)
                for p in parts[1:]:
                    out = out + p[...].astype(F32)
                dst[...] = out.astype(dtype)
                return
            count = dims[0] * (dims[1] if len(dims) > 1 else 1)

            def one(i, carry):
                index = (i,) if len(dims) == 1 else (lax.div(i, dims[1]), lax.rem(i, dims[1]))
                out = parts[0][index].astype(F32)
                for p in parts[1:]:
                    out = out + p[index].astype(F32)
                dst[index if place is None else place(*index)] = out.astype(dtype)
                return carry

            lax.fori_loop(0, count, one, 0)

        def neighbours(n, phase):
            axis = ORDERS[STREAMS[n][0]][phase]
            right, left = moved(pos, axis, 1), moved(pos, axis, 3)
            return pos[axis], {0: (0, left[axis], left, 4, 3), 1: (1, right[axis], right, 5, 2)}

        def sent(phase):
            for n, (j, kind) in enumerate(STREAMS):
                ref = (recv0, recv1, recv2)[phase][kind].at[j, pl.ds(0, 3 if phase == 0 else 6)]
                remote(ref, ref, s_rs.at[n, phase], r_rs.at[n, phase, 0], sibling).wait_send()

        items = {phase: [(n, h) for n, (j, kind) in enumerate(STREAMS) for h in (0, 1) if has_half(kind, phase, h)] for phase in range(3)}

        def small_start(phase):
            axis = ORDERS[0][phase]
            cur = (sa1, sa2, gs.at[section])[phase]
            got = (sg0, sg1, sg2)[phase]
            copies = []
            for by in (1, 2, 3):
                to = moved(pos, axis, by)
                c = remote(cur.at[to[axis]], got.at[by - 1], s_small.at[3 + phase, by - 1], r_small.at[3 + phase, by - 1], device(to))
                c.start()
                copies.append(c)

            def done():
                for c in copies:
                    c.wait()
                out = cur[pos[axis]] + got[0] + got[1] + got[2]
                if phase == 0:
                    return out
                (sa1, sa2)[phase - 1][...] = out
                return None

            return done

        term(10, tgot, tgot).wait_recv()
        gs[section] += tgot[...]
        done = small_start(2)
        for n, h in items[2]:
            j, kind = STREAMS[n]
            _, halves = neighbours(n, 2)
            load(n, h, 0, grad_part(n, halves[h][1], h), ob[kind].at[j, h]).start()
        for n, h in items[2]:
            j, kind = STREAMS[n]
            slot = neighbours(n, 2)[1][h][0]
            rs_copy(n, 2, slot, ab[kind].at[j, h], moved(pos, 0, 1)).wait_recv()
            load(n, h, 1, recv2[kind].at[j, slot], ab[kind].at[j, h]).start()
        for n, h in items[2]:
            j, kind = STREAMS[n]
            here, halves = neighbours(n, 2)
            _, block, to, slot, _ = halves[h]
            load(n, h, 0, grad_part(n, block, h), ob[kind].at[j, h]).wait()
            load(n, h, 1, recv2[kind].at[j, 0], ab[kind].at[j, h]).wait()
            add(ab[kind].at[j, h], [ab[kind].at[j, h], ob[kind].at[j, h]], (2, 4), BF)
            rs_copy(n, 2, slot, ab[kind].at[j, h], to).start()
            load(n, h, 0, grad_part(n, here, h), ob[kind].at[j, h]).start()
        done()
        for n, h in items[2]:
            j, kind = STREAMS[n]
            slot = neighbours(n, 2)[1][h][4]
            rs_copy(n, 2, slot, ab[kind].at[j, h], moved(pos, 0, 1)).wait_recv()
            load(n, h, 2, recv2[kind].at[j, slot], db[kind].at[j, h]).start()

        def last2(n, h):
            j, kind = STREAMS[n]
            order = ORDERS[j]
            low = min(order[:2])
            load(n, h, 0, grad_part(n, 0, h), ob[kind].at[j, h]).wait()
            load(n, h, 2, recv2[kind].at[j, 0], db[kind].at[j, h]).wait()
            load(n, h, 3, recv2[kind].at[j, 0], eb[kind].at[j, h]).wait()
            place = (lambda a, b: (j, 2 * h + a, b)) if order[1] == low else (lambda a, b: (j, b, 2 * h + a))
            add(acc2[kind], [ob[kind].at[j, h], db[kind].at[j, h], eb[kind].at[j, h]], (2, 4), BF, place)

        before = None
        for n, h in items[2]:
            j, kind = STREAMS[n]
            slot = neighbours(n, 2)[1][h][3]
            rs_copy(n, 2, slot, ab[kind].at[j, h], moved(pos, 0, 1)).wait_recv()
            load(n, h, 3, recv2[kind].at[j, slot], eb[kind].at[j, h]).start()
            if before is not None:
                last2(*before)
            before = (n, h)
        last2(*before)

        for phase in (1, 0):
            recv, buf = (recv0, recv1)[phase], (b0, b1)[phase]

            def part(n, k, h):
                j, kind = STREAMS[n]
                return acc2[kind].at[j, k, pl.ds(2 * h, 2)] if phase == 1 else acc1[kind].at[j, k]

            dims = (2,) if phase == 1 else ()

            def fetch(n, h, slot, which):
                j, kind = STREAMS[n]
                rs_copy(n, phase, slot, buf[kind].at[j, slot], moved(pos, 0, 1)).wait_recv()
                load(n, h, which, recv[kind].at[j, slot], buf[kind].at[j, slot]).start()

            def fetched(n, h, slot, which):
                j, kind = STREAMS[n]
                load(n, h, which, recv[kind].at[j, slot], buf[kind].at[j, slot]).wait()
                return buf[kind].at[j, slot]

            done = small_start(phase)
            for n in range(9):
                rs_start(n, phase, part)
            for n, h in items[phase]:
                fetch(n, h, neighbours(n, phase)[1][h][0], 1)
            for n, h in items[phase]:
                slot, block, to, summed, _ = neighbours(n, phase)[1][h]
                ref = fetched(n, h, slot, 1)
                add(ref, [ref, part(n, block, h)], dims, BF)
                rs_copy(n, phase, summed, ref, to).start()
            last_tile = done()
            for n, h in items[phase]:
                fetch(n, h, neighbours(n, phase)[1][h][4], 2)

            def last(n, h):
                j, kind = STREAMS[n]
                here, halves = neighbours(n, phase)
                parts = [part(n, here, h), fetched(n, h, halves[h][4], 2), fetched(n, h, halves[h][3], 3)]
                if phase == 1:
                    add(acc1[kind], parts, dims, BF, lambda a: (j, 2 * h + a))
                else:
                    add(fin[kind].at[j], parts, dims, F32)

            before = None
            for n, h in items[phase]:
                fetch(n, h, neighbours(n, phase)[1][h][3], 3)
                if before is not None:
                    last(*before)
                before = (n, h)
            last(*before)

        for j in range(3):
            fsend[j] = jnp.where(even, fin[0][j, 24:48, :], fin[0][j, 0:24, :])
        last_e = jnp.concatenate([fin[2][j] for j in range(3)], axis=0)
        gsend[...] = jnp.where(even, last_e[24:48], last_e[0:24])
        swap_f = misc(5, fsend, fgot, device(partner))
        swap_g = misc(6, gsend, ggot, device(partner))
        swap_f.start()
        swap_g.start()
        for j in range(3):
            for i, at in enumerate(group_columns(2 * j + parity)):
                lanes = slice(512 * i, 512 * i + 512)
                d_win[:, at] = jnp.where(even, fin[0][j, 0:24, lanes], fin[0][j, 24:48, lanes])
            d_wout[:, 512 * j : 512 * j + 512] = fin[1][j]
        d_taps[...] = last_tile[0:4, 0:52]
        d_bias[...] = last_tile[4:5, 0:52]
        d_pre[...] = last_tile[5:6, 0:24]
        d_gate[...] = last_tile[6:7, 0:48]
        d_dtb[...] = last_tile[7:8, 0:48]
        d_alog[...] = last_tile[5:6, 64:112]
        d_skip[...] = last_tile[6:7, 64:112]
        swap_f.wait()
        swap_g.wait()
        for j in range(3):
            for i, at in enumerate(group_columns(2 * j + 1 - parity)):
                d_win[:, at] = fgot[j, :, 512 * i : 512 * i + 512]
        mine, theirs = jnp.where(even, last_e[0:24], last_e[24:48]), ggot[...]
        d_win[:, 2 * DI : 2 * DI + 2 * N] = jnp.where(even, mine, theirs)
        d_win[:, 2 * DI + 2 * N :] = jnp.where(even, theirs, mine)[:, 0:H]
        for phase in range(3):
            sent(phase)

    shapes = []
    for lead, dtype in (((3, 2, 2, 4), BF),) * 4 + (((3, 4, 4), BF), ((3, 4), BF), ((3, 6, 2), BF), ((3, 6), BF), ((3,), F32)):
        shapes += [V(lead + dims, dtype) for dims in KINDS]
    shapes += [V((3, 24, 1024), F32), V((24, 256), F32), V((4, 4, 8, 128), F32), V((4, 8, 128), F32)]
    pl.run_scoped(sums, *shapes, pltpu.SemaphoreType.DMA((9, 2, 4)))

    end.wait()
    for n, (j, kind) in enumerate(STREAMS):
        ref = gath[kind].at[section, j]
        remote(ref, ref, s_sib.at[n], r_sib.at[n], sibling).wait_send()

    @pl.when(jnp.logical_not(leading))
    def _():
        ag_sent(2)

    for n, ref in enumerate((us_, os_, dvs)):
        term(n, ref.at[2], ref.at[1]).wait_send()
    for g in (4, 5):
        dterm(g).wait_send()
    term(9, dpes.at[2], dpes.at[1]).wait_send()
    term(10, tgot, tgot).wait_send()


def step(ends, segs, counts, win, taps, bias, pre, gate, wout, dtb, alog, skip):
    vm = pl.BlockSpec(memory_space=pltpu.VMEM)
    any_ = pl.BlockSpec(memory_space=pl.ANY)
    s = jax.ShapeDtypeStruct
    V, S = pltpu.VMEM, pltpu.SemaphoreType.DMA
    large = []
    for lead in ((2, 3, 4, 4, 4), (3, 4, 4, 4), (3, 6, 2, 4), (3, 6, 2), (3, 6)):
        large += [s(lead + dims, BF) for dims in KINDS]
    return pl.pallas_call(
        step_kernel,
        out_shape=[
            s((2, T, D), BF), s((24, 6448), F32), s((4, 52), F32), s((1, 52), F32), s((1, 24), F32), s((1, 48), F32), s((48, D), F32),
            s((1, H), F32), s((1, H), F32), s((1, H), F32),
        ] + large,
        in_specs=[vm, vm, pl.BlockSpec(memory_space=pltpu.SMEM)] + [vm] * 9,
        out_specs=[vm] * 10 + [any_] * 15,
        scratch_shapes=[
            V((3, 24, 1024), BF), V((24, 256), BF), V((3, 24, 1024), F32), V((24, 256), F32), V((2, 4, 4, 4, 8, 128), F32),
            V((2, 8, CC), F32), V((2, 8, 128), F32), V((2, 8, CC), F32), V((4, 4, 4, 8, 128), F32),
            V((3, 4, 4, 8, 128), F32), V((3, 4, 8, 128), F32), V((3, 8, 128), F32),
            V((T, D), BF), V((T, D), BF), V((3, T, D), BF), V((3, T, DI), BF), V((3, T, D), BF), V((14, T, 1024), BF), V((3, 2, T, 256), BF),
            S((7,)), S((7,)), S((9, 3)), S((9, 3, 8)), S((6, 3)), S((6, 3)), S((9,)), S((9,)), S((9, 3)), S((9, 3, 6)), S((11,)), S((11,)), S((9,)),
            pltpu.SemaphoreType.REGULAR,
        ],
        compiler_params=pltpu.CompilerParams(collective_id=0, has_side_effects=True, vmem_limit_bytes=63 * 1024 * 1024),
        name="train_step",
    )(ends, segs, counts, win, taps, bias, pre, gate, wout, dtb, alog, skip)[:10]


def body(ends_in, seg_ids, block_counts, in_weight, conv_weight, conv_bias, pre_gain, gate_gain, out_weight, dt_bias, a_log, skip):
    outs = step(
        ends_in[0].reshape(2, T, D), seg_ids, block_counts, in_weight[0], conv_weight[0], conv_bias, pre_gain, gate_gain, out_weight[0], dt_bias, a_log, skip
    )
    ends_out, d_in, d_taps, d_bias, d_pre, d_gate, d_out, d_dtb, d_alog, d_skip = outs
    return ends_out.reshape(1, 2 * T, D), d_in[None], d_taps[None], d_bias, d_pre, d_gate, d_out[None], d_dtb, d_alog, d_skip


def solution(mesh):
    placed = (
        P("section", "dp", None),
        P("dp", None),
        P("dp"),
        P("section", "dp", None),
        P("section", None, "dp"),
        P("section", "dp"),
        P("section", "dp"),
        P("section", "dp"),
        P("section", "dp", None),
        P("section", None),
        P("section", None),
        P("section", None),
    )
    return jax.shard_map(
        body,
        mesh=mesh,
        in_specs=placed,
        out_specs=(
            P("section", "dp", None),
            P("section", "dp", None),
            P("section", None, "dp"),
            P("section", "dp"),
            P("section", "dp"),
            P("section", "dp"),
            P("section", "dp", None),
            P("section", None),
            P("section", None),
            P("section", None),
        ),
        check_vma=False,
    )
```

```python
import jax
import jax.numpy as jnp
from jax import lax
from jax.experimental import pallas as pl
from jax.experimental.pallas import tpu as pltpu
from jax.sharding import PartitionSpec as P

D = 1536
DI = 3072
N = 128
H = 48
CC = 3328
T = 128
EPSILON = 1e-05
F32 = jnp.float32
BF = jnp.bfloat16
GROUPS = 6
LOG2E = 1.4426950408889634
MESH = pl.DeviceIdType.MESH
KINDS = ((48, 1024), (48, 512), (16, 256))
ORDERS = ((2, 1, 0), (1, 0, 2), (0, 2, 1))
STREAMS = tuple((j, kind) for j in range(3) for kind in range(3))


def moved(pos, axis, by):
    out = list(pos)
    out[axis] = lax.rem(pos[axis] + by, 4)
    return tuple(out)


def block_index(order, phase, pos, half, sub=None):
    index = [pos[0], pos[1], pos[2]]
    for a in order[:phase]:
        index[a] = slice(None)
    if phase > 0 and half is not None:
        index[min(order[:phase])] = pl.ds(2 * half, 2) if sub is None else 2 * half + sub
    return tuple(index)


def has_half(kind, phase, half):
    return phase != 0 or half == (0 if kind == 0 else 1)


def dot(a, b, dims=((1,), (0,))):
    return lax.dot_general(a, b, (dims, ((), ())), preferred_element_type=F32)


def sigmoid(v):
    return 1.0 / (1.0 + jnp.exp(-v))


def total(v):
    return jnp.sum(v, axis=0, keepdims=True)


def exact_dot(zeros_ones, wide, dims=((1,), (0,)), flip=False, terms=3):
    out = None
    for _ in range(terms):
        term = wide.astype(BF)
        wide = wide - term.astype(F32)
        part = dot(term, zeros_ones, dims) if flip else dot(zeros_ones, term, dims)
        out = part if out is None else out + part
    return out


def keep_lanes(v, keep):
    return jnp.where(keep, v, jnp.zeros_like(v))


def step_kernel(*refs):
    it = iter(refs)
    take = lambda n: [next(it) for _ in range(n)]
    ends, segs, counts, win, taps_in, bias_in, pre_in, gate_in, wout, dtb_in, alog_in, skip_in = take(12)
    ends_out, d_win, d_wout, d_small = take(4)
    gath, grad, recv2 = take(3), take(3), take(3)
    wgot, egot, gs, par, hp, gr, tgot, sg2, sg1, sg0, swapped, leaving, us_, os_, dvs, dps, dpes = take(17)
    (s_misc, r_misc, s_ag, r_ag, s_small, r_small, s_sib, r_sib, s_rs, r_rs, s_terms, r_terms, own_sem, go_sem, ready_sem) = take(15)

    section = lax.axis_index("section")
    dp = lax.axis_index("dp")
    pos = (lax.div(dp, 16), lax.rem(lax.div(dp, 4), 4), lax.rem(dp, 4))
    parity = lax.rem(pos[2], 2)
    even = parity == 0
    partner = (pos[0], pos[1], pos[2] + 1 - 2 * parity)
    leading = section == 0

    def device(at, s=None):
        return {"section": section if s is None else s, "dp": at[0] * 16 + at[1] * 4 + at[2]}

    sibling = device(pos, 1 - section)

    def remote(src, dst, s, r, to):
        return pltpu.make_async_remote_copy(src, dst, s, r, device_id=to, device_id_type=MESH)

    def misc(n, src, dst, to):
        return remote(src, dst, s_misc.at[n], r_misc.at[n], to)

    barrier = pltpu.get_barrier_semaphore()
    for axis in range(3):
        for by in (1, 2, 3):
            pl.semaphore_signal(barrier, inc=1, device_id=device(moved(pos, axis, by)), device_id_type=MESH)
    pl.semaphore_signal(barrier, inc=1, device_id=sibling, device_id_type=MESH)

    def group_columns(g):
        return [pl.ds(pl.multiple_of(512 * g + first, 128), 512) for first in (0, DI)]

    def ag_copy(n, phase, slot, src, index, to):
        j, kind = STREAMS[n]
        return remote(src, gath[kind].at[section, j].at[index], s_ag.at[n, phase], r_ag.at[n, phase, slot], device(to))

    def ag_start(n, phase, unit=None):
        j, kind = STREAMS[n]
        order = ORDERS[j]
        right, left = moved(pos, order[phase], 1), moved(pos, order[phase], 3)
        for slot, (h, to) in enumerate(((0, right), (1, left), (1, right), (0, left))):
            if has_half(kind, phase, h):
                index = block_index(order, phase, pos, h)
                src = unit[kind].at[j] if phase == 0 else gath[kind].at[section, j].at[index]
                ag_copy(n, phase, slot, src, index, to).start()

    def ag_pieces(n, phase, at, h):
        order = ORDERS[STREAMS[n][0]]
        if phase < 2:
            return [block_index(order, phase, at, h)]
        return [block_index(order, phase, at, h, q) for q in range(2)]

    def to_sibling(n, index):
        j, kind = STREAMS[n]
        ref = gath[kind].at[section, j].at[index]
        remote(ref, ref, s_sib.at[n], r_sib.at[n], sibling).start()

    def ag_arrived(n, phase, slot, index):
        j, kind = STREAMS[n]
        ag_copy(n, phase, slot, gath[kind].at[section, j].at[index], index, moved(pos, 0, 1)).wait_recv()
        if phase == 2:
            to_sibling(n, index)

    def ag_forward(phase):
        for n, (j, kind) in enumerate(STREAMS):
            order = ORDERS[j]
            right, left = moved(pos, order[phase], 1), moved(pos, order[phase], 3)
            for slot, h, source, to in ((0, 0, left, right), (1, 1, right, left)):
                if has_half(kind, phase, h):
                    ag_arrived(n, phase, slot, block_index(order, phase, source, h))
                    for q, index in enumerate(ag_pieces(n, phase, source, h)):
                        ag_copy(n, phase, 4 + 2 * slot + q, gath[kind].at[section, j].at[index], index, to).start()

    def ag_rest(phase):
        for n, (j, kind) in enumerate(STREAMS):
            order = ORDERS[j]
            right, left = moved(pos, order[phase], 1), moved(pos, order[phase], 3)
            for slot, h, source in ((2, 1, left), (3, 0, right)):
                if has_half(kind, phase, h):
                    ag_arrived(n, phase, slot, block_index(order, phase, source, h))
        for q in range(2 if phase == 2 else 1):
            for n, (j, kind) in enumerate(STREAMS):
                far = moved(pos, ORDERS[j][phase], 2)
                for slot in (0, 1):
                    if has_half(kind, phase, slot):
                        ag_arrived(n, phase, 4 + 2 * slot + q, ag_pieces(n, phase, far, slot)[q])

    def ag_sent(phase):
        for n, (j, kind) in enumerate(STREAMS):
            index = {0: (0, 0, pl.ds(0, 3)), 1: (0, pl.ds(0, 3)), 2: (pl.ds(0, 3),)}[phase]
            ref = gath[kind].at[section, j].at[index]
            remote(ref, ref, s_ag.at[n, phase], r_ag.at[n, phase, 0], sibling).wait_send()

    def small_gather(phase):
        axis = (2, 1, 0)[phase]
        index = tuple(pos[: 3 - phase])
        sent = []
        for by in (1, 2, 3):
            ref = gs.at[section].at[index]
            c = remote(ref, ref, s_small.at[phase, by - 1], r_small.at[phase, by - 1], device(moved(pos, axis, by)))
            c.start()
            sent.append(c)
        return sent

    swap_ends = misc(2, ends.at[1 - section], swapped, sibling)
    small_across = misc(3, gs.at[section], gs.at[section], sibling)

    def prologue(wsend, esend, uw, uo, ue, us):
        unit = (uw, uo, ue)
        bc = win[:, 2 * DI : 2 * DI + 2 * N].astype(F32)
        rz = jnp.concatenate([win[:, 2 * DI + 2 * N :].astype(F32), jnp.zeros((24, 2 * N - H), F32)], axis=1)
        for j in range(3):
            for i, at in enumerate(group_columns(2 * j + 1 - parity)):
                wsend[j, :, 512 * i : 512 * i + 512] = win[:, at]
        esend[...] = jnp.where(even, rz, bc).astype(BF)
        us[...] = jnp.zeros((8, 128), F32)
        us[0:4, 0:52] = taps_in[...].astype(F32)
        us[4:5, 0:52] = bias_in[...].astype(F32)
        us[5:6, 0:24] = pre_in[...].astype(F32)
        us[6:7, 0:48] = gate_in[...].astype(F32)
        us[7:8, 0:48] = dtb_in[...].astype(F32)
        us[5:6, 64:112] = alog_in[...].astype(F32)
        us[6:7, 64:112] = skip_in[...].astype(F32)
        gs[section, pos[0], pos[1], pos[2]] = us[...]
        for j in range(3):
            uo[j] = wout[:, 512 * j : 512 * j + 512]

        pl.semaphore_wait(barrier, 10)
        swap_w = misc(0, wsend, wgot, device(partner))
        swap_e = misc(1, esend, egot, device(partner))
        for c in (swap_w, swap_e, swap_ends):
            c.start()

        small = small_gather(0)
        swap_w.wait()
        swap_e.wait()
        for j in range(3):
            for i, at in enumerate(group_columns(2 * j + parity)):
                lanes = slice(512 * i, 512 * i + 512)
                mine, theirs = win[:, at].astype(F32), wgot[j, :, lanes].astype(F32)
                uw[j, :, lanes] = jnp.concatenate([jnp.where(even, mine, theirs), jnp.where(even, theirs, mine)], axis=0).astype(BF)
        mine, theirs = jnp.where(even, bc, rz), egot[...].astype(F32)
        both = jnp.concatenate([jnp.where(even, mine, theirs), jnp.where(even, theirs, mine)], axis=0).astype(BF)
        for j in range(3):
            ue[j] = both[16 * j : 16 * j + 16, :]
        own = []
        for n, (j, kind) in enumerate(STREAMS):
            ag_start(n, 0, unit)
            c = pltpu.make_async_copy(unit[kind].at[j], gath[kind].at[section, j].at[pos], own_sem.at[n])
            c.start()
            own.append(c)
        for c in small:
            c.wait()
        small = small_gather(1)
        ag_forward(0)
        for c in small:
            c.wait()
        small = small_gather(2)
        for c in own:
            c.wait()
        ag_rest(0)
        for c in small:
            c.wait()
        small_across.start()
        ag_sent(0)

    pl.run_scoped(
        prologue,
        pltpu.VMEM((3, 24, 1024), BF), pltpu.VMEM((24, 256), BF), pltpu.VMEM((3, 48, 1024), BF), pltpu.VMEM((3, 48, 512), BF), pltpu.VMEM((3, 16, 256), BF), pltpu.VMEM((8, 128), F32),
    )

    def own_across():
        for n, (j, kind) in enumerate(STREAMS):
            to_sibling(n, block_index(ORDERS[j], 2, pos, None))

    def go(n):
        pl.semaphore_signal(go_sem.at[n], inc=1, device_id=sibling, device_id_type=MESH)

    @pl.when(leading)
    def _():
        for n in range(9):
            ag_start(n, 1)

    misc(3, gs.at[1 - section], gs.at[1 - section], sibling).wait()
    for l in range(2):
        hp[l] = gs[l, 0, 0, 0]
        for i in range(64):
            tile = gs.at[l, i // 16, i // 4 % 4, i % 4]
            par[l, 0:5, 52 * i : 52 * i + 52] = tile[0:5, 0:52]
            par[l, 7:8, 24 * i : 24 * i + 24] = tile[5:6, 0:24]
            par[l, 5:6, 48 * i : 48 * i + 48] = tile[6:7, 0:48]
    swap_ends.wait()

    def from_sibling(l):
        for n, (j, kind) in enumerate(STREAMS):
            ref = gath[kind].at[l, j]
            remote(ref, ref, s_sib.at[n], r_sib.at[n], sibling).wait_recv()

    @pl.when(leading)
    def _():
        ag_forward(1)
        go(0)
        ag_rest(1)
        for n in range(9):
            ag_start(n, 2)
        own_across()
        ag_forward(2)
        go(1)
        ag_rest(2)

    @pl.when(jnp.logical_not(leading))
    def _():
        pl.semaphore_wait(go_sem.at[0], 1)
        for n in range(9):
            ag_start(n, 1)
        ag_forward(1)
        ag_rest(1)
        own_across()
        pl.semaphore_wait(go_sem.at[1], 1)
        for n in range(9):
            ag_start(n, 2)
        from_sibling(0)

    landing = {}

    def rs_copy(n, phase, slot, src, to):
        j, kind = STREAMS[n]
        if phase == 2 and slot >= 4:
            dst = landing[2, kind].at[j, slot - 4]
        elif phase == 2:
            dst = recv2[kind].at[j, slot]
        else:
            dst = landing[phase, kind].at[j, slot if phase == 1 else slot // 2]
        return remote(src, dst, s_rs.at[n, phase], r_rs.at[n, phase, slot], device(to))

    def rs_start(n, phase, part):
        j, kind = STREAMS[n]
        axis = ORDERS[j][phase]
        right, left, far = (moved(pos, axis, by) for by in (1, 3, 2))
        for slot, at, h, to in ((0, far, 0, left), (1, far, 1, right), (2, left, 1, left), (3, right, 0, right)):
            if has_half(kind, phase, h):
                rs_copy(n, phase, slot, part(n, at[axis], h), to).start()

    def grad_part(n, k, h):
        j, kind = STREAMS[n]
        at = list(pos)
        at[ORDERS[j][2]] = k
        return grad[kind].at[(j,) + block_index(ORDERS[j], 2, tuple(at), h)]

    def term(n, src, dst):
        return remote(src, dst, s_terms.at[n], r_terms.at[n], sibling)

    def dterm(g):
        return term(3 + g, dps.at[12 + lax.rem(g, 2)], dps.at[6 + g])

    def layers(wbuf, ebuf, obuf, zbuf, xbuf, ybuf, tbuf, hbuf, pebuf, masks, allowed, tri, sel, qcol, qrow, dtrow, heads, smat, gbuf, dgacc, rowq, rowx, acc, rbuf, ut, ot, wsem, esem, osem, gsem):
        def copy_w(l, g):
            j, p = lax.div(g, 2), lax.rem(g, 2)
            return [pltpu.make_async_copy(gath[0].at[l, j, :, :, 2 * m + p], wbuf.at[g, :, :, pl.ds(48 * m, 48)], wsem.at[g, m]) for m in range(2)]

        def copy_e(l):
            return [pltpu.make_async_copy(gath[2].at[l, j, :, :, 2 * m + p], ebuf.at[p, :, :, m, j], esem.at[p, m, j]) for p in range(2) for m in range(2) for j in range(3)]

        def copy_o(l, j):
            return [pltpu.make_async_copy(gath[1].at[l, j], obuf.at[j], osem.at[j])]

        def start(copies):
            for c in copies:
                c.start()

        def finish(copies):
            for c in copies:
                c.wait()

        def weights_e(p):
            return ebuf[p].reshape(D, 256)

        def start_all(l):
            start(copy_e(l))
            for g in range(GROUPS):
                start(copy_w(l, jnp.int32(g)))
            for j in range(3):
                start(copy_o(l, j))

        start_all(0)

        rows = lax.broadcasted_iota(jnp.int32, (T, T), 0)
        cols = lax.broadcasted_iota(jnp.int32, (T, T), 1)
        seg = jnp.where(leading, segs[0:1, :], segs[1:2, :]).astype(F32)
        seg_s = jnp.broadcast_to(seg, (T, T))
        seg_t = jnp.transpose(seg_s)
        allowed[...] = jnp.where(rows >= cols, jnp.where(seg_t == seg_s, 1.0, 0.0), 0.0)
        for d in (1, 2, 3):
            masks[d - 1] = jnp.where(rows >= d, jnp.where(pltpu.roll(seg_t, d, 0) == seg_t, 1.0, 0.0), 0.0)
        masks[3] = jnp.where(rows < counts[section], 1.0, 0.0)
        tri[...] = jnp.where(rows >= cols, 1.0, 0.0).astype(BF)
        srow = lax.broadcasted_iota(jnp.int32, (512, T), 0)
        scol = lax.broadcasted_iota(jnp.int32, (512, T), 1)
        sel[...] = jnp.where(lax.div(srow, 64) == scol, 1.0, 0.0).astype(BF)
        low_lanes = cols < 64
        for l in range(2):
            skips = hp[l, 6:7, 64:112]
            skips = jnp.concatenate([skips, jnp.zeros((1, 80), F32)], axis=1)
            skips = jnp.broadcast_to(skips, (8, T))
            for g in range(GROUPS):
                mine = skips if g == 0 else pltpu.roll(skips, T - 8 * g, 1)
                mine = jnp.where(cols[0:8] < 8, mine, 0.0)
                par[l, 6:7, 512 * g : 512 * g + 512] = dot(mine.astype(BF), sel[...], ((1,), (1,)))[0:1]

        def conv(px, taps, bias):
            s1 = pltpu.roll(px, 1, 0) * masks[0]
            s2 = pltpu.roll(px, 2, 0) * masks[1]
            s3 = pltpu.roll(px, 3, 0) * masks[2]
            c = bias + taps[3:4] * px + taps[2:3] * s1 + taps[1:2] * s2 + taps[0:1] * s3
            return c, (s3, s2, s1, px)

        def conv_back(dc, taps):
            out = taps[3:4] * dc
            out = out + taps[2:3] * pltpu.roll(dc * masks[0], T - 1, 0)
            out = out + taps[1:2] * pltpu.roll(dc * masks[1], T - 2, 0)
            return out + taps[0:1] * pltpu.roll(dc * masks[2], T - 3, 0)

        def decay(g, hh):
            gap = jnp.broadcast_to(qcol[g][:, hh : hh + 1], (T, T)) - qrow[g][hh : hh + 1, :]
            return jnp.exp2(jnp.minimum(gap, 0.0)) * dtrow[g][hh : hh + 1, :]

        def rate_bias(l):
            return hp[l, 7:8, :]

        def rate(l):
            tile = pltpu.roll(hp[l], 64, 1)
            return -jnp.exp(jnp.where(cols[0:1] < H, tile[5:6, :], 0.0))

        def tile_at(g, k):
            return pl.ds(pl.multiple_of(512 * g + 128 * k, 128), 128)

        def prepare(l):
            q = heads[l, 1]
            qt = jnp.transpose(q)
            dtt = jnp.transpose(heads[l, 0])
            for g in range(GROUPS):
                qcol[g] = q if g == 0 else pltpu.roll(q, T - 8 * g, 1)
                qrow[g] = qt[8 * g : 8 * g + 8, :]
                dtrow[g] = dtt[8 * g : 8 * g + 8, :]

        def slot(l):
            return lax.select(section == l, 0, 2)

        def first_input():
            return jnp.where(leading, ends[section].astype(F32), swapped[...].astype(F32))

        def forward(l, h):
            if l == 1:
                hbuf[...] = h.astype(BF)
            rs = lax.rsqrt(jnp.sum(h * h, axis=1, keepdims=True) * (1.0 / D) + EPSILON)
            rbuf[l, 0] = jnp.broadcast_to(rs, (T, T))
            us_[slot(l)] = (h * rs * par[l, 7:8, 0:D] * masks[3][:, 0:1]).astype(BF)
            finish(copy_e(l))
            pebuf[l, :, 0:256] = dot(us_[slot(l)], weights_e(0))
            pebuf[l, :, 256:384] = dot(us_[slot(l)], weights_e(1))[:, 0:128]
            for j in range(2):
                at = slice(DI + 128 * j, DI + 128 * j + 128)
                c, _ = conv(pebuf[l, :, 128 * j : 128 * j + 128], par[l, 0:4, at], par[l, 4:5, at])
                smat[l, j] = (c * sigmoid(c)).astype(BF)
            v = pebuf[l, :, 256:384] + rate_bias(l)
            dt = jnp.maximum(v, 0.0) + jnp.log1p(jnp.exp(-jnp.abs(v)))
            heads[l, 0] = dt
            heads[l, 1] = exact_dot(tri[...], dt * rate(l)) * LOG2E
            gbuf[l] = dot(smat[l, 1], smat[l, 0], ((1,), (1,))) * allowed[...]
            prepare(l)
            acc[:, 0:128] = jnp.zeros((T, T), F32)

            def group(g, carry):
                finish(copy_w(l, g))
                p = dot(us_[slot(l)], wbuf[g].reshape(D, 1024))
                wide = pl.ds(pl.multiple_of(512 * g, 128), 512)
                zbuf[l, :, wide] = p[:, 0:512]
                xbuf[l, :, wide] = p[:, 512:1024]
                for k in range(4):
                    at = tile_at(g, k)
                    c, _ = conv(xbuf[l, :, at], par[l, 0:4, at], par[l, 4:5, at])
                    x = c * sigmoid(c)
                    xb = x.astype(BF)
                    both = jnp.concatenate([keep_lanes(xb, low_lanes), keep_lanes(xb, ~low_lanes)], axis=0)
                    w = jnp.concatenate([(gbuf[l] * decay(g, 2 * k + i)).astype(BF) for i in range(2)], axis=1)
                    y = dot(w, both) + par[l, 6:7, at] * x
                    ybuf[l, :, at] = y
                    z = zbuf[l, :, at]
                    e = y * (z * sigmoid(z))
                    tbuf[:, at] = e
                    acc[:, 0:128] += e * e
                return carry

            lax.fori_loop(0, GROUPS, group, 0)
            r = lax.rsqrt(jnp.sum(acc[:, 0:128], axis=1, keepdims=True) * (1.0 / DI) + EPSILON)
            rbuf[l, 1] = jnp.broadcast_to(r, (T, T))
            for g in range(GROUPS):
                at = slice(512 * g, 512 * g + 512)
                os_[slot(l), :, at] = (tbuf[:, at] * r * par[l, 5:6, at]).astype(BF)
            for j in range(3):
                finish(copy_o(l, j))
                acc[:, 512 * j : 512 * j + 512] = dot(os_[slot(l)], obuf[j].reshape(DI, 512))
            return h + acc[...]

        def backward(l, dh):
            dvs[slot(l)] = dh.astype(BF)

            @pl.when(section != l)
            def _():
                for n, ref in enumerate((us_, os_, dvs)):
                    term(n, ref.at[2], ref.at[1]).start()

            if l == 0:
                for j in range(3):
                    finish(copy_o(0, j))
            acc[:, 0:128] = jnp.zeros((T, T), F32)

            def first(zz, carry):
                wide = pl.ds(pl.multiple_of(768 * zz, 128), 768)
                do = None
                for j in range(3):
                    part = dot(dvs[slot(l), :, 512 * j : 512 * j + 512], obuf[j, zz].reshape(768, 512), ((1,), (1,)))
                    do = part if do is None else do + part
                tbuf[:, wide] = do
                for k in range(6):
                    at = pl.ds(pl.multiple_of(768 * zz + 128 * k, 128), 128)
                    z = zbuf[l, :, at]
                    e = ybuf[l, :, at] * (z * sigmoid(z))
                    prod = tbuf[:, at] * e
                    gr[l, 5:6, at] = total(prod * rbuf[l, 1])
                    acc[:, 0:128] += prod * par[l, 5:6, at]
                return carry

            lax.fori_loop(0, 4, first, 0)
            if l == 1:
                @pl.when(leading)
                def _():
                    for j in range(3):
                        start(copy_o(0, j))
            r = rbuf[l, 1]
            masks[4] = jnp.broadcast_to(jnp.sum(acc[:, 0:128], axis=1, keepdims=True) * (1.0 / DI), (T, T)) * r * r * r
            prepare(l)
            dgacc[...] = jnp.zeros((T, T), F32)
            rowq[...] = jnp.zeros((T, T), F32)
            rowx[...] = jnp.zeros((T, T), F32)
            acc[...] = jnp.zeros((T, D), F32)

            def second(g, carry):
                if l == 0:
                    finish(copy_w(0, g))

                here = lax.select(section == l, g, 12 + lax.rem(g, 2))

                @pl.when(jnp.logical_and(section != l, g >= 2))
                def _():
                    dterm(g - 2).wait_send()

                sums_q, sums_x = None, None
                for k in range(4):
                    at = tile_at(g, k)
                    z = zbuf[l, :, at]
                    y = ybuf[l, :, at]
                    sz = sigmoid(z)
                    silu = z * sz
                    de = rbuf[l, 1] * (tbuf[:, at] * par[l, 5:6, at]) - (y * silu) * masks[4]
                    dyb = (de * silu).astype(BF)
                    dz = de * y * (sz + silu * (1.0 - sz))
                    dps[here, :, 128 * k : 128 * k + 128] = dz.astype(BF)
                    taps = par[l, 0:4, at]
                    c, shifts = conv(xbuf[l, :, at], taps, par[l, 4:5, at])
                    sc = sigmoid(c)
                    x = c * sc
                    xb = x.astype(BF)
                    dyw = dyb.astype(F32)
                    skip = par[l, 6:7, at]
                    xt = jnp.concatenate([keep_lanes(xb, low_lanes), keep_lanes(xb, ~low_lanes)], axis=0)
                    dyt = jnp.concatenate([keep_lanes(dyb, low_lanes), keep_lanes(dyb, ~low_lanes)], axis=0)
                    dw = dot(dyb, xt, ((1,), (1,)))
                    ws, dg = [], None
                    for i in range(2):
                        e = decay(g, 2 * k + i)
                        ws.append((gbuf[l] * e).astype(BF))
                        part = dw[:, 128 * i : 128 * i + 128] * e
                        dg = part if dg is None else dg + part
                    dgacc[...] += dg
                    dx0 = dot(jnp.concatenate(ws, axis=0), dyt, ((0,), (0,)))
                    dx = dx0 + skip * dyw
                    gr[l, 6:7, at] = total(dyw * x)
                    one = sel[128 * k : 128 * k + 128, :]
                    part = exact_dot(one, dyw * (y - skip * x), flip=True, terms=2)
                    sums_q = part if sums_q is None else sums_q + part
                    part = exact_dot(one, xb.astype(F32) * dx0, flip=True, terms=2)
                    sums_x = part if sums_x is None else sums_x + part
                    dc = dx * (sc + x * (1.0 - sc))
                    for t in range(4):
                        gr[l, t : t + 1, at] = total(dc * shifts[t])
                    gr[l, 4:5, at] = total(dc)
                    dps[here, :, 512 + 128 * k : 640 + 128 * k] = conv_back(dc, taps).astype(BF)
                rowq[...] += pltpu.roll(sums_q, 8 * g, 1)
                rowx[...] += pltpu.roll(sums_x, 8 * g, 1)

                @pl.when(section != l)
                def _():
                    dterm(g).start()

                acc[...] += dot(dps[here], wbuf[g].reshape(D, 1024), ((1,), (1,)))
                if l == 1:
                    @pl.when(leading)
                    def _():
                        start(copy_w(0, g))
                return carry

            lax.fori_loop(0, GROUPS, second, 0)
            dg = (dgacc[...] * allowed[...]).astype(BF)
            d_states = (dot(dg, smat[l, 1], ((0,), (0,))), dot(dg, smat[l, 0]))
            for j in range(2):
                at = slice(DI + 128 * j, DI + 128 * j + 128)
                taps = par[l, 0:4, at]
                c, shifts = conv(pebuf[l, :, 128 * j : 128 * j + 128], taps, par[l, 4:5, at])
                sc = sigmoid(c)
                dc = d_states[j] * (sc + c * sc * (1.0 - sc))
                for t in range(4):
                    gr[l, t : t + 1, at] = total(dc * shifts[t])
                gr[l, 4:5, at] = total(dc)
                dpes[slot(l), 0, :, 128 * j : 128 * j + 128] = conv_back(dc, taps).astype(BF)
            v = pebuf[l, :, 256:384] + rate_bias(l)
            sv = sigmoid(v)
            dt = heads[l, 0]
            back = exact_dot(tri[...], rowq[...] - rowx[...], ((0,), (0,)))
            ratio = jnp.where(v < -15.0, 1.0, sv / jnp.maximum(dt, 1e-30))
            dr = jnp.where(cols < H, rowx[...] * ratio + back * rate(l) * sv, 0.0)
            d_rate = total(jnp.where(cols < H, back * dt, 0.0)) * rate(l)
            dpes[slot(l), 1, :, 0:128] = dr.astype(BF)
            dpes[slot(l), 1, :, 128:256] = jnp.zeros((T, T), BF)

            @pl.when(section != l)
            def _():
                term(9, dpes.at[2], dpes.at[1]).start()

            if l == 0:
                finish(copy_e(0))
            du = acc[...]
            for p in range(2):
                du = du + dot(dpes[slot(l), p], weights_e(p), ((1,), (1,)))
            if l == 1:
                @pl.when(leading)
                def _():
                    start(copy_e(0))

            h = hbuf[...].astype(F32) if l == 1 else first_input()
            hn = h * rbuf[l, 0][:, 0:1]
            du = du * masks[3][:, 0:1]
            gr[l, 7:8, 0:D] = total(du * hn)
            t = du * par[l, 7:8, 0:D]
            s = jnp.sum(t * hn, axis=1, keepdims=True) * (1.0 / D)
            dh_in = dh + rbuf[l, 0][:, 0:1] * (t - hn * s)
            skips = jnp.zeros((8, T), F32)
            for g in range(GROUPS):
                mine = exact_dot(sel[...], jnp.broadcast_to(gr[l, 6:7, 512 * g : 512 * g + 512], (8, 512)), flip=True)
                skips = skips + (mine if g == 0 else pltpu.roll(mine, 8 * g, 1))
            for i in range(64):
                tile = gs.at[l, i // 16, i // 4 % 4, i % 4]
                tile[0:5, 0:52] = gr[l, 0:5, 52 * i : 52 * i + 52]
                tile[5:6, 0:24] = gr[l, 7:8, 24 * i : 24 * i + 24]
                tile[6:7, 0:48] = gr[l, 5:6, 48 * i : 48 * i + 48]
                tile[7:8, 0:128] = total(dr)
                tile[5:6, 64:112] = d_rate[:, 0:48]
                tile[6:7, 64:112] = skips[0:1, 0:48]

            @pl.when(section != l)
            def _():
                term(10, gs.at[l], tgot).start()

            return dh_in

        def products(l):
            for n, ref in enumerate((us_, os_, dvs)):
                term(n, ref.at[2], ref.at[1]).wait_recv()
            for g in range(GROUPS):
                dterm(g).wait_recv()
            term(9, dpes.at[2], dpes.at[1]).wait_recv()

            def stacked(ref, *index):
                return jnp.concatenate([ref[(0,) + index], ref[(1,) + index]], axis=0)

            for ref, turned, count in ((us_, ut, D // 128), (os_, ot, DI // 128)):
                def turn(i, carry):
                    at = pl.ds(pl.multiple_of(128 * i, 128), 128)
                    turned[at, :] = jnp.transpose(stacked(ref, slice(None), at))
                    return carry

                lax.fori_loop(0, count, turn, 0)

            for p in range(2):
                for zz in range(4):
                    de = dot(ut[384 * zz : 384 * zz + 384, :], stacked(dpes, p))
                    ebuf[p, zz] = de.astype(BF).reshape(4, 2, 3, 16, 256)
            for p in range(2):
                for m in range(2):
                    for j in range(3):
                        pltpu.make_async_copy(ebuf.at[p, :, :, m, j], grad[2].at[j, :, :, 2 * m + p], gsem.at[j, 2]).start()

            def wstep(i, carry):
                g, zz = lax.div(i, 4), lax.rem(i, 4)
                u = ut[pl.ds(pl.multiple_of(384 * zz, 128), 384), :]
                for half in range(2):
                    at = slice(512 * half, 512 * half + 512)
                    d = jnp.concatenate([dps[g, :, at], dps[6 + g, :, at]], axis=0)
                    wbuf[g, zz, :, :, at] = dot(u, d).astype(BF).reshape(4, 96, 512)
                j, p = lax.div(g, 2), lax.rem(g, 2)
                for m in range(2):
                    pltpu.make_async_copy(wbuf.at[g, zz, :, pl.ds(48 * m, 48)], grad[0].at[j, zz, :, 2 * m + p], gsem.at[j, 0]).start()
                return carry

            def ostep(i, carry):
                j, zz = lax.div(i, 4), lax.rem(i, 4)
                d = stacked(dvs, slice(None), pl.ds(pl.multiple_of(512 * j, 128), 512))
                for half in range(2):
                    o = ot[pl.ds(pl.multiple_of(768 * zz + 384 * half, 128), 384), :]
                    obuf[j, zz, 2 * half : 2 * half + 2] = dot(o, d).astype(BF).reshape(2, 4, 48, 512)
                pltpu.make_async_copy(obuf.at[j, zz], grad[1].at[j, zz], gsem.at[j, 1]).start()
                return carry

            def written(j, kind):
                pltpu.make_async_copy(grad[kind].at[j], grad[kind].at[j], gsem.at[j, kind]).wait()
                rs_start(3 * j + kind, 2, grad_part)

            for j in range(3):
                lax.fori_loop(8 * j, 8 * j + 8, wstep, 0)
                if j > 0:
                    written(j - 1, 1)
                lax.fori_loop(4 * j, 4 * j + 4, ostep, 0)
                written(j, 0)
            written(2, 1)
            for j in range(3):
                written(j, 2)

        middle = forward(0, first_input()).astype(BF).astype(F32)

        @pl.when(jnp.logical_not(leading))
        def _():
            ag_forward(2)
            ag_rest(2)

        @pl.when(leading)
        def _():
            from_sibling(1)

        start_all(1)
        out = forward(1, middle).astype(BF)

        @pl.when(leading)
        def _():
            leaving[...] = out

        @pl.when(jnp.logical_not(leading))
        def _():
            ends_out[section] = out

        cotangent = jnp.where(leading, swapped[...].astype(F32), ends[section].astype(F32))
        d_middle = backward(1, cotangent).astype(BF).astype(F32)

        @pl.when(jnp.logical_not(leading))
        def _():
            products(1)
            for j in range(3):
                start(copy_o(0, j))
            for g in range(GROUPS):
                start(copy_w(0, jnp.int32(g)))
            start(copy_e(0))

        d_first = backward(0, d_middle).astype(BF)

        @pl.when(leading)
        def _():
            ends_out[section] = d_first
            products(0)

        @pl.when(jnp.logical_not(leading))
        def _():
            leaving[...] = d_first

    V = pltpu.VMEM
    pl.run_scoped(
        layers,
        V((6, 4, 4, 96, 1024), BF), V((2, 4, 4, 2, 3, 16, 256), BF), V((3, 4, 4, 4, 48, 512), BF),
        V((2, T, DI), F32), V((2, T, DI), F32), V((2, T, DI), F32), V((T, DI), F32), V((T, D), BF), V((2, T, 384), F32),
        V((5, T, T), F32), V((T, T), F32), V((T, T), BF), V((512, T), BF), V((6, T, T), F32), V((6, 8, T), F32), V((6, 8, T), F32),
        V((2, 2, T, T), F32), V((2, 2, T, T), BF), V((2, T, T), F32), V((T, T), F32), V((T, T), F32), V((T, T), F32), V((T, D), F32), V((2, 2, T, T), F32),
        V((D, 256), BF), V((DI, 256), BF),
        pltpu.SemaphoreType.DMA((6, 2)), pltpu.SemaphoreType.DMA((2, 2, 3)), pltpu.SemaphoreType.DMA((3,)), pltpu.SemaphoreType.DMA((3, 3)),
    )

    end = misc(4, leaving, ends_out.at[section], sibling)
    end.start()

    def sums(*bufs):
        it = iter(bufs)
        take = lambda n: [next(it) for _ in range(n)]
        ab, ob, db, eb, acc2, acc1, b1, b0, fin = (take(3) for _ in range(9))
        fsend, gsend, fgot, ggot, sa2, sa1, lsem = it
        for kind in range(3):
            landing[2, kind], landing[1, kind], landing[0, kind] = eb[kind], b1[kind], b0[kind]
        for axis in range(3):
            for by in (1, 3):
                pl.semaphore_signal(ready_sem, inc=1, device_id=device(moved(pos, axis, by)), device_id_type=MESH)

        def load(n, h, which, src, dst):
            return pltpu.make_async_copy(src, dst, lsem.at[n, h, which])

        def add(dst, parts, dims, dtype, place=None):
            if not dims:
                out = parts[0][...].astype(F32)
                for p in parts[1:]:
                    out = out + p[...].astype(F32)
                dst[...] = out.astype(dtype)
                return
            count = dims[0] * (dims[1] if len(dims) > 1 else 1)

            def one(i, carry):
                index = (i,) if len(dims) == 1 else (lax.div(i, dims[1]), lax.rem(i, dims[1]))
                out = parts[0][index].astype(F32)
                for p in parts[1:]:
                    out = out + p[index].astype(F32)
                dst[index if place is None else place(*index)] = out.astype(dtype)
                return carry

            lax.fori_loop(0, count, one, 0)

        def neighbours(n, phase):
            axis = ORDERS[STREAMS[n][0]][phase]
            right, left = moved(pos, axis, 1), moved(pos, axis, 3)
            return pos[axis], {0: (0, left[axis], left, 4, 3), 1: (1, right[axis], right, 5, 2)}

        def sent(phase):
            for n, (j, kind) in enumerate(STREAMS):
                if phase == 2:
                    ref = grad[kind].at[j, pl.ds(0, 3)]
                else:
                    ref = landing[phase, kind].at[j, pl.ds(0, 3 if phase == 0 else 6)]
                remote(ref, ref, s_rs.at[n, phase], r_rs.at[n, phase, 0], sibling).wait_send()

        items = {phase: [(3 * j + kind, h) for kind in range(3) for j in range(3) for h in (0, 1) if has_half(kind, phase, h)] for phase in range(3)}
        by_kind = [3 * j + kind for kind in range(3) for j in range(3)]

        def small_start(phase):
            axis = ORDERS[0][phase]
            cur = (sa1, sa2, gs.at[section])[phase]
            got = (sg0, sg1, sg2)[phase]
            copies = []
            for by in (1, 2, 3):
                to = moved(pos, axis, by)
                c = remote(cur.at[to[axis]], got.at[by - 1], s_small.at[3 + phase, by - 1], r_small.at[3 + phase, by - 1], device(to))
                c.start()
                copies.append(c)

            def done():
                for c in copies:
                    c.wait()
                out = cur[pos[axis]] + got[0] + got[1] + got[2]
                if phase == 0:
                    return out
                (sa1, sa2)[phase - 1][...] = out
                return None

            return done

        term(10, tgot, tgot).wait_recv()
        gs[section] += tgot[...]
        for n, h in items[2]:
            j, kind = STREAMS[n]
            _, halves = neighbours(n, 2)
            load(n, h, 0, grad_part(n, halves[h][1], h), ob[kind].at[j, h]).start()
        for n, h in items[2]:
            j, kind = STREAMS[n]
            slot = neighbours(n, 2)[1][h][0]
            rs_copy(n, 2, slot, ab[kind].at[j, h], moved(pos, 0, 1)).wait_recv()
            load(n, h, 1, recv2[kind].at[j, slot], ab[kind].at[j, h]).start()
        pl.semaphore_wait(ready_sem, 6)
        done = small_start(2)
        for n, h in items[2]:
            j, kind = STREAMS[n]
            here, halves = neighbours(n, 2)
            _, block, to, slot, _ = halves[h]
            load(n, h, 0, grad_part(n, block, h), ob[kind].at[j, h]).wait()
            load(n, h, 1, recv2[kind].at[j, 0], ab[kind].at[j, h]).wait()
            add(ab[kind].at[j, h], [ab[kind].at[j, h], ob[kind].at[j, h]], (2, 4), BF)
            rs_copy(n, 2, slot, ab[kind].at[j, h], to).start()
            load(n, h, 0, grad_part(n, here, h), ob[kind].at[j, h]).start()
        done()
        for n, h in items[2]:
            j, kind = STREAMS[n]
            slot = neighbours(n, 2)[1][h][4]
            rs_copy(n, 2, slot, ab[kind].at[j, h], moved(pos, 0, 1)).wait_recv()
            load(n, h, 2, recv2[kind].at[j, slot], db[kind].at[j, h]).start()

        def last2(n, h):
            j, kind = STREAMS[n]
            order = ORDERS[j]
            low = min(order[:2])
            load(n, h, 0, grad_part(n, 0, h), ob[kind].at[j, h]).wait()
            load(n, h, 2, recv2[kind].at[j, 0], db[kind].at[j, h]).wait()
            place = (lambda a, b: (j, 2 * h + a, b)) if order[1] == low else (lambda a, b: (j, b, 2 * h + a))
            add(acc2[kind], [ob[kind].at[j, h], db[kind].at[j, h], eb[kind].at[j, h]], (2, 4), BF, place)

        def part_of(phase):
            def part(n, k, h):
                j, kind = STREAMS[n]
                return acc2[kind].at[j, k, pl.ds(2 * h, 2)] if phase == 1 else acc1[kind].at[j, k]

            return part

        def arrived(n, phase, slot):
            j, kind = STREAMS[n]
            ref = landing[phase, kind].at[j, {2: slot - 4, 1: slot, 0: slot // 2}[phase]]
            rs_copy(n, phase, slot, ref, moved(pos, 0, 1)).wait_recv()
            return ref

        for n, h in items[2]:
            arrived(n, 2, neighbours(n, 2)[1][h][3])
            last2(n, h)
            if h == 1:
                rs_start(n, 1, part_of(1))
        done = small_start(1)
        last_tile = None
        for phase in (1, 0):
            part = part_of(phase)
            dims = (2,) if phase == 1 else ()
            for n, h in items[phase]:
                slot, block, to, summed, _ = neighbours(n, phase)[1][h]
                ref = arrived(n, phase, slot)
                add(ref, [ref, part(n, block, h)], dims, BF)
                rs_copy(n, phase, summed, ref, to).start()
            last_tile = done()
            for n, h in items[phase]:
                j, kind = STREAMS[n]
                here, halves = neighbours(n, phase)
                parts = [part(n, here, h), arrived(n, phase, halves[h][4]), arrived(n, phase, halves[h][3])]
                if phase == 0:
                    add(fin[kind].at[j], parts, dims, F32)
                    continue
                add(acc1[kind], parts, dims, BF, lambda a: (j, 2 * h + a))
                if h == 1:
                    rs_start(n, 0, part_of(0))
            if phase == 1:
                done = small_start(0)

        for j in range(3):
            fsend[j] = jnp.where(even, fin[0][j, 24:48, :], fin[0][j, 0:24, :])
        last_e = jnp.concatenate([fin[2][j] for j in range(3)], axis=0)
        gsend[...] = jnp.where(even, last_e[24:48], last_e[0:24])
        swap_f = misc(5, fsend, fgot, device(partner))
        swap_g = misc(6, gsend, ggot, device(partner))
        swap_f.start()
        swap_g.start()
        for j in range(3):
            for i, at in enumerate(group_columns(2 * j + parity)):
                lanes = slice(512 * i, 512 * i + 512)
                d_win[:, at] = jnp.where(even, fin[0][j, 0:24, lanes], fin[0][j, 24:48, lanes])
            d_wout[:, 512 * j : 512 * j + 512] = fin[1][j]
        d_small[...] = last_tile
        swap_f.wait()
        swap_g.wait()
        for j in range(3):
            for i, at in enumerate(group_columns(2 * j + 1 - parity)):
                d_win[:, at] = fgot[j, :, 512 * i : 512 * i + 512]
        mine, theirs = jnp.where(even, last_e[0:24], last_e[24:48]), ggot[...]
        d_win[:, 2 * DI : 2 * DI + 2 * N] = jnp.where(even, mine, theirs)
        d_win[:, 2 * DI + 2 * N :] = jnp.where(even, theirs, mine)[:, 0:H]
        for phase in range(3):
            sent(phase)

    shapes = []
    for lead, dtype in (((3, 2, 2, 4), BF),) * 4 + (((3, 4, 4), BF), ((3, 4), BF), ((3, 6, 2), BF), ((3, 3), BF), ((3,), F32)):
        shapes += [V(lead + dims, dtype) for dims in KINDS]
    shapes += [V((3, 24, 1024), F32), V((24, 256), F32)] * 2 + [V((4, 4, 8, 128), F32), V((4, 8, 128), F32)]
    pl.run_scoped(sums, *shapes, pltpu.SemaphoreType.DMA((9, 2, 4)))

    end.wait()
    for n, (j, kind) in enumerate(STREAMS):
        ref = gath[kind].at[section, j]
        remote(ref, ref, s_sib.at[n], r_sib.at[n], sibling).wait_send()

    ag_sent(1)
    ag_sent(2)
    for n, ref in enumerate((us_, os_, dvs)):
        term(n, ref.at[2], ref.at[1]).wait_send()
    for g in (4, 5):
        dterm(g).wait_send()
    term(9, dpes.at[2], dpes.at[1]).wait_send()
    term(10, tgot, tgot).wait_send()


def step(ends, segs, counts, win, taps, bias, pre, gate, wout, dtb, alog, skip):
    vm = pl.BlockSpec(memory_space=pltpu.VMEM)
    any_ = pl.BlockSpec(memory_space=pl.ANY)
    s = jax.ShapeDtypeStruct
    V, S = pltpu.VMEM, pltpu.SemaphoreType.DMA
    large = []
    for lead in ((2, 3, 4, 4, 4), (3, 4, 4, 4), (3, 4, 2, 4)):
        large += [s(lead + dims, BF) for dims in KINDS]
    return pl.pallas_call(
        step_kernel,
        out_shape=[
            s((2, T, D), BF), s((24, 6448), F32), s((48, D), F32), s((8, 128), F32),
        ] + large,
        in_specs=[vm, vm, pl.BlockSpec(memory_space=pltpu.SMEM)] + [vm] * 9,
        out_specs=[vm] * 4 + [any_] * 9,
        scratch_shapes=[
            V((3, 24, 1024), BF), V((24, 256), BF), V((2, 4, 4, 4, 8, 128), F32),
            V((2, 8, CC), F32), V((2, 8, 128), F32), V((2, 8, CC), F32), V((4, 4, 4, 8, 128), F32),
            V((3, 4, 4, 8, 128), F32), V((3, 4, 8, 128), F32), V((3, 8, 128), F32),
            V((T, D), BF), V((T, D), BF), V((3, T, D), BF), V((3, T, DI), BF), V((3, T, D), BF), V((14, T, 1024), BF), V((3, 2, T, 256), BF),
            S((7,)), S((7,)), S((9, 3)), S((9, 3, 8)), S((6, 3)), S((6, 3)), S((9,)), S((9,)), S((9, 3)), S((9, 3, 6)), S((11,)), S((11,)), S((9,)),
            pltpu.SemaphoreType.REGULAR((2,)), pltpu.SemaphoreType.REGULAR,
        ],
        compiler_params=pltpu.CompilerParams(collective_id=0, has_side_effects=True, vmem_limit_bytes=63 * 1024 * 1024),
        name="train_step",
    )(ends, segs, counts, win, taps, bias, pre, gate, wout, dtb, alog, skip)[:4]


def results_kernel(ends, win, wout, tile, ends_out, d_win, d_taps, d_bias, d_pre, d_gate, d_wout, d_dtb, d_alog, d_skip):
    ends_out[...] = ends[...]
    d_win[...] = win[...]
    d_wout[...] = wout[...]
    d_taps[...] = tile[0:4, 0:52]
    d_bias[...] = tile[4:5, 0:52]
    d_pre[...] = tile[5:6, 0:24]
    d_gate[...] = tile[6:7, 0:48]
    d_dtb[...] = tile[7:8, 0:48]
    d_alog[...] = tile[5:6, 64:112]
    d_skip[...] = tile[6:7, 64:112]


def results(ends, win, wout, tile):
    vm = pl.BlockSpec(memory_space=pltpu.VMEM)
    s = jax.ShapeDtypeStruct
    return pl.pallas_call(
        results_kernel,
        out_shape=[
            s((2, T, D), BF), s((24, 6448), F32), s((4, 52), F32), s((1, 52), F32), s((1, 24), F32), s((1, 48), F32), s((48, D), F32),
            s((1, H), F32), s((1, H), F32), s((1, H), F32),
        ],
        in_specs=[vm] * 4,
        out_specs=[vm] * 10,
        name="results",
    )(ends, win, wout, tile)


def body(ends_in, seg_ids, block_counts, in_weight, conv_weight, conv_bias, pre_gain, gate_gain, out_weight, dt_bias, a_log, skip):
    outs = results(*step(
        ends_in[0].reshape(2, T, D), seg_ids, block_counts, in_weight[0], conv_weight[0], conv_bias, pre_gain, gate_gain, out_weight[0], dt_bias, a_log, skip
    ))
    ends_out, d_in, d_taps, d_bias, d_pre, d_gate, d_out, d_dtb, d_alog, d_skip = outs
    return ends_out.reshape(1, 2 * T, D), d_in[None], d_taps[None], d_bias, d_pre, d_gate, d_out[None], d_dtb, d_alog, d_skip


def solution(mesh):
    placed = (
        P("section", "dp", None),
        P("dp", None),
        P("dp"),
        P("section", "dp", None),
        P("section", None, "dp"),
        P("section", "dp"),
        P("section", "dp"),
        P("section", "dp"),
        P("section", "dp", None),
        P("section", None),
        P("section", None),
        P("section", None),
    )
    return jax.shard_map(
        body,
        mesh=mesh,
        in_specs=placed,
        out_specs=(
            P("section", "dp", None),
            P("section", "dp", None),
            P("section", None, "dp"),
            P("section", "dp"),
            P("section", "dp"),
            P("section", "dp"),
            P("section", "dp", None),
            P("section", None),
            P("section", None),
            P("section", None),
        ),
        check_vma=False,
    )
```

```python
import jax
import jax.numpy as jnp
from jax import lax
from jax.experimental import pallas as pl
from jax.experimental.pallas import tpu as pltpu
from jax.sharding import PartitionSpec as P

D = 1536
DI = 3072
N = 128
H = 48
CC = 3328
T = 128
EPSILON = 1e-05
F32 = jnp.float32
BF = jnp.bfloat16
GROUPS = 6
LOG2E = 1.4426950408889634
MESH = pl.DeviceIdType.MESH
KINDS = ((48, 1024), (48, 512), (16, 256))
ORDERS = ((2, 1, 0), (1, 0, 2), (0, 2, 1))
STREAMS = tuple((j, kind) for j in range(3) for kind in range(3))


def moved(pos, axis, by):
    out = list(pos)
    out[axis] = lax.rem(pos[axis] + by, 4)
    return tuple(out)


def block_index(order, phase, pos, half, sub=None):
    index = [pos[0], pos[1], pos[2]]
    for a in order[:phase]:
        index[a] = slice(None)
    if phase > 0 and half is not None:
        index[min(order[:phase])] = pl.ds(2 * half, 2) if sub is None else 2 * half + sub
    return tuple(index)


def has_half(kind, phase, half):
    return phase != 0 or half == (0 if kind == 0 else 1)


def dot(a, b, dims=((1,), (0,))):
    return lax.dot_general(a, b, (dims, ((), ())), preferred_element_type=F32)


def sigmoid(v):
    return 1.0 / (1.0 + jnp.exp(-v))


def total(v):
    return jnp.sum(v, axis=0, keepdims=True)


def exact_dot(zeros_ones, wide, dims=((1,), (0,)), flip=False, terms=3):
    out = None
    for _ in range(terms):
        term = wide.astype(BF)
        wide = wide - term.astype(F32)
        part = dot(term, zeros_ones, dims) if flip else dot(zeros_ones, term, dims)
        out = part if out is None else out + part
    return out


def keep_lanes(v, keep):
    return jnp.where(keep, v, jnp.zeros_like(v))


def step_kernel(*refs):
    it = iter(refs)
    take = lambda n: [next(it) for _ in range(n)]
    ends, segs, counts, win, taps_in, bias_in, pre_in, gate_in, wout, dtb_in, alog_in, skip_in = take(12)
    ends_out, d_win, d_wout, d_small = take(4)
    gath, grad, recv2 = take(3), take(3), take(3)
    spill, = take(1)
    wgot, egot, gs, par, hp, gr, hg, sg2, sg1, sg0, swapped, hbuf, us_, os_, dvs, dps, dpes = take(17)
    (s_misc, r_misc, s_ag, r_ag, s_small, r_small, s_sib, r_sib, s_rs, r_rs, s_terms, r_terms, own_sem, go_sem, ready_sem) = take(15)

    section = lax.axis_index("section")
    dp = lax.axis_index("dp")
    pos = (lax.div(dp, 16), lax.rem(lax.div(dp, 4), 4), lax.rem(dp, 4))
    parity = lax.rem(pos[2], 2)
    even = parity == 0
    partner = (pos[0], pos[1], pos[2] + 1 - 2 * parity)
    leading = section == 0

    def device(at, s=None):
        return {"section": section if s is None else s, "dp": at[0] * 16 + at[1] * 4 + at[2]}

    sibling = device(pos, 1 - section)

    def remote(src, dst, s, r, to):
        return pltpu.make_async_remote_copy(src, dst, s, r, device_id=to, device_id_type=MESH)

    def misc(n, src, dst, to):
        return remote(src, dst, s_misc.at[n], r_misc.at[n], to)

    barrier = pltpu.get_barrier_semaphore()
    for axis in range(3):
        for by in (1, 2, 3):
            pl.semaphore_signal(barrier, inc=1, device_id=device(moved(pos, axis, by)), device_id_type=MESH)
    pl.semaphore_signal(barrier, inc=1, device_id=sibling, device_id_type=MESH)

    def group_columns(g):
        return [pl.ds(pl.multiple_of(512 * g + first, 128), 512) for first in (0, DI)]

    def ag_copy(n, phase, slot, src, index, to):
        j, kind = STREAMS[n]
        return remote(src, gath[kind].at[section, j].at[index], s_ag.at[n, phase], r_ag.at[n, phase, slot], device(to))

    def ag_start(n, phase, unit=None):
        j, kind = STREAMS[n]
        order = ORDERS[j]
        right, left = moved(pos, order[phase], 1), moved(pos, order[phase], 3)
        for slot, (h, to) in enumerate(((0, right), (1, left), (1, right), (0, left))):
            if has_half(kind, phase, h):
                index = block_index(order, phase, pos, h)
                src = unit[kind].at[j] if phase == 0 else gath[kind].at[section, j].at[index]
                ag_copy(n, phase, slot, src, index, to).start()

    def ag_pieces(n, phase, at, h):
        order = ORDERS[STREAMS[n][0]]
        if phase < 2:
            return [block_index(order, phase, at, h)]
        return [block_index(order, phase, at, h, q) for q in range(2)]

    def to_sibling(n, index):
        j, kind = STREAMS[n]
        ref = gath[kind].at[section, j].at[index]
        remote(ref, ref, s_sib.at[n], r_sib.at[n], sibling).start()

    def ag_arrived(n, phase, slot, index, share):
        j, kind = STREAMS[n]
        ag_copy(n, phase, slot, gath[kind].at[section, j].at[index], index, moved(pos, 0, 1)).wait_recv()
        if share:
            to_sibling(n, index)

    def ag_forward(phase, share=False):
        for n, (j, kind) in enumerate(STREAMS):
            order = ORDERS[j]
            right, left = moved(pos, order[phase], 1), moved(pos, order[phase], 3)
            for slot, h, source, to in ((0, 0, left, right), (1, 1, right, left)):
                if has_half(kind, phase, h):
                    ag_arrived(n, phase, slot, block_index(order, phase, source, h), share)
                    for q, index in enumerate(ag_pieces(n, phase, source, h)):
                        ag_copy(n, phase, 4 + 2 * slot + q, gath[kind].at[section, j].at[index], index, to).start()

    def ag_rest(phase, share=False):
        for n, (j, kind) in enumerate(STREAMS):
            order = ORDERS[j]
            right, left = moved(pos, order[phase], 1), moved(pos, order[phase], 3)
            for slot, h, source in ((2, 1, left), (3, 0, right)):
                if has_half(kind, phase, h):
                    ag_arrived(n, phase, slot, block_index(order, phase, source, h), share)
        for q in range(2 if phase == 2 else 1):
            for n, (j, kind) in enumerate(STREAMS):
                far = moved(pos, ORDERS[j][phase], 2)
                for slot in (0, 1):
                    if has_half(kind, phase, slot):
                        ag_arrived(n, phase, 4 + 2 * slot + q, ag_pieces(n, phase, far, slot)[q], share)

    def ag_sent(phase):
        for n, (j, kind) in enumerate(STREAMS):
            index = {0: (0, 0, pl.ds(0, 3)), 1: (0, pl.ds(0, 3)), 2: (pl.ds(0, 3),)}[phase]
            ref = gath[kind].at[section, j].at[index]
            remote(ref, ref, s_ag.at[n, phase], r_ag.at[n, phase, 0], sibling).wait_send()

    def small_gather(phase):
        axis = (2, 1, 0)[phase]
        index = tuple(pos[: 3 - phase])
        sent = []
        for by in (1, 2, 3):
            ref = gs.at[section].at[index]
            c = remote(ref, ref, s_small.at[phase, by - 1], r_small.at[phase, by - 1], device(moved(pos, axis, by)))
            c.start()
            sent.append(c)
        return sent

    trailing = jnp.logical_not(leading)
    cotangent_0 = misc(2, ends.at[0], swapped, sibling)
    small_across = misc(3, gs.at[section], gs.at[section], sibling)

    def prologue(wsend, esend, uw, uo, ue, us):
        unit = (uw, uo, ue)
        bc = win[:, 2 * DI : 2 * DI + 2 * N].astype(F32)
        rz = jnp.concatenate([win[:, 2 * DI + 2 * N :].astype(F32), jnp.zeros((24, 2 * N - H), F32)], axis=1)
        for j in range(3):
            for i, at in enumerate(group_columns(2 * j + 1 - parity)):
                wsend[j, :, 512 * i : 512 * i + 512] = win[:, at]
        esend[...] = jnp.where(even, rz, bc).astype(BF)
        us[...] = jnp.zeros((8, 128), F32)
        us[0:4, 0:52] = taps_in[...].astype(F32)
        us[4:5, 0:52] = bias_in[...].astype(F32)
        us[5:6, 0:24] = pre_in[...].astype(F32)
        us[6:7, 0:48] = gate_in[...].astype(F32)
        us[7:8, 0:48] = dtb_in[...].astype(F32)
        us[5:6, 64:112] = alog_in[...].astype(F32)
        us[6:7, 64:112] = skip_in[...].astype(F32)
        gs[section, pos[0], pos[1], pos[2]] = us[...]
        for j in range(3):
            uo[j] = wout[:, 512 * j : 512 * j + 512]

        pl.semaphore_wait(barrier, 10)
        swap_w = misc(0, wsend, wgot, device(partner))
        swap_e = misc(1, esend, egot, device(partner))
        swap_w.start()
        swap_e.start()

        @pl.when(trailing)
        def _():
            cotangent_0.start()


        small = small_gather(0)
        swap_w.wait()
        swap_e.wait()
        for j in range(3):
            for i, at in enumerate(group_columns(2 * j + parity)):
                lanes = slice(512 * i, 512 * i + 512)
                mine, theirs = win[:, at].astype(F32), wgot[j, :, lanes].astype(F32)
                uw[j, :, lanes] = jnp.concatenate([jnp.where(even, mine, theirs), jnp.where(even, theirs, mine)], axis=0).astype(BF)
        mine, theirs = jnp.where(even, bc, rz), egot[...].astype(F32)
        both = jnp.concatenate([jnp.where(even, mine, theirs), jnp.where(even, theirs, mine)], axis=0).astype(BF)
        for j in range(3):
            ue[j] = both[16 * j : 16 * j + 16, :]
        own = []
        for n, (j, kind) in enumerate(STREAMS):
            ag_start(n, 0, unit)
            c = pltpu.make_async_copy(unit[kind].at[j], gath[kind].at[section, j].at[pos], own_sem.at[n])
            c.start()
            own.append(c)
        for c in small:
            c.wait()
        small = small_gather(1)
        ag_forward(0)
        for c in small:
            c.wait()
        small = small_gather(2)
        for c in own:
            c.wait()
        ag_rest(0)
        for c in small:
            c.wait()
        small_across.start()
        ag_sent(0)

    pl.run_scoped(
        prologue,
        pltpu.VMEM((3, 24, 1024), BF), pltpu.VMEM((24, 256), BF), pltpu.VMEM((3, 48, 1024), BF), pltpu.VMEM((3, 48, 512), BF), pltpu.VMEM((3, 16, 256), BF), pltpu.VMEM((8, 128), F32),
    )

    def own_across():
        for n, (j, kind) in enumerate(STREAMS):
            to_sibling(n, block_index(ORDERS[j], 2, pos, None))

    def go(n):
        pl.semaphore_signal(go_sem.at[n], inc=1, device_id=sibling, device_id_type=MESH)

    @pl.when(leading)
    def _():
        for n in range(9):
            ag_start(n, 1)

    misc(3, gs.at[1 - section], gs.at[1 - section], sibling).wait()
    for l in range(2):
        hp[l] = gs[l, 0, 0, 0]
        for i in range(64):
            tile = gs.at[l, i // 16, i // 4 % 4, i % 4]
            par[l, 0:5, 52 * i : 52 * i + 52] = tile[0:5, 0:52]
            par[l, 7:8, 24 * i : 24 * i + 24] = tile[5:6, 0:24]
            par[l, 5:6, 48 * i : 48 * i + 48] = tile[6:7, 0:48]
    def from_sibling(l):
        for n, (j, kind) in enumerate(STREAMS):
            ref = gath[kind].at[l, j]
            remote(ref, ref, s_sib.at[n], r_sib.at[n], sibling).wait_recv()

    @pl.when(leading)
    def _():
        ag_forward(1)
        go(0)
        ag_rest(1)
        for n in range(9):
            ag_start(n, 2)
        ag_forward(2)
        go(1)
        ag_rest(2)

    @pl.when(trailing)
    def _():
        pl.semaphore_wait(go_sem.at[0], 1)
        for n in range(9):
            ag_start(n, 1)
        ag_forward(1)
        ag_rest(1)
        own_across()
        pl.semaphore_wait(go_sem.at[1], 1)
        for n in range(9):
            ag_start(n, 2)

    landing = {}

    def rs_copy(n, phase, slot, src, to):
        j, kind = STREAMS[n]
        if phase == 2 and slot >= 4:
            dst = landing[2, kind].at[j, slot - 4]
        elif phase == 2:
            dst = recv2[kind].at[j, slot]
        else:
            dst = landing[phase, kind].at[j, slot if phase == 1 else slot // 2]
        return remote(src, dst, s_rs.at[n, phase], r_rs.at[n, phase, slot], device(to))

    def rs_start(n, phase, part):
        j, kind = STREAMS[n]
        axis = ORDERS[j][phase]
        right, left, far = (moved(pos, axis, by) for by in (1, 3, 2))
        for slot, at, h, to in ((0, far, 0, left), (1, far, 1, right), (2, left, 1, left), (3, right, 0, right)):
            if has_half(kind, phase, h):
                rs_copy(n, phase, slot, part(n, at[axis], h), to).start()

    def grad_part(n, k, h):
        j, kind = STREAMS[n]
        at = list(pos)
        at[ORDERS[j][2]] = k
        return grad[kind].at[(j,) + block_index(ORDERS[j], 2, tuple(at), h)]

    def term(n, src, dst):
        return remote(src, dst, s_terms.at[n], r_terms.at[n], sibling)

    def dterm(g):
        return term(3 + g, dps.at[12 + lax.rem(g, 2)], dps.at[6 + g])

    def layers(wbuf, ebuf, obuf, zbuf, xbuf, ybuf, tbuf, pebuf, masks, coef, allowed, tri, sel, qcol, qrow, dtrow, heads, smat, gbuf, dgacc, rowq, rowx, acc, rbuf, ut, ot, wsem, esem, osem, gsem, psem):
        def copy_w(l, g):
            j, p = lax.div(g, 2), lax.rem(g, 2)
            return [pltpu.make_async_copy(gath[0].at[l, j, :, :, 2 * m + p], wbuf.at[g, :, :, pl.ds(48 * m, 48)], wsem.at[g, m]) for m in range(2)]

        def copy_e(l):
            return [pltpu.make_async_copy(gath[2].at[l, j, :, :, 2 * m + p], ebuf.at[p, :, :, m, j], esem.at[p, m, j]) for p in range(2) for m in range(2) for j in range(3)]

        def copy_o(l, j):
            return [pltpu.make_async_copy(gath[1].at[l, j], obuf.at[j], osem.at[j])]

        def start(copies):
            for c in copies:
                c.start()

        def finish(copies):
            for c in copies:
                c.wait()

        def weights_e(p):
            return ebuf[p].reshape(D, 256)

        def start_all(l):
            start(copy_e(l))
            for g in range(GROUPS):
                start(copy_w(l, jnp.int32(g)))
            for j in range(3):
                start(copy_o(l, j))

        @pl.when(leading)
        def _():
            start_all(0)

        rows = lax.broadcasted_iota(jnp.int32, (T, T), 0)
        cols = lax.broadcasted_iota(jnp.int32, (T, T), 1)
        def set_block(b):
            seg = jnp.where(b == 0, segs[0:1, :], segs[1:2, :]).astype(F32)
            seg_s = jnp.broadcast_to(seg, (T, T))
            seg_t = jnp.transpose(seg_s)
            allowed[...] = jnp.where(rows >= cols, jnp.where(seg_t == seg_s, 1.0, 0.0), 0.0)
            for d in (1, 2, 3):
                masks[d - 1] = jnp.where(rows >= d, jnp.where(pltpu.roll(seg_t, d, 0) == seg_t, 1.0, 0.0), 0.0)
            masks[3] = jnp.where(rows < counts[b], 1.0, 0.0)

        tri[...] = jnp.where(rows >= cols, 1.0, 0.0).astype(BF)
        srow = lax.broadcasted_iota(jnp.int32, (512, T), 0)
        scol = lax.broadcasted_iota(jnp.int32, (512, T), 1)
        sel[...] = jnp.where(lax.div(srow, 64) == scol, 1.0, 0.0).astype(BF)
        low_lanes = cols < 64
        for l in range(2):
            skips = hp[l, 6:7, 64:112]
            skips = jnp.concatenate([skips, jnp.zeros((1, 80), F32)], axis=1)
            skips = jnp.broadcast_to(skips, (8, T))
            for g in range(GROUPS):
                mine = skips if g == 0 else pltpu.roll(skips, T - 8 * g, 1)
                mine = jnp.where(cols[0:8] < 8, mine, 0.0)
                par[l, 6:7, 512 * g : 512 * g + 512] = dot(mine.astype(BF), sel[...], ((1,), (1,)))[0:1]

        def conv(px, taps, bias):
            s1 = pltpu.roll(px, 1, 0) * masks[0]
            s2 = pltpu.roll(px, 2, 0) * masks[1]
            s3 = pltpu.roll(px, 3, 0) * masks[2]
            c = bias + taps[3:4] * px + taps[2:3] * s1 + taps[1:2] * s2 + taps[0:1] * s3
            return c, (s3, s2, s1, px)

        def conv_back(dc, taps):
            out = taps[3:4] * dc
            out = out + taps[2:3] * pltpu.roll(dc * masks[0], T - 1, 0)
            out = out + taps[1:2] * pltpu.roll(dc * masks[1], T - 2, 0)
            return out + taps[0:1] * pltpu.roll(dc * masks[2], T - 3, 0)

        def decay(g, hh):
            gap = jnp.broadcast_to(qcol[g][:, hh : hh + 1], (T, T)) - qrow[g][hh : hh + 1, :]
            return jnp.exp2(jnp.minimum(gap, 0.0)) * dtrow[g][hh : hh + 1, :]

        def rate_bias(l):
            return hp[l, 7:8, :]

        def rate(l):
            tile = pltpu.roll(hp[l], 64, 1)
            return -jnp.exp(jnp.where(cols[0:1] < H, tile[5:6, :], 0.0))

        def tile_at(g, k):
            return pl.ds(pl.multiple_of(512 * g + 128 * k, 128), 128)

        def prepare(s):
            q = heads[s, 1]
            qt = jnp.transpose(q)
            dtt = jnp.transpose(heads[s, 0])
            for g in range(GROUPS):
                qcol[g] = q if g == 0 else pltpu.roll(q, T - 8 * g, 1)
                qrow[g] = qt[8 * g : 8 * g + 8, :]
                dtrow[g] = dtt[8 * g : 8 * g + 8, :]

        def when_first(first, fn):
            if first is True:
                fn()
            else:
                pl.when(first)(fn)

        def forward(l, h, s, z, b, sl, first):
            set_block(b)
            rs = lax.rsqrt(jnp.sum(h * h, axis=1, keepdims=True) * (1.0 / D) + EPSILON)
            rbuf[s, 0] = jnp.broadcast_to(rs, (T, T))
            us_[sl] = (h * rs * par[l, 7:8, 0:D] * masks[3][:, 0:1]).astype(BF)
            when_first(first, lambda: finish(copy_e(l)))
            pebuf[s, :, 0:256] = dot(us_[sl], weights_e(0))
            pebuf[s, :, 256:384] = dot(us_[sl], weights_e(1))[:, 0:128]
            for j in range(2):
                at = slice(DI + 128 * j, DI + 128 * j + 128)
                c, _ = conv(pebuf[s, :, 128 * j : 128 * j + 128], par[l, 0:4, at], par[l, 4:5, at])
                smat[s, j] = (c * sigmoid(c)).astype(BF)
            v = pebuf[s, :, 256:384] + rate_bias(l)
            dt = jnp.maximum(v, 0.0) + jnp.log1p(jnp.exp(-jnp.abs(v)))
            heads[s, 0] = dt
            heads[s, 1] = exact_dot(tri[...], dt * rate(l)) * LOG2E
            gbuf[s] = dot(smat[s, 1], smat[s, 0], ((1,), (1,))) * allowed[...]
            prepare(s)
            acc[:, 0:128] = jnp.zeros((T, T), F32)

            def group(g, carry):
                when_first(first, lambda: finish(copy_w(l, g)))
                wide = pl.ds(pl.multiple_of(512 * g, 128), 512)
                zbuf[z, :, wide] = dot(us_[sl], wbuf[g, :, :, :, 0:512].reshape(D, 512))
                xbuf[z, :, wide] = dot(us_[sl], wbuf[g, :, :, :, 512:1024].reshape(D, 512))
                for k in range(4):
                    at = tile_at(g, k)
                    c, _ = conv(xbuf[z, :, at], par[l, 0:4, at], par[l, 4:5, at])
                    x = c * sigmoid(c)
                    xb = x.astype(BF)
                    both = jnp.concatenate([keep_lanes(xb, low_lanes), keep_lanes(xb, ~low_lanes)], axis=0)
                    w = jnp.concatenate([(gbuf[s] * decay(g, 2 * k + i)).astype(BF) for i in range(2)], axis=1)
                    y = dot(w, both) + par[l, 6:7, at] * x
                    ybuf[z, :, at] = y
                    zz_ = zbuf[z, :, at]
                    e = y * (zz_ * sigmoid(zz_))
                    tbuf[:, at] = e
                    acc[:, 0:128] += e * e
                return carry

            lax.fori_loop(0, GROUPS, group, 0)
            r = lax.rsqrt(jnp.sum(acc[:, 0:128], axis=1, keepdims=True) * (1.0 / DI) + EPSILON)
            rbuf[s, 1] = jnp.broadcast_to(r, (T, T))
            for g in range(GROUPS):
                at = slice(512 * g, 512 * g + 512)
                os_[sl, :, at] = (tbuf[:, at] * r * par[l, 5:6, at]).astype(BF)
            for j in range(3):
                when_first(first, lambda j=j: finish(copy_o(l, j)))
                acc[:, 512 * j : 512 * j + 512] = dot(os_[sl], obuf[j].reshape(DI, 512))
            return h + acc[...]

        def backward(l, h, dh, s, z, b, sl, gi, first):
            set_block(b)
            if l == 1:
                dvs[sl] = dh.astype(BF)

            if l == 1:
                @pl.when(leading)
                def _():
                    for n, ref in enumerate((us_, os_, dvs)):
                        term(n, ref.at[2], ref.at[1]).start()
            else:
                when_first(first, lambda: [finish(copy_o(0, j)) for j in range(3)] and None)
            acc[:, 0:128] = jnp.zeros((T, T), F32)

            def gated_back(zz, carry):
                wide = pl.ds(pl.multiple_of(768 * zz, 128), 768)
                do = None
                for j in range(3):
                    part = dot(dvs[sl, :, 512 * j : 512 * j + 512], obuf[j, zz].reshape(768, 512), ((1,), (1,)))
                    do = part if do is None else do + part
                tbuf[:, wide] = do
                for k in range(6):
                    at = pl.ds(pl.multiple_of(768 * zz + 128 * k, 128), 128)
                    zz_ = zbuf[z, :, at]
                    e = ybuf[z, :, at] * (zz_ * sigmoid(zz_))
                    prod = tbuf[:, at] * e
                    gr[gi, 5:6, at] = total(prod * rbuf[s, 1])
                    acc[:, 0:128] += prod * par[l, 5:6, at]
                return carry

            lax.fori_loop(0, 4, gated_back, 0)
            if l == 1:
                @pl.when(leading)
                def _():
                    for j in range(3):
                        start(copy_o(0, j))
            r = rbuf[s, 1]
            coef[...] = jnp.broadcast_to(jnp.sum(acc[:, 0:128], axis=1, keepdims=True) * (1.0 / DI), (T, T)) * r * r * r
            prepare(s)
            dgacc[...] = jnp.zeros((T, T), F32)
            rowq[...] = jnp.zeros((T, T), F32)
            rowx[...] = jnp.zeros((T, T), F32)
            acc[...] = jnp.zeros((T, D), F32)

            def second(g, carry):
                if l == 0:
                    when_first(first, lambda: finish(copy_w(0, g)))
                    here = 6 * b + g
                else:
                    here = lax.select(leading, 12 + lax.rem(g, 2), g)

                    @pl.when(jnp.logical_and(leading, g >= 2))
                    def _():
                        dterm(g - 2).wait_send()

                sums_q, sums_x = None, None
                for k in range(4):
                    at = tile_at(g, k)
                    zz_ = zbuf[z, :, at]
                    y = ybuf[z, :, at]
                    sz = sigmoid(zz_)
                    silu = zz_ * sz
                    de = rbuf[s, 1] * (tbuf[:, at] * par[l, 5:6, at]) - (y * silu) * coef[...]
                    dyb = (de * silu).astype(BF)
                    dz = de * y * (sz + silu * (1.0 - sz))
                    dps[here, :, 128 * k : 128 * k + 128] = dz.astype(BF)
                    taps = par[l, 0:4, at]
                    c, shifts = conv(xbuf[z, :, at], taps, par[l, 4:5, at])
                    sc = sigmoid(c)
                    x = c * sc
                    xb = x.astype(BF)
                    dyw = dyb.astype(F32)
                    skip = par[l, 6:7, at]
                    xt = jnp.concatenate([keep_lanes(xb, low_lanes), keep_lanes(xb, ~low_lanes)], axis=0)
                    dyt = jnp.concatenate([keep_lanes(dyb, low_lanes), keep_lanes(dyb, ~low_lanes)], axis=0)
                    dw = dot(dyb, xt, ((1,), (1,)))
                    ws, dg = [], None
                    for i in range(2):
                        e = decay(g, 2 * k + i)
                        ws.append((gbuf[s] * e).astype(BF))
                        part = dw[:, 128 * i : 128 * i + 128] * e
                        dg = part if dg is None else dg + part
                    dgacc[...] += dg
                    dx0 = dot(jnp.concatenate(ws, axis=0), dyt, ((0,), (0,)))
                    dx = dx0 + skip * dyw
                    gr[gi, 6:7, at] = total(dyw * x)
                    one = sel[128 * k : 128 * k + 128, :]
                    part = exact_dot(one, dyw * (y - skip * x), flip=True, terms=2)
                    sums_q = part if sums_q is None else sums_q + part
                    part = exact_dot(one, xb.astype(F32) * dx0, flip=True, terms=2)
                    sums_x = part if sums_x is None else sums_x + part
                    dc = dx * (sc + x * (1.0 - sc))
                    for t in range(4):
                        gr[gi, t : t + 1, at] = total(dc * shifts[t])
                    gr[gi, 4:5, at] = total(dc)
                    dps[here, :, 512 + 128 * k : 640 + 128 * k] = conv_back(dc, taps).astype(BF)
                rowq[...] += pltpu.roll(sums_q, 8 * g, 1)
                rowx[...] += pltpu.roll(sums_x, 8 * g, 1)

                if l == 1:
                    @pl.when(leading)
                    def _():
                        dterm(g).start()

                for zz in range(4):
                    acc[:, 384 * zz : 384 * zz + 384] += dot(dps[here], wbuf[g, zz].reshape(384, 1024), ((1,), (1,)))
                if l == 1:
                    @pl.when(leading)
                    def _():
                        start(copy_w(0, g))
                return carry

            lax.fori_loop(0, GROUPS, second, 0)
            dg = (dgacc[...] * allowed[...]).astype(BF)
            d_states = (dot(dg, smat[s, 1], ((0,), (0,))), dot(dg, smat[s, 0]))
            for j in range(2):
                at = slice(DI + 128 * j, DI + 128 * j + 128)
                taps = par[l, 0:4, at]
                c, shifts = conv(pebuf[s, :, 128 * j : 128 * j + 128], taps, par[l, 4:5, at])
                sc = sigmoid(c)
                dc = d_states[j] * (sc + c * sc * (1.0 - sc))
                for t in range(4):
                    gr[gi, t : t + 1, at] = total(dc * shifts[t])
                gr[gi, 4:5, at] = total(dc)
                dpes[sl, 0, :, 128 * j : 128 * j + 128] = conv_back(dc, taps).astype(BF)
            v = pebuf[s, :, 256:384] + rate_bias(l)
            sv = sigmoid(v)
            dt = heads[s, 0]
            back = exact_dot(tri[...], rowq[...] - rowx[...], ((0,), (0,)))
            ratio = jnp.where(v < -15.0, 1.0, sv / jnp.maximum(dt, 1e-30))
            dr = jnp.where(cols < H, rowx[...] * ratio + back * rate(l) * sv, 0.0)
            d_rate = total(jnp.where(cols < H, back * dt, 0.0)) * rate(l)
            dpes[sl, 1, :, 0:128] = dr.astype(BF)
            dpes[sl, 1, :, 128:256] = jnp.zeros((T, T), BF)

            if l == 1:
                @pl.when(leading)
                def _():
                    term(9, dpes.at[2], dpes.at[1]).start()
            else:
                when_first(first, lambda: finish(copy_e(0)))
            du = acc[...]
            for p in range(2):
                du = du + dot(dpes[sl, p], weights_e(p), ((1,), (1,)))
            if l == 1:
                @pl.when(leading)
                def _():
                    start(copy_e(0))

            hn = h * rbuf[s, 0][:, 0:1]
            du = du * masks[3][:, 0:1]
            gr[gi, 7:8, 0:D] = total(du * hn)
            t = du * par[l, 7:8, 0:D]
            mean = jnp.sum(t * hn, axis=1, keepdims=True) * (1.0 / D)
            dh_in = dh + rbuf[s, 0][:, 0:1] * (t - hn * mean)
            hg[gi, 0:1] = total(dr)
            hg[gi, 1:2] = d_rate
            return dh_in

        def small_tiles(l):
            skips = jnp.zeros((8, T), F32)
            for g in range(GROUPS):
                mine = exact_dot(sel[...], jnp.broadcast_to(gr[0, 6:7, 512 * g : 512 * g + 512], (8, 512)), flip=True)
                skips = skips + (mine if g == 0 else pltpu.roll(mine, 8 * g, 1))
            for i in range(64):
                tile = gs.at[l, i // 16, i // 4 % 4, i % 4]
                tile[0:5, 0:52] = gr[0, 0:5, 52 * i : 52 * i + 52]
                tile[5:6, 0:24] = gr[0, 7:8, 24 * i : 24 * i + 24]
                tile[6:7, 0:48] = gr[0, 5:6, 48 * i : 48 * i + 48]
                tile[7:8, 0:128] = hg[0, 0:1]
                tile[5:6, 64:112] = hg[0, 1:2, 0:48]
                tile[6:7, 64:112] = skips[0:1, 0:48]

        def products(l):
            if l == 1:
                for n, ref in enumerate((us_, os_, dvs)):
                    term(n, ref.at[2], ref.at[1]).wait_recv()
                for g in range(GROUPS):
                    dterm(g).wait_recv()
                term(9, dpes.at[2], dpes.at[1]).wait_recv()

            def stacked(ref, *index):
                return jnp.concatenate([ref[(0,) + index], ref[(1,) + index]], axis=0)

            def turn(i, carry):
                at = pl.ds(pl.multiple_of(128 * i, 128), 128)
                ut[at, :] = jnp.transpose(stacked(us_, slice(None), at))
                return carry

            lax.fori_loop(0, D // 128, turn, 0)

            for p in range(2):
                for zz in range(4):
                    de = dot(ut[384 * zz : 384 * zz + 384, :], stacked(dpes, p))
                    ebuf[p, zz] = de.astype(BF).reshape(4, 2, 3, 16, 256)
            for p in range(2):
                for m in range(2):
                    for j in range(3):
                        pltpu.make_async_copy(ebuf.at[p, :, :, m, j], grad[2].at[j, :, :, 2 * m + p], gsem.at[j, 2]).start()

            def wstep(i, carry):
                g, zz = lax.div(i, 4), lax.rem(i, 4)
                u = ut[pl.ds(pl.multiple_of(384 * zz, 128), 384), :]
                for half in range(2):
                    at = slice(512 * half, 512 * half + 512)
                    d = jnp.concatenate([dps[g, :, at], dps[6 + g, :, at]], axis=0)
                    wbuf[g, zz, :, :, at] = dot(u, d).astype(BF).reshape(4, 96, 512)
                j, p = lax.div(g, 2), lax.rem(g, 2)
                for m in range(2):
                    pltpu.make_async_copy(wbuf.at[g, zz, :, pl.ds(48 * m, 48)], grad[0].at[j, zz, :, 2 * m + p], gsem.at[j, 0]).start()
                return carry

            def ostep(zz, carry):
                for i in range(6):
                    at = pl.ds(pl.multiple_of(768 * zz + 128 * i, 128), 128)
                    ot[128 * i : 128 * i + 128, :] = jnp.transpose(stacked(os_, slice(None), at))
                for j in range(3):
                    d = stacked(dvs, slice(None), slice(512 * j, 512 * j + 512))
                    for half in range(2):
                        o = ot[384 * half : 384 * half + 384, :]
                        obuf[j, zz, 2 * half : 2 * half + 2] = dot(o, d).astype(BF).reshape(2, 4, 48, 512)
                    pltpu.make_async_copy(obuf.at[j, zz], grad[1].at[j, zz], gsem.at[j, 1]).start()
                return carry

            def written(j, kind):
                pltpu.make_async_copy(grad[kind].at[j], grad[kind].at[j], gsem.at[j, kind]).wait()
                rs_start(3 * j + kind, 2, grad_part)

            for j in range(3):
                lax.fori_loop(8 * j, 8 * j + 8, wstep, 0)
                if j > 0:
                    written(j - 1, 0)
            lax.fori_loop(0, 4, ostep, 0)
            written(2, 0)
            for kind in (1, 2):
                for j in range(3):
                    written(j, kind)

        middle_1 = misc(7, dvs.at[0], hbuf, sibling)
        out_0 = misc(4, ends_out.at[0], ends_out.at[0], sibling)
        d_middle_1 = misc(8, dvs.at[2], dvs.at[1], sibling)
        sets = [pltpu.make_async_copy(ref.at[0], spill.at[n], psem.at[n]) for n, ref in enumerate((zbuf, xbuf, ybuf))]
        sets_back = [pltpu.make_async_copy(spill.at[n], ref.at[0], psem.at[n]) for n, ref in enumerate((zbuf, xbuf, ybuf))]

        @pl.when(leading)
        def _():
            def block(b, carry):
                out = forward(0, ends[b].astype(F32), b, b, b, b, b == 0).astype(BF)

                @pl.when(b == 0)
                def _():
                    hbuf[...] = out
                    start(sets)

                @pl.when(b == 1)
                def _():
                    dvs[0] = out
                    middle_1.start()

                return carry

            lax.fori_loop(0, 2, block, 0)
            finish(sets)
            cotangent_0.wait_recv()
            from_sibling(1)

        @pl.when(trailing)
        def _():
            ag_forward(2, True)
            ag_rest(2, True)
            cotangent_0.wait_send()
            middle_1.wait_recv()

        start_all(1)
        out = forward(1, hbuf[...].astype(F32), 2, 0, section, lax.select(leading, 2, 0), True).astype(BF)

        @pl.when(leading)
        def _():
            ends_out[0] = out
            out_0.start()

        @pl.when(trailing)
        def _():
            ends_out[1] = out

        cotangent = jnp.where(leading, swapped[...].astype(F32), ends[1].astype(F32))
        d_middle = backward(1, hbuf[...].astype(F32), cotangent, 2, 0, section, lax.select(leading, 2, 0), 0, True).astype(BF)

        @pl.when(trailing)
        def _():
            dvs[2] = d_middle
            d_middle_1.start()
            small_tiles(1)
            products(1)
            d_middle_1.wait_send()
            out_0.wait_recv()

        @pl.when(leading)
        def _():
            start(sets_back)
            middle_1.wait_send()
            dvs[0] = d_middle
            small_tiles(1)
            term(10, gs.at[1], gs.at[0]).start()
            out_0.wait_send()
            d_middle_1.wait_recv()

            def block(i, carry):
                b = 1 - i

                @pl.when(i == 1)
                def _():
                    finish(sets_back)

                ends_out[b] = backward(0, ends[b].astype(F32), dvs[b].astype(F32), b, b, b, b, i, i == 0).astype(BF)
                return carry

            lax.fori_loop(0, 2, block, 0)
            gr[0] += gr[1]
            hg[0] += hg[1]
            small_tiles(0)
            products(0)

    V = pltpu.VMEM
    pl.run_scoped(
        layers,
        V((6, 4, 4, 96, 1024), BF), V((2, 4, 4, 2, 3, 16, 256), BF), V((3, 4, 4, 4, 48, 512), BF),
        V((2, T, DI), F32), V((2, T, DI), F32), V((2, T, DI), F32), V((T, DI), F32), V((3, T, 384), F32),
        V((4, T, T), F32), V((T, T), F32), V((T, T), F32), V((T, T), BF), V((512, T), BF), V((6, T, T), F32), V((6, 8, T), F32), V((6, 8, T), F32),
        V((3, 2, T, T), F32), V((3, 2, T, T), BF), V((3, T, T), F32), V((T, T), F32), V((T, T), F32), V((T, T), F32), V((T, D), F32), V((3, 2, T, T), F32),
        V((D, 256), BF), V((768, 256), BF),
        pltpu.SemaphoreType.DMA((6, 2)), pltpu.SemaphoreType.DMA((2, 2, 3)), pltpu.SemaphoreType.DMA((3,)), pltpu.SemaphoreType.DMA((3, 3)), pltpu.SemaphoreType.DMA((3,)),
    )

    def sums(*bufs):
        it = iter(bufs)
        take = lambda n: [next(it) for _ in range(n)]
        ab, ob, db, eb, acc2, acc1, b1, b0, fin = (take(3) for _ in range(9))
        fsend, gsend, fgot, ggot, sa2, sa1, lsem = it
        for kind in range(3):
            landing[2, kind], landing[1, kind], landing[0, kind] = eb[kind], b1[kind], b0[kind]
        for axis in range(3):
            for by in (1, 3):
                pl.semaphore_signal(ready_sem, inc=1, device_id=device(moved(pos, axis, by)), device_id_type=MESH)

        def load(n, h, which, src, dst):
            return pltpu.make_async_copy(src, dst, lsem.at[n, h, which])

        def add(dst, parts, dims, dtype, place=None):
            if not dims:
                out = parts[0][...].astype(F32)
                for p in parts[1:]:
                    out = out + p[...].astype(F32)
                dst[...] = out.astype(dtype)
                return
            count = dims[0] * (dims[1] if len(dims) > 1 else 1)

            def one(i, carry):
                index = (i,) if len(dims) == 1 else (lax.div(i, dims[1]), lax.rem(i, dims[1]))
                out = parts[0][index].astype(F32)
                for p in parts[1:]:
                    out = out + p[index].astype(F32)
                dst[index if place is None else place(*index)] = out.astype(dtype)
                return carry

            lax.fori_loop(0, count, one, 0)

        def neighbours(n, phase):
            axis = ORDERS[STREAMS[n][0]][phase]
            right, left = moved(pos, axis, 1), moved(pos, axis, 3)
            return pos[axis], {0: (0, left[axis], left, 4, 3), 1: (1, right[axis], right, 5, 2)}

        def sent(phase):
            for n, (j, kind) in enumerate(STREAMS):
                if phase == 2:
                    ref = grad[kind].at[j, pl.ds(0, 3)]
                else:
                    ref = landing[phase, kind].at[j, pl.ds(0, 3 if phase == 0 else 6)]
                remote(ref, ref, s_rs.at[n, phase], r_rs.at[n, phase, 0], sibling).wait_send()

        items = {phase: [(3 * j + kind, h) for kind in range(3) for j in range(3) for h in (0, 1) if has_half(kind, phase, h)] for phase in range(3)}
        by_kind = [3 * j + kind for kind in range(3) for j in range(3)]

        def small_start(phase):
            axis = ORDERS[0][phase]
            cur = (sa1, sa2, gs.at[section])[phase]
            got = (sg0, sg1, sg2)[phase]
            copies = []
            for by in (1, 2, 3):
                to = moved(pos, axis, by)
                c = remote(cur.at[to[axis]], got.at[by - 1], s_small.at[3 + phase, by - 1], r_small.at[3 + phase, by - 1], device(to))
                c.start()
                copies.append(c)

            def done():
                for c in copies:
                    c.wait()
                out = cur[pos[axis]] + got[0] + got[1] + got[2]
                if phase == 0:
                    return out
                (sa1, sa2)[phase - 1][...] = out
                return None

            return done

        @pl.when(trailing)
        def _():
            term(10, gs.at[1], gs.at[0]).wait_recv()
            gs[1] += gs[0]

        for n, h in items[2]:
            j, kind = STREAMS[n]
            _, halves = neighbours(n, 2)
            load(n, h, 0, grad_part(n, halves[h][1], h), ob[kind].at[j, h]).start()
        for n, h in items[2]:
            j, kind = STREAMS[n]
            slot = neighbours(n, 2)[1][h][0]
            rs_copy(n, 2, slot, ab[kind].at[j, h], moved(pos, 0, 1)).wait_recv()
            load(n, h, 1, recv2[kind].at[j, slot], ab[kind].at[j, h]).start()
        pl.semaphore_wait(ready_sem, 6)
        done = small_start(2)
        for n, h in items[2]:
            j, kind = STREAMS[n]
            here, halves = neighbours(n, 2)
            _, block, to, slot, _ = halves[h]
            load(n, h, 0, grad_part(n, block, h), ob[kind].at[j, h]).wait()
            load(n, h, 1, recv2[kind].at[j, 0], ab[kind].at[j, h]).wait()
            add(ab[kind].at[j, h], [ab[kind].at[j, h], ob[kind].at[j, h]], (2, 4), BF)
            rs_copy(n, 2, slot, ab[kind].at[j, h], to).start()
            load(n, h, 0, grad_part(n, here, h), ob[kind].at[j, h]).start()
        done()
        for n, h in items[2]:
            j, kind = STREAMS[n]
            slot = neighbours(n, 2)[1][h][4]
            rs_copy(n, 2, slot, ab[kind].at[j, h], moved(pos, 0, 1)).wait_recv()
            load(n, h, 2, recv2[kind].at[j, slot], db[kind].at[j, h]).start()

        def last2(n, h):
            j, kind = STREAMS[n]
            order = ORDERS[j]
            low = min(order[:2])
            load(n, h, 0, grad_part(n, 0, h), ob[kind].at[j, h]).wait()
            load(n, h, 2, recv2[kind].at[j, 0], db[kind].at[j, h]).wait()
            place = (lambda a, b: (j, 2 * h + a, b)) if order[1] == low else (lambda a, b: (j, b, 2 * h + a))
            add(acc2[kind], [ob[kind].at[j, h], db[kind].at[j, h], eb[kind].at[j, h]], (2, 4), BF, place)

        def part_of(phase):
            def part(n, k, h):
                j, kind = STREAMS[n]
                return acc2[kind].at[j, k, pl.ds(2 * h, 2)] if phase == 1 else acc1[kind].at[j, k]

            return part

        def arrived(n, phase, slot):
            j, kind = STREAMS[n]
            ref = landing[phase, kind].at[j, {2: slot - 4, 1: slot, 0: slot // 2}[phase]]
            rs_copy(n, phase, slot, ref, moved(pos, 0, 1)).wait_recv()
            return ref

        for n, h in items[2]:
            arrived(n, 2, neighbours(n, 2)[1][h][3])
            last2(n, h)
            if h == 1:
                rs_start(n, 1, part_of(1))
        done = small_start(1)
        last_tile = None
        for phase in (1, 0):
            part = part_of(phase)
            dims = (2,) if phase == 1 else ()
            for n, h in items[phase]:
                slot, block, to, summed, _ = neighbours(n, phase)[1][h]
                ref = arrived(n, phase, slot)
                add(ref, [ref, part(n, block, h)], dims, BF)
                rs_copy(n, phase, summed, ref, to).start()
            last_tile = done()
            for n, h in items[phase]:
                j, kind = STREAMS[n]
                here, halves = neighbours(n, phase)
                parts = [part(n, here, h), arrived(n, phase, halves[h][4]), arrived(n, phase, halves[h][3])]
                if phase == 0:
                    add(fin[kind].at[j], parts, dims, F32)
                    continue
                add(acc1[kind], parts, dims, BF, lambda a: (j, 2 * h + a))
                if h == 1:
                    rs_start(n, 0, part_of(0))
            if phase == 1:
                done = small_start(0)

        for j in range(3):
            fsend[j] = jnp.where(even, fin[0][j, 24:48, :], fin[0][j, 0:24, :])
        last_e = jnp.concatenate([fin[2][j] for j in range(3)], axis=0)
        gsend[...] = jnp.where(even, last_e[24:48], last_e[0:24])
        swap_f = misc(5, fsend, fgot, device(partner))
        swap_g = misc(6, gsend, ggot, device(partner))
        swap_f.start()
        swap_g.start()
        for j in range(3):
            for i, at in enumerate(group_columns(2 * j + parity)):
                lanes = slice(512 * i, 512 * i + 512)
                d_win[:, at] = jnp.where(even, fin[0][j, 0:24, lanes], fin[0][j, 24:48, lanes])
            d_wout[:, 512 * j : 512 * j + 512] = fin[1][j]
        d_small[...] = last_tile
        swap_f.wait()
        swap_g.wait()
        for j in range(3):
            for i, at in enumerate(group_columns(2 * j + 1 - parity)):
                d_win[:, at] = fgot[j, :, 512 * i : 512 * i + 512]
        mine, theirs = jnp.where(even, last_e[0:24], last_e[24:48]), ggot[...]
        d_win[:, 2 * DI : 2 * DI + 2 * N] = jnp.where(even, mine, theirs)
        d_win[:, 2 * DI + 2 * N :] = jnp.where(even, theirs, mine)[:, 0:H]
        for phase in range(3):
            sent(phase)

    shapes = []
    for lead, dtype in (((3, 2, 2, 4), BF),) * 4 + (((3, 4, 4), BF), ((3, 4), BF), ((3, 6, 2), BF), ((3, 3), BF), ((3,), F32)):
        shapes += [V(lead + dims, dtype) for dims in KINDS]
    shapes += [V((3, 24, 1024), F32), V((24, 256), F32)] * 2 + [V((4, 4, 8, 128), F32), V((4, 8, 128), F32)]
    pl.run_scoped(sums, *shapes, pltpu.SemaphoreType.DMA((9, 2, 4)))

    @pl.when(trailing)
    def _():
        for n, (j, kind) in enumerate(STREAMS):
            ref = gath[kind].at[1, j]
            remote(ref, ref, s_sib.at[n], r_sib.at[n], sibling).wait_send()

    @pl.when(leading)
    def _():
        for n, ref in enumerate((us_, os_, dvs)):
            term(n, ref.at[2], ref.at[1]).wait_send()
        for g in (4, 5):
            dterm(g).wait_send()
        term(9, dpes.at[2], dpes.at[1]).wait_send()
        term(10, gs.at[1], gs.at[0]).wait_send()

    ag_sent(1)
    ag_sent(2)


def step(ends, segs, counts, win, taps, bias, pre, gate, wout, dtb, alog, skip):
    vm = pl.BlockSpec(memory_space=pltpu.VMEM)
    any_ = pl.BlockSpec(memory_space=pl.ANY)
    s = jax.ShapeDtypeStruct
    V, S = pltpu.VMEM, pltpu.SemaphoreType.DMA
    large = []
    for lead in ((2, 3, 4, 4, 4), (3, 4, 4, 4), (3, 4, 2, 4)):
        large += [s(lead + dims, BF) for dims in KINDS]
    return pl.pallas_call(
        step_kernel,
        out_shape=[
            s((2, T, D), BF), s((24, 6448), F32), s((48, D), F32), s((8, 128), F32),
        ] + large + [s((3, T, DI), F32)],
        in_specs=[vm, vm, pl.BlockSpec(memory_space=pltpu.SMEM)] + [vm] * 9,
        out_specs=[vm] * 4 + [any_] * 10,
        scratch_shapes=[
            V((3, 24, 1024), BF), V((24, 256), BF), V((2, 4, 4, 4, 8, 128), F32),
            V((2, 8, CC), F32), V((2, 8, 128), F32), V((2, 8, CC), F32), V((2, 8, 128), F32),
            V((3, 4, 4, 8, 128), F32), V((3, 4, 8, 128), F32), V((3, 8, 128), F32),
            V((T, D), BF), V((T, D), BF), V((3, T, D), BF), V((3, T, DI), BF), V((3, T, D), BF), V((14, T, 1024), BF), V((3, 2, T, 256), BF),
            S((9,)), S((9,)), S((9, 3)), S((9, 3, 8)), S((6, 3)), S((6, 3)), S((9,)), S((9,)), S((9, 3)), S((9, 3, 6)), S((11,)), S((11,)), S((9,)),
            pltpu.SemaphoreType.REGULAR((2,)), pltpu.SemaphoreType.REGULAR,
        ],
        compiler_params=pltpu.CompilerParams(collective_id=0, has_side_effects=True, vmem_limit_bytes=65280 * 1024),
        name="train_step",
    )(ends, segs, counts, win, taps, bias, pre, gate, wout, dtb, alog, skip)[:4]


def results_kernel(ends, win, wout, tile, ends_out, d_win, d_taps, d_bias, d_pre, d_gate, d_wout, d_dtb, d_alog, d_skip):
    ends_out[...] = ends[...]
    d_win[...] = win[...]
    d_wout[...] = wout[...]
    d_taps[...] = tile[0:4, 0:52]
    d_bias[...] = tile[4:5, 0:52]
    d_pre[...] = tile[5:6, 0:24]
    d_gate[...] = tile[6:7, 0:48]
    d_dtb[...] = tile[7:8, 0:48]
    d_alog[...] = tile[5:6, 64:112]
    d_skip[...] = tile[6:7, 64:112]


def results(ends, win, wout, tile):
    vm = pl.BlockSpec(memory_space=pltpu.VMEM)
    s = jax.ShapeDtypeStruct
    return pl.pallas_call(
        results_kernel,
        out_shape=[
            s((2, T, D), BF), s((24, 6448), F32), s((4, 52), F32), s((1, 52), F32), s((1, 24), F32), s((1, 48), F32), s((48, D), F32),
            s((1, H), F32), s((1, H), F32), s((1, H), F32),
        ],
        in_specs=[vm] * 4,
        out_specs=[vm] * 10,
        name="results",
    )(ends, win, wout, tile)


def body(ends_in, seg_ids, block_counts, in_weight, conv_weight, conv_bias, pre_gain, gate_gain, out_weight, dt_bias, a_log, skip):
    outs = results(*step(
        ends_in[0].reshape(2, T, D), seg_ids, block_counts, in_weight[0], conv_weight[0], conv_bias, pre_gain, gate_gain, out_weight[0], dt_bias, a_log, skip
    ))
    ends_out, d_in, d_taps, d_bias, d_pre, d_gate, d_out, d_dtb, d_alog, d_skip = outs
    return ends_out.reshape(1, 2 * T, D), d_in[None], d_taps[None], d_bias, d_pre, d_gate, d_out[None], d_dtb, d_alog, d_skip


def solution(mesh):
    placed = (
        P("section", "dp", None),
        P("dp", None),
        P("dp"),
        P("section", "dp", None),
        P("section", None, "dp"),
        P("section", "dp"),
        P("section", "dp"),
        P("section", "dp"),
        P("section", "dp", None),
        P("section", None),
        P("section", None),
        P("section", None),
    )
    return jax.shard_map(
        body,
        mesh=mesh,
        in_specs=placed,
        out_specs=(
            P("section", "dp", None),
            P("section", "dp", None),
            P("section", None, "dp"),
            P("section", "dp"),
            P("section", "dp"),
            P("section", "dp"),
            P("section", "dp", None),
            P("section", None),
            P("section", None),
            P("section", None),
        ),
        check_vma=False,
    )
```

```python
import jax
import jax.numpy as jnp
from jax import lax
from jax.experimental import pallas as pl
from jax.experimental.pallas import tpu as pltpu
from jax.sharding import PartitionSpec as P

D = 1536
DI = 3072
N = 128
H = 48
CC = 3328
T = 128
EPSILON = 1e-05
F32 = jnp.float32
BF = jnp.bfloat16
GROUPS = 6
LOG2E = 1.4426950408889634
MESH = pl.DeviceIdType.MESH
KINDS = ((48, 1024), (48, 512), (16, 256))
ORDERS = ((2, 1, 0), (1, 0, 2), (0, 2, 1))
STREAMS = tuple((j, kind) for j in range(3) for kind in range(3))
ALL = (0, 3, 6, 1, 4, 7, 2, 5, 8)
OUT = (1, 4, 7)
REST = (0, 3, 6, 2, 5, 8)


def moved(pos, axis, by):
    out = list(pos)
    out[axis] = lax.rem(pos[axis] + by, 4)
    return tuple(out)


def block_index(order, phase, pos, half, sub=None):
    index = [pos[0], pos[1], pos[2]]
    for a in order[:phase]:
        index[a] = slice(None)
    if phase > 0 and half is not None:
        index[min(order[:phase])] = pl.ds(2 * half, 2) if sub is None else 2 * half + sub
    return tuple(index)


def has_half(kind, phase, half):
    return phase != 0 or half == (0 if kind == 0 else 1)


def dot(a, b, dims=((1,), (0,))):
    return lax.dot_general(a, b, (dims, ((), ())), preferred_element_type=F32)


def sigmoid(v):
    return 0.5 * jnp.tanh(0.5 * v) + 0.5


def total(v):
    return jnp.sum(v, axis=0, keepdims=True)


def exact_dot(zeros_ones, wide, dims=((1,), (0,)), flip=False, terms=3):
    out = None
    for _ in range(terms):
        term = wide.astype(BF)
        wide = wide - term.astype(F32)
        part = dot(term, zeros_ones, dims) if flip else dot(zeros_ones, term, dims)
        out = part if out is None else out + part
    return out


def keep_lanes(v, keep):
    return jnp.where(keep, v, jnp.zeros_like(v))


def step_kernel(*refs):
    it = iter(refs)
    take = lambda n: [next(it) for _ in range(n)]
    ends, segs, counts, win, taps_in, bias_in, pre_in, gate_in, wout, dtb_in, alog_in, skip_in = take(12)
    ends_out, d_win, d_wout, d_small = take(4)
    gath, grad, recv2 = take(3), take(3), take(3)
    spill, = take(1)
    wgot, egot, gs, par, hp, gr, hg, sg2, sg1, sg0, swapped, hbuf, us_, os_, dvs, dps, dpes = take(17)
    (s_misc, r_misc, s_ag, r_ag, s_small, r_small, s_sib, r_sib, s_rs, r_rs, s_terms, r_terms, own_sem, go_sem, ready_sem) = take(15)

    section = lax.axis_index("section")
    dp = lax.axis_index("dp")
    pos = (lax.div(dp, 16), lax.rem(lax.div(dp, 4), 4), lax.rem(dp, 4))
    parity = lax.rem(pos[2], 2)
    even = parity == 0
    partner = (pos[0], pos[1], pos[2] + 1 - 2 * parity)
    leading = section == 0

    def device(at, s=None):
        return {"section": section if s is None else s, "dp": at[0] * 16 + at[1] * 4 + at[2]}

    sibling = device(pos, 1 - section)

    def remote(src, dst, s, r, to):
        return pltpu.make_async_remote_copy(src, dst, s, r, device_id=to, device_id_type=MESH)

    def misc(n, src, dst, to):
        return remote(src, dst, s_misc.at[n], r_misc.at[n], to)

    barrier = pltpu.get_barrier_semaphore()
    for axis in range(3):
        for by in (1, 2, 3):
            pl.semaphore_signal(barrier, inc=1, device_id=device(moved(pos, axis, by)), device_id_type=MESH)
    pl.semaphore_signal(barrier, inc=1, device_id=sibling, device_id_type=MESH)

    def group_columns(g):
        return [pl.ds(pl.multiple_of(512 * g + first, 128), 512) for first in (0, DI)]

    def ag_copy(n, phase, slot, src, index, to):
        j, kind = STREAMS[n]
        return remote(src, gath[kind].at[section, j].at[index], s_ag.at[n, phase], r_ag.at[n, phase, slot], device(to))

    def ag_start(n, phase, unit=None):
        j, kind = STREAMS[n]
        order = ORDERS[j]
        right, left = moved(pos, order[phase], 1), moved(pos, order[phase], 3)
        for slot, (h, to) in enumerate(((0, right), (1, left), (1, right), (0, left))):
            if has_half(kind, phase, h):
                index = block_index(order, phase, pos, h)
                src = unit[kind].at[j] if phase == 0 else gath[kind].at[section, j].at[index]
                ag_copy(n, phase, slot, src, index, to).start()

    def ag_pieces(n, phase, at, h):
        order = ORDERS[STREAMS[n][0]]
        if phase < 2:
            return [block_index(order, phase, at, h)]
        return [block_index(order, phase, at, h, q) for q in range(2)]

    def to_sibling(n, index):
        j, kind = STREAMS[n]
        ref = gath[kind].at[section, j].at[index]
        remote(ref, ref, s_sib.at[n], r_sib.at[n], sibling).start()

    def ag_arrived(n, phase, slot, index, share):
        j, kind = STREAMS[n]
        ag_copy(n, phase, slot, gath[kind].at[section, j].at[index], index, moved(pos, 0, 1)).wait_recv()
        if share:
            to_sibling(n, index)

    def ag_forward(phase, share=False, part=ALL):
        for n in part:
            j, kind = STREAMS[n]
            order = ORDERS[j]
            right, left = moved(pos, order[phase], 1), moved(pos, order[phase], 3)
            for slot, h, source, to in ((0, 0, left, right), (1, 1, right, left)):
                if has_half(kind, phase, h):
                    ag_arrived(n, phase, slot, block_index(order, phase, source, h), share)
                    for q, index in enumerate(ag_pieces(n, phase, source, h)):
                        ag_copy(n, phase, 4 + 2 * slot + q, gath[kind].at[section, j].at[index], index, to).start()

    def ag_rest(phase, share=False, part=ALL):
        for n in part:
            j, kind = STREAMS[n]
            order = ORDERS[j]
            right, left = moved(pos, order[phase], 1), moved(pos, order[phase], 3)
            for slot, h, source in ((2, 1, left), (3, 0, right)):
                if has_half(kind, phase, h):
                    ag_arrived(n, phase, slot, block_index(order, phase, source, h), share)
        for q in range(2 if phase == 2 else 1):
            for n in part:
                j, kind = STREAMS[n]
                far = moved(pos, ORDERS[j][phase], 2)
                for slot in (0, 1):
                    if has_half(kind, phase, slot):
                        ag_arrived(n, phase, 4 + 2 * slot + q, ag_pieces(n, phase, far, slot)[q], share)

    def ag_sent(phase):
        for n, (j, kind) in enumerate(STREAMS):
            index = {0: (0, 0, pl.ds(0, 3)), 1: (0, pl.ds(0, 3)), 2: (pl.ds(0, 3),)}[phase]
            ref = gath[kind].at[section, j].at[index]
            remote(ref, ref, s_ag.at[n, phase], r_ag.at[n, phase, 0], sibling).wait_send()

    def small_gather(phase):
        axis = (2, 1, 0)[phase]
        index = tuple(pos[: 3 - phase])
        sent = []
        for by in (1, 2, 3):
            ref = gs.at[section].at[index]
            c = remote(ref, ref, s_small.at[phase, by - 1], r_small.at[phase, by - 1], device(moved(pos, axis, by)))
            c.start()
            sent.append(c)
        return sent

    trailing = jnp.logical_not(leading)
    cotangent_0 = misc(2, ends.at[0], swapped, sibling)
    small_across = misc(3, gs.at[section], gs.at[section], sibling)

    def prologue(wsend, esend, uw, uo, ue, us):
        unit = (uw, uo, ue)
        bc = win[:, 2 * DI : 2 * DI + 2 * N].astype(F32)
        rz = jnp.concatenate([win[:, 2 * DI + 2 * N :].astype(F32), jnp.zeros((24, 2 * N - H), F32)], axis=1)
        for j in range(3):
            for i, at in enumerate(group_columns(2 * j + 1 - parity)):
                wsend[j, :, 512 * i : 512 * i + 512] = win[:, at]
        esend[...] = jnp.where(even, rz, bc).astype(BF)
        us[...] = jnp.zeros((8, 128), F32)
        us[0:4, 0:52] = taps_in[...].astype(F32)
        us[4:5, 0:52] = bias_in[...].astype(F32)
        us[5:6, 0:24] = pre_in[...].astype(F32)
        us[6:7, 0:48] = gate_in[...].astype(F32)
        us[7:8, 0:48] = dtb_in[...].astype(F32)
        us[5:6, 64:112] = alog_in[...].astype(F32)
        us[6:7, 64:112] = skip_in[...].astype(F32)
        gs[section, pos[0], pos[1], pos[2]] = us[...]
        for j in range(3):
            uo[j] = wout[:, 512 * j : 512 * j + 512]

        pl.semaphore_wait(barrier, 10)
        swap_w = misc(0, wsend, wgot, device(partner))
        swap_e = misc(1, esend, egot, device(partner))
        swap_w.start()
        swap_e.start()

        @pl.when(trailing)
        def _():
            cotangent_0.start()


        def first_phase(part):
            copies = []
            for n in part:
                j, kind = STREAMS[n]
                ag_start(n, 0, unit)
                c = pltpu.make_async_copy(unit[kind].at[j], gath[kind].at[section, j].at[pos], own_sem.at[n])
                c.start()
                copies.append(c)
            return copies

        small = small_gather(0)
        own = first_phase(OUT)
        swap_w.wait()
        swap_e.wait()
        for j in range(3):
            for i, at in enumerate(group_columns(2 * j + parity)):
                lanes = slice(512 * i, 512 * i + 512)
                mine, theirs = win[:, at].astype(F32), wgot[j, :, lanes].astype(F32)
                uw[j, :, lanes] = jnp.concatenate([jnp.where(even, mine, theirs), jnp.where(even, theirs, mine)], axis=0).astype(BF)
        mine, theirs = jnp.where(even, bc, rz), egot[...].astype(F32)
        both = jnp.concatenate([jnp.where(even, mine, theirs), jnp.where(even, theirs, mine)], axis=0).astype(BF)
        for j in range(3):
            ue[j] = both[16 * j : 16 * j + 16, :]
        own_rest = first_phase(REST)
        for c in small:
            c.wait()
        small = small_gather(1)
        ag_forward(0, part=OUT)
        for c in own:
            c.wait()
        ag_rest(0, part=OUT)
        for n in OUT:
            ag_start(n, 1)
        ag_forward(0, part=REST)
        for c in small:
            c.wait()
        small = small_gather(2)
        for c in own_rest:
            c.wait()
        ag_rest(0, part=REST)

        @pl.when(leading)
        def _():
            for n in REST:
                ag_start(n, 1)

        for c in small:
            c.wait()
        small_across.start()
        ag_forward(1, part=OUT)
        ag_rest(1, part=OUT)

        @pl.when(leading)
        def _():
            for n in OUT:
                ag_start(n, 2)

        ag_sent(0)

    pl.run_scoped(
        prologue,
        pltpu.VMEM((3, 24, 1024), BF), pltpu.VMEM((24, 256), BF), pltpu.VMEM((3, 48, 1024), BF), pltpu.VMEM((3, 48, 512), BF), pltpu.VMEM((3, 16, 256), BF), pltpu.VMEM((8, 128), F32),
    )

    def own_across():
        for n, (j, kind) in enumerate(STREAMS):
            to_sibling(n, block_index(ORDERS[j], 2, pos, None))

    misc(3, gs.at[1 - section], gs.at[1 - section], sibling).wait()
    for l in range(2):
        hp[l] = gs[l, 0, 0, 0]
        for i in range(64):
            tile = gs.at[l, i // 16, i // 4 % 4, i % 4]
            par[l, 0:5, 52 * i : 52 * i + 52] = tile[0:5, 0:52]
            par[l, 7:8, 24 * i : 24 * i + 24] = tile[5:6, 0:24]
            par[l, 5:6, 48 * i : 48 * i + 48] = tile[6:7, 0:48]
    def from_sibling(n):
        j, kind = STREAMS[n]
        ref = gath[kind].at[1, j]
        remote(ref, ref, s_sib.at[n], r_sib.at[n], sibling).wait_recv()

    @pl.when(leading)
    def _():
        ag_forward(1, part=REST)
        ag_rest(1, part=REST)
        for n in REST:
            ag_start(n, 2)
        ag_forward(2)
        pl.semaphore_signal(go_sem, inc=1, device_id=sibling, device_id_type=MESH)
        ag_rest(2)

    @pl.when(trailing)
    def _():
        for n in REST:
            ag_start(n, 1)
        ag_forward(1, part=REST)
        ag_rest(1, part=REST)
        own_across()
        pl.semaphore_wait(go_sem, 1)
        for n in ALL:
            ag_start(n, 2)

    landing = {}

    def rs_copy(n, phase, slot, src, to):
        j, kind = STREAMS[n]
        if phase == 2 and slot >= 4:
            dst = landing[2, kind].at[j, slot - 4]
        elif phase == 2:
            dst = recv2[kind].at[j, slot]
        else:
            dst = landing[phase, kind].at[j, slot if phase == 1 else slot // 2]
        return remote(src, dst, s_rs.at[n, phase], r_rs.at[n, phase, slot], device(to))

    def rs_start(n, phase, part):
        j, kind = STREAMS[n]
        axis = ORDERS[j][phase]
        right, left, far = (moved(pos, axis, by) for by in (1, 3, 2))
        for slot, at, h, to in ((0, far, 0, left), (1, far, 1, right), (2, left, 1, left), (3, right, 0, right)):
            if has_half(kind, phase, h):
                rs_copy(n, phase, slot, part(n, at[axis], h), to).start()

    def grad_part(n, k, h):
        j, kind = STREAMS[n]
        at = list(pos)
        at[ORDERS[j][2]] = k
        return grad[kind].at[(j,) + block_index(ORDERS[j], 2, tuple(at), h)]

    def term(n, src, dst):
        return remote(src, dst, s_terms.at[n], r_terms.at[n], sibling)

    def dterm(g):
        return term(3 + g, dps.at[12 + lax.rem(g, 2)], dps.at[6 + g])

    def layers(wbuf, ebuf, obuf, zbuf, xbuf, ybuf, tbuf, pebuf, masks, coef, allowed, tri, sel, qcol, qrow, dtrow, heads, smat, gbuf, dgacc, rowq, rowx, acc, rbuf, ut, ot, wsem, esem, osem, gsem, psem):
        def copy_w(l, g):
            j, p = lax.div(g, 2), lax.rem(g, 2)
            return [pltpu.make_async_copy(gath[0].at[l, j, :, :, 2 * m + p], wbuf.at[g, :, :, pl.ds(48 * m, 48)], wsem.at[g, m]) for m in range(2)]

        def copy_e(l):
            return [pltpu.make_async_copy(gath[2].at[l, j, :, :, 2 * m + p], ebuf.at[p, :, :, m, j], esem.at[p, m, j]) for p in range(2) for m in range(2) for j in range(3)]

        def copy_o(l, j):
            return [pltpu.make_async_copy(gath[1].at[l, j], obuf.at[j], osem.at[j])]

        def start(copies):
            for c in copies:
                c.start()

        def finish(copies):
            for c in copies:
                c.wait()

        def weights_e(p):
            return ebuf[p].reshape(D, 256)

        def start_all(l):
            start(copy_e(l))
            for g in range(GROUPS):
                start(copy_w(l, jnp.int32(g)))
            for j in range(3):
                start(copy_o(l, j))

        @pl.when(leading)
        def _():
            start_all(0)

        rows = lax.broadcasted_iota(jnp.int32, (T, T), 0)
        cols = lax.broadcasted_iota(jnp.int32, (T, T), 1)
        def set_block(b):
            seg = jnp.where(b == 0, segs[0:1, :], segs[1:2, :]).astype(F32)
            seg_s = jnp.broadcast_to(seg, (T, T))
            seg_t = jnp.transpose(seg_s)
            allowed[...] = jnp.where(rows >= cols, jnp.where(seg_t == seg_s, 1.0, 0.0), 0.0)
            for d in (1, 2, 3):
                masks[d - 1] = jnp.where(rows >= d, jnp.where(pltpu.roll(seg_t, d, 0) == seg_t, 1.0, 0.0), 0.0)
            masks[3] = jnp.where(rows < counts[b], 1.0, 0.0)

        tri[...] = jnp.where(rows >= cols, 1.0, 0.0).astype(BF)
        srow = lax.broadcasted_iota(jnp.int32, (512, T), 0)
        scol = lax.broadcasted_iota(jnp.int32, (512, T), 1)
        sel[...] = jnp.where(lax.div(srow, 64) == scol, 1.0, 0.0).astype(BF)
        low_lanes = cols < 64
        for l in range(2):
            skips = hp[l, 6:7, 64:112]
            skips = jnp.concatenate([skips, jnp.zeros((1, 80), F32)], axis=1)
            skips = jnp.broadcast_to(skips, (8, T))
            for g in range(GROUPS):
                mine = skips if g == 0 else pltpu.roll(skips, T - 8 * g, 1)
                mine = jnp.where(cols[0:8] < 8, mine, 0.0)
                par[l, 6:7, 512 * g : 512 * g + 512] = dot(mine.astype(BF), sel[...], ((1,), (1,)))[0:1]

        def conv(px, taps, bias):
            s1 = pltpu.roll(px, 1, 0) * masks[0]
            s2 = pltpu.roll(px, 2, 0) * masks[1]
            s3 = pltpu.roll(px, 3, 0) * masks[2]
            c = bias + taps[3:4] * px + taps[2:3] * s1 + taps[1:2] * s2 + taps[0:1] * s3
            return c, (s3, s2, s1, px)

        def conv_back(dc, taps):
            out = taps[3:4] * dc
            out = out + taps[2:3] * pltpu.roll(dc * masks[0], T - 1, 0)
            out = out + taps[1:2] * pltpu.roll(dc * masks[1], T - 2, 0)
            return out + taps[0:1] * pltpu.roll(dc * masks[2], T - 3, 0)

        def decay(g, hh):
            gap = jnp.broadcast_to(qcol[g][:, hh : hh + 1], (T, T)) - qrow[g][hh : hh + 1, :]
            return jnp.exp2(jnp.minimum(gap, 0.0)) * dtrow[g][hh : hh + 1, :]

        def rate_bias(l):
            return hp[l, 7:8, :]

        def rate(l):
            tile = pltpu.roll(hp[l], 64, 1)
            return -jnp.exp(jnp.where(cols[0:1] < H, tile[5:6, :], 0.0))

        def tile_at(g, k):
            return pl.ds(pl.multiple_of(512 * g + 128 * k, 128), 128)

        def prepare(s):
            q = heads[s, 1]
            qt = jnp.transpose(q)
            dtt = jnp.transpose(heads[s, 0])
            for g in range(GROUPS):
                qcol[g] = q if g == 0 else pltpu.roll(q, T - 8 * g, 1)
                qrow[g] = qt[8 * g : 8 * g + 8, :]
                dtrow[g] = dtt[8 * g : 8 * g + 8, :]

        def when_first(first, fn):
            if first is True:
                fn()
            else:
                pl.when(first)(fn)

        def forward(l, h, s, z, b, sl, first):
            set_block(b)
            rs = lax.rsqrt(jnp.sum(h * h, axis=1, keepdims=True) * (1.0 / D) + EPSILON)
            rbuf[s, 0] = jnp.broadcast_to(rs, (T, T))
            us_[sl] = (h * rs * par[l, 7:8, 0:D] * masks[3][:, 0:1]).astype(BF)
            when_first(first, lambda: finish(copy_e(l)))
            pebuf[s, :, 0:256] = dot(us_[sl], weights_e(0))
            pebuf[s, :, 256:384] = dot(us_[sl], weights_e(1))[:, 0:128]
            for j in range(2):
                at = slice(DI + 128 * j, DI + 128 * j + 128)
                c, _ = conv(pebuf[s, :, 128 * j : 128 * j + 128], par[l, 0:4, at], par[l, 4:5, at])
                smat[s, j] = (c * sigmoid(c)).astype(BF)
            v = pebuf[s, :, 256:384] + rate_bias(l)
            dt = jnp.maximum(v, 0.0) + jnp.log1p(jnp.exp(-jnp.abs(v)))
            heads[s, 0] = dt
            heads[s, 1] = exact_dot(tri[...], dt * rate(l)) * LOG2E
            gbuf[s] = dot(smat[s, 1], smat[s, 0], ((1,), (1,))) * allowed[...]
            prepare(s)
            acc[:, 0:128] = jnp.zeros((T, T), F32)

            def group(g, carry):
                when_first(first, lambda: finish(copy_w(l, g)))
                wide = pl.ds(pl.multiple_of(512 * g, 128), 512)
                zbuf[z, :, wide] = dot(us_[sl], wbuf[g, :, :, :, 0:512].reshape(D, 512))
                xbuf[z, :, wide] = dot(us_[sl], wbuf[g, :, :, :, 512:1024].reshape(D, 512))
                for k in range(4):
                    at = tile_at(g, k)
                    c, _ = conv(xbuf[z, :, at], par[l, 0:4, at], par[l, 4:5, at])
                    x = c * sigmoid(c)
                    xb = x.astype(BF)
                    both = jnp.concatenate([keep_lanes(xb, low_lanes), keep_lanes(xb, ~low_lanes)], axis=0)
                    w = jnp.concatenate([(gbuf[s] * decay(g, 2 * k + i)).astype(BF) for i in range(2)], axis=1)
                    y = dot(w, both) + par[l, 6:7, at] * x
                    ybuf[z, :, at] = y
                    zz_ = zbuf[z, :, at]
                    e = y * (zz_ * sigmoid(zz_))
                    tbuf[:, at] = e
                    acc[:, 0:128] += e * e
                return carry

            lax.fori_loop(0, GROUPS, group, 0)
            r = lax.rsqrt(jnp.sum(acc[:, 0:128], axis=1, keepdims=True) * (1.0 / DI) + EPSILON)
            rbuf[s, 1] = jnp.broadcast_to(r, (T, T))
            for g in range(GROUPS):
                at = slice(512 * g, 512 * g + 512)
                os_[sl, :, at] = (tbuf[:, at] * r * par[l, 5:6, at]).astype(BF)
            for j in range(3):
                when_first(first, lambda j=j: finish(copy_o(l, j)))
                acc[:, 512 * j : 512 * j + 512] = dot(os_[sl], obuf[j].reshape(DI, 512))
            return h + acc[...]

        def backward(l, h, dh, s, z, b, sl, gi, first):
            set_block(b)
            if l == 1:
                dvs[sl] = dh.astype(BF)

            if l == 1:
                @pl.when(leading)
                def _():
                    for n, ref in enumerate((us_, os_, dvs)):
                        term(n, ref.at[2], ref.at[1]).start()
            else:
                when_first(first, lambda: [finish(copy_o(0, j)) for j in range(3)] and None)
            acc[:, 0:128] = jnp.zeros((T, T), F32)

            def gated_back(zz, carry):
                wide = pl.ds(pl.multiple_of(768 * zz, 128), 768)
                do = None
                for j in range(3):
                    part = dot(dvs[sl, :, 512 * j : 512 * j + 512], obuf[j, zz].reshape(768, 512), ((1,), (1,)))
                    do = part if do is None else do + part
                tbuf[:, wide] = do
                for k in range(6):
                    at = pl.ds(pl.multiple_of(768 * zz + 128 * k, 128), 128)
                    zz_ = zbuf[z, :, at]
                    e = ybuf[z, :, at] * (zz_ * sigmoid(zz_))
                    prod = tbuf[:, at] * e
                    gr[gi, 5:6, at] = total(prod * rbuf[s, 1])
                    acc[:, 0:128] += prod * par[l, 5:6, at]
                return carry

            lax.fori_loop(0, 4, gated_back, 0)
            if l == 1:
                @pl.when(leading)
                def _():
                    for j in range(3):
                        start(copy_o(0, j))
            r = rbuf[s, 1]
            coef[...] = jnp.broadcast_to(jnp.sum(acc[:, 0:128], axis=1, keepdims=True) * (1.0 / DI), (T, T)) * r * r * r
            prepare(s)
            dgacc[...] = jnp.zeros((T, T), F32)
            rowq[...] = jnp.zeros((T, T), F32)
            rowx[...] = jnp.zeros((T, T), F32)
            acc[...] = jnp.zeros((T, D), F32)

            def second(g, carry):
                if l == 0:
                    when_first(first, lambda: finish(copy_w(0, g)))
                    here = 6 * b + g
                else:
                    here = lax.select(leading, 12 + lax.rem(g, 2), g)

                    @pl.when(jnp.logical_and(leading, g >= 2))
                    def _():
                        dterm(g - 2).wait_send()

                sums_q, sums_x = None, None
                for k in range(4):
                    at = tile_at(g, k)
                    zz_ = zbuf[z, :, at]
                    y = ybuf[z, :, at]
                    sz = sigmoid(zz_)
                    silu = zz_ * sz
                    de = rbuf[s, 1] * (tbuf[:, at] * par[l, 5:6, at]) - (y * silu) * coef[...]
                    dyb = (de * silu).astype(BF)
                    dz = de * y * (sz + silu * (1.0 - sz))
                    dps[here, :, 128 * k : 128 * k + 128] = dz.astype(BF)
                    taps = par[l, 0:4, at]
                    c, shifts = conv(xbuf[z, :, at], taps, par[l, 4:5, at])
                    sc = sigmoid(c)
                    x = c * sc
                    xb = x.astype(BF)
                    dyw = dyb.astype(F32)
                    skip = par[l, 6:7, at]
                    xt = jnp.concatenate([keep_lanes(xb, low_lanes), keep_lanes(xb, ~low_lanes)], axis=0)
                    dyt = jnp.concatenate([keep_lanes(dyb, low_lanes), keep_lanes(dyb, ~low_lanes)], axis=0)
                    dw = dot(dyb, xt, ((1,), (1,)))
                    ws, dg = [], None
                    for i in range(2):
                        e = decay(g, 2 * k + i)
                        ws.append((gbuf[s] * e).astype(BF))
                        part = dw[:, 128 * i : 128 * i + 128] * e
                        dg = part if dg is None else dg + part
                    dgacc[...] += dg
                    dx0 = dot(jnp.concatenate(ws, axis=0), dyt, ((0,), (0,)))
                    dx = dx0 + skip * dyw
                    gr[gi, 6:7, at] = total(dyw * x)
                    one = sel[128 * k : 128 * k + 128, :]
                    part = exact_dot(one, dyw * (y - skip * x), flip=True, terms=2)
                    sums_q = part if sums_q is None else sums_q + part
                    part = exact_dot(one, xb.astype(F32) * dx0, flip=True, terms=2)
                    sums_x = part if sums_x is None else sums_x + part
                    dc = dx * (sc + x * (1.0 - sc))
                    for t in range(4):
                        gr[gi, t : t + 1, at] = total(dc * shifts[t])
                    gr[gi, 4:5, at] = total(dc)
                    dps[here, :, 512 + 128 * k : 640 + 128 * k] = conv_back(dc, taps).astype(BF)
                rowq[...] += pltpu.roll(sums_q, 8 * g, 1)
                rowx[...] += pltpu.roll(sums_x, 8 * g, 1)

                if l == 1:
                    @pl.when(leading)
                    def _():
                        dterm(g).start()

                for zz in range(4):
                    acc[:, 384 * zz : 384 * zz + 384] += dot(dps[here], wbuf[g, zz].reshape(384, 1024), ((1,), (1,)))
                if l == 1:
                    @pl.when(leading)
                    def _():
                        start(copy_w(0, g))
                return carry

            lax.fori_loop(0, GROUPS, second, 0)
            dg = (dgacc[...] * allowed[...]).astype(BF)
            d_states = (dot(dg, smat[s, 1], ((0,), (0,))), dot(dg, smat[s, 0]))
            for j in range(2):
                at = slice(DI + 128 * j, DI + 128 * j + 128)
                taps = par[l, 0:4, at]
                c, shifts = conv(pebuf[s, :, 128 * j : 128 * j + 128], taps, par[l, 4:5, at])
                sc = sigmoid(c)
                dc = d_states[j] * (sc + c * sc * (1.0 - sc))
                for t in range(4):
                    gr[gi, t : t + 1, at] = total(dc * shifts[t])
                gr[gi, 4:5, at] = total(dc)
                dpes[sl, 0, :, 128 * j : 128 * j + 128] = conv_back(dc, taps).astype(BF)
            v = pebuf[s, :, 256:384] + rate_bias(l)
            sv = 1.0 / (1.0 + jnp.exp(-v))
            dt = heads[s, 0]
            back = exact_dot(tri[...], rowq[...] - rowx[...], ((0,), (0,)))
            ratio = jnp.where(v < -15.0, 1.0, sv / jnp.maximum(dt, 1e-30))
            dr = jnp.where(cols < H, rowx[...] * ratio + back * rate(l) * sv, 0.0)
            d_rate = total(jnp.where(cols < H, back * dt, 0.0)) * rate(l)
            dpes[sl, 1, :, 0:128] = dr.astype(BF)
            dpes[sl, 1, :, 128:256] = jnp.zeros((T, T), BF)

            if l == 1:
                @pl.when(leading)
                def _():
                    term(9, dpes.at[2], dpes.at[1]).start()
            else:
                when_first(first, lambda: finish(copy_e(0)))
            du = acc[...]
            for p in range(2):
                du = du + dot(dpes[sl, p], weights_e(p), ((1,), (1,)))
            if l == 1:
                @pl.when(leading)
                def _():
                    start(copy_e(0))

            hn = h * rbuf[s, 0][:, 0:1]
            du = du * masks[3][:, 0:1]
            gr[gi, 7:8, 0:D] = total(du * hn)
            t = du * par[l, 7:8, 0:D]
            mean = jnp.sum(t * hn, axis=1, keepdims=True) * (1.0 / D)
            dh_in = dh + rbuf[s, 0][:, 0:1] * (t - hn * mean)
            hg[gi, 0:1] = total(dr)
            hg[gi, 1:2] = d_rate
            return dh_in

        def small_tiles(l):
            skips = jnp.zeros((8, T), F32)
            for g in range(GROUPS):
                mine = exact_dot(sel[...], jnp.broadcast_to(gr[0, 6:7, 512 * g : 512 * g + 512], (8, 512)), flip=True)
                skips = skips + (mine if g == 0 else pltpu.roll(mine, 8 * g, 1))
            for i in range(64):
                tile = gs.at[l, i // 16, i // 4 % 4, i % 4]
                tile[0:5, 0:52] = gr[0, 0:5, 52 * i : 52 * i + 52]
                tile[5:6, 0:24] = gr[0, 7:8, 24 * i : 24 * i + 24]
                tile[6:7, 0:48] = gr[0, 5:6, 48 * i : 48 * i + 48]
                tile[7:8, 0:128] = hg[0, 0:1]
                tile[5:6, 64:112] = hg[0, 1:2, 0:48]
                tile[6:7, 64:112] = skips[0:1, 0:48]

        def products(l):
            if l == 1:
                for n, ref in enumerate((us_, os_, dvs)):
                    term(n, ref.at[2], ref.at[1]).wait_recv()
                for g in range(GROUPS):
                    dterm(g).wait_recv()
                term(9, dpes.at[2], dpes.at[1]).wait_recv()

            def stacked(ref, *index):
                return jnp.concatenate([ref[(0,) + index], ref[(1,) + index]], axis=0)

            def turn(i, carry):
                at = pl.ds(pl.multiple_of(128 * i, 128), 128)
                ut[at, :] = jnp.transpose(stacked(us_, slice(None), at))
                return carry

            lax.fori_loop(0, D // 128, turn, 0)

            for p in range(2):
                for zz in range(4):
                    de = dot(ut[384 * zz : 384 * zz + 384, :], stacked(dpes, p))
                    ebuf[p, zz] = de.astype(BF).reshape(4, 2, 3, 16, 256)
            for p in range(2):
                for m in range(2):
                    for j in range(3):
                        pltpu.make_async_copy(ebuf.at[p, :, :, m, j], grad[2].at[j, :, :, 2 * m + p], gsem.at[j, 2]).start()

            def wstep(i, carry):
                g, zz = lax.div(i, 4), lax.rem(i, 4)
                u = ut[pl.ds(pl.multiple_of(384 * zz, 128), 384), :]
                for half in range(2):
                    at = slice(512 * half, 512 * half + 512)
                    d = jnp.concatenate([dps[g, :, at], dps[6 + g, :, at]], axis=0)
                    wbuf[g, zz, :, :, at] = dot(u, d).astype(BF).reshape(4, 96, 512)
                j, p = lax.div(g, 2), lax.rem(g, 2)
                for m in range(2):
                    pltpu.make_async_copy(wbuf.at[g, zz, :, pl.ds(48 * m, 48)], grad[0].at[j, zz, :, 2 * m + p], gsem.at[j, 0]).start()
                return carry

            def ostep(zz, carry):
                for i in range(6):
                    at = pl.ds(pl.multiple_of(768 * zz + 128 * i, 128), 128)
                    ot[128 * i : 128 * i + 128, :] = jnp.transpose(stacked(os_, slice(None), at))
                for j in range(3):
                    d = stacked(dvs, slice(None), slice(512 * j, 512 * j + 512))
                    for half in range(2):
                        o = ot[384 * half : 384 * half + 384, :]
                        obuf[j, zz, 2 * half : 2 * half + 2] = dot(o, d).astype(BF).reshape(2, 4, 48, 512)
                    pltpu.make_async_copy(obuf.at[j, zz], grad[1].at[j, zz], gsem.at[j, 1]).start()
                return carry

            def written(j, kind):
                pltpu.make_async_copy(grad[kind].at[j], grad[kind].at[j], gsem.at[j, kind]).wait()
                rs_start(3 * j + kind, 2, grad_part)

            for j in range(3):
                lax.fori_loop(8 * j, 8 * j + 8, wstep, 0)
                if j > 0:
                    written(j - 1, 0)
            lax.fori_loop(0, 4, ostep, 0)
            written(2, 0)
            for kind in (1, 2):
                for j in range(3):
                    written(j, kind)

        middle_1 = misc(7, dvs.at[0], hbuf, sibling)
        out_0 = misc(4, ends_out.at[0], ends_out.at[0], sibling)
        d_middle_1 = misc(8, dvs.at[2], dvs.at[1], sibling)
        sets = [pltpu.make_async_copy(ref.at[0], spill.at[n], psem.at[n]) for n, ref in enumerate((zbuf, xbuf, ybuf))]
        sets_back = [pltpu.make_async_copy(spill.at[n], ref.at[0], psem.at[n]) for n, ref in enumerate((zbuf, xbuf, ybuf))]

        @pl.when(leading)
        def _():
            def block(b, carry):
                out = forward(0, ends[b].astype(F32), b, b, b, b, b == 0).astype(BF)

                @pl.when(b == 0)
                def _():
                    hbuf[...] = out
                    start(sets)

                @pl.when(b == 1)
                def _():
                    dvs[0] = out
                    middle_1.start()

                return carry

            lax.fori_loop(0, 2, block, 0)
            finish(sets)
            cotangent_0.wait_recv()
            for n in range(9):
                j, kind = STREAMS[n]
                from_sibling(n)
                if kind == 0:
                    start(copy_w(1, jnp.int32(2 * j)))
                    start(copy_w(1, jnp.int32(2 * j + 1)))
                elif kind == 1:
                    start(copy_o(1, j))
            start(copy_e(1))

        @pl.when(trailing)
        def _():
            ag_forward(2, True)
            ag_rest(2, True)
            start_all(1)
            cotangent_0.wait_send()
            middle_1.wait_recv()

        out = forward(1, hbuf[...].astype(F32), 2, 0, section, lax.select(leading, 2, 0), True).astype(BF)

        @pl.when(leading)
        def _():
            ends_out[0] = out
            out_0.start()

        @pl.when(trailing)
        def _():
            ends_out[1] = out

        cotangent = jnp.where(leading, swapped[...].astype(F32), ends[1].astype(F32))
        d_middle = backward(1, hbuf[...].astype(F32), cotangent, 2, 0, section, lax.select(leading, 2, 0), 0, True).astype(BF)

        @pl.when(trailing)
        def _():
            dvs[2] = d_middle
            d_middle_1.start()
            small_tiles(1)
            products(1)
            d_middle_1.wait_send()
            out_0.wait_recv()

        @pl.when(leading)
        def _():
            start(sets_back)
            middle_1.wait_send()
            dvs[0] = d_middle
            small_tiles(1)
            term(10, gs.at[1], gs.at[0]).start()
            out_0.wait_send()
            d_middle_1.wait_recv()

            def block(i, carry):
                b = 1 - i

                @pl.when(i == 1)
                def _():
                    finish(sets_back)

                ends_out[b] = backward(0, ends[b].astype(F32), dvs[b].astype(F32), b, b, b, b, i, i == 0).astype(BF)
                return carry

            lax.fori_loop(0, 2, block, 0)
            gr[0] += gr[1]
            hg[0] += hg[1]
            small_tiles(0)
            products(0)

    V = pltpu.VMEM
    pl.run_scoped(
        layers,
        V((6, 4, 4, 96, 1024), BF), V((2, 4, 4, 2, 3, 16, 256), BF), V((3, 4, 4, 4, 48, 512), BF),
        V((2, T, DI), F32), V((2, T, DI), F32), V((2, T, DI), F32), V((T, DI), F32), V((3, T, 384), F32),
        V((4, T, T), F32), V((T, T), F32), V((T, T), F32), V((T, T), BF), V((512, T), BF), V((6, T, T), F32), V((6, 8, T), F32), V((6, 8, T), F32),
        V((3, 2, T, T), F32), V((3, 2, T, T), BF), V((3, T, T), F32), V((T, T), F32), V((T, T), F32), V((T, T), F32), V((T, D), F32), V((3, 2, T, T), F32),
        V((D, 256), BF), V((768, 256), BF),
        pltpu.SemaphoreType.DMA((6, 2)), pltpu.SemaphoreType.DMA((2, 2, 3)), pltpu.SemaphoreType.DMA((3,)), pltpu.SemaphoreType.DMA((3, 3)), pltpu.SemaphoreType.DMA((3,)),
    )

    def sums(*bufs):
        it = iter(bufs)
        take = lambda n: [next(it) for _ in range(n)]
        ab, ob, db, eb, acc2, acc1, b1, b0, fin = (take(3) for _ in range(9))
        fsend, gsend, fgot, ggot, sa2, sa1, lsem = it
        for kind in range(3):
            landing[2, kind], landing[1, kind], landing[0, kind] = eb[kind], b1[kind], b0[kind]
        for axis in range(3):
            for by in (1, 3):
                pl.semaphore_signal(ready_sem, inc=1, device_id=device(moved(pos, axis, by)), device_id_type=MESH)

        def load(n, h, which, src, dst):
            return pltpu.make_async_copy(src, dst, lsem.at[n, h, which])

        def add(dst, parts, dims, dtype, place=None):
            if not dims:
                out = parts[0][...].astype(F32)
                for p in parts[1:]:
                    out = out + p[...].astype(F32)
                dst[...] = out.astype(dtype)
                return
            count = dims[0] * (dims[1] if len(dims) > 1 else 1)

            def one(i, carry):
                index = (i,) if len(dims) == 1 else (lax.div(i, dims[1]), lax.rem(i, dims[1]))
                out = parts[0][index].astype(F32)
                for p in parts[1:]:
                    out = out + p[index].astype(F32)
                dst[index if place is None else place(*index)] = out.astype(dtype)
                return carry

            lax.fori_loop(0, count, one, 0)

        def neighbours(n, phase):
            axis = ORDERS[STREAMS[n][0]][phase]
            right, left = moved(pos, axis, 1), moved(pos, axis, 3)
            return pos[axis], {0: (0, left[axis], left, 4, 3), 1: (1, right[axis], right, 5, 2)}

        def sent(phase):
            for n, (j, kind) in enumerate(STREAMS):
                if phase == 2:
                    ref = grad[kind].at[j, pl.ds(0, 3)]
                else:
                    ref = landing[phase, kind].at[j, pl.ds(0, 3 if phase == 0 else 6)]
                remote(ref, ref, s_rs.at[n, phase], r_rs.at[n, phase, 0], sibling).wait_send()

        items = {phase: [(3 * j + kind, h) for kind in range(3) for j in range(3) for h in (0, 1) if has_half(kind, phase, h)] for phase in range(3)}


        def small_start(phase):
            axis = ORDERS[0][phase]
            cur = (sa1, sa2, gs.at[section])[phase]
            got = (sg0, sg1, sg2)[phase]
            copies = []
            for by in (1, 2, 3):
                to = moved(pos, axis, by)
                c = remote(cur.at[to[axis]], got.at[by - 1], s_small.at[3 + phase, by - 1], r_small.at[3 + phase, by - 1], device(to))
                c.start()
                copies.append(c)

            def done():
                for c in copies:
                    c.wait()
                out = cur[pos[axis]] + got[0] + got[1] + got[2]
                if phase == 0:
                    return out
                (sa1, sa2)[phase - 1][...] = out
                return None

            return done

        @pl.when(trailing)
        def _():
            term(10, gs.at[1], gs.at[0]).wait_recv()
            gs[1] += gs[0]

        for n, h in items[2]:
            j, kind = STREAMS[n]
            _, halves = neighbours(n, 2)
            load(n, h, 0, grad_part(n, halves[h][1], h), ob[kind].at[j, h]).start()
        for n, h in items[2]:
            j, kind = STREAMS[n]
            slot = neighbours(n, 2)[1][h][0]
            rs_copy(n, 2, slot, ab[kind].at[j, h], moved(pos, 0, 1)).wait_recv()
            load(n, h, 1, recv2[kind].at[j, slot], ab[kind].at[j, h]).start()
        pl.semaphore_wait(ready_sem, 6)
        done = small_start(2)
        for n, h in items[2]:
            j, kind = STREAMS[n]
            here, halves = neighbours(n, 2)
            _, block, to, slot, _ = halves[h]
            load(n, h, 0, grad_part(n, block, h), ob[kind].at[j, h]).wait()
            load(n, h, 1, recv2[kind].at[j, 0], ab[kind].at[j, h]).wait()
            add(ab[kind].at[j, h], [ab[kind].at[j, h], ob[kind].at[j, h]], (2, 4), BF)
            rs_copy(n, 2, slot, ab[kind].at[j, h], to).start()
            load(n, h, 0, grad_part(n, here, h), ob[kind].at[j, h]).start()
        done()
        for n, h in items[2]:
            j, kind = STREAMS[n]
            slot = neighbours(n, 2)[1][h][4]
            rs_copy(n, 2, slot, ab[kind].at[j, h], moved(pos, 0, 1)).wait_recv()
            load(n, h, 2, recv2[kind].at[j, slot], db[kind].at[j, h]).start()

        def last2(n, h):
            j, kind = STREAMS[n]
            order = ORDERS[j]
            low = min(order[:2])
            load(n, h, 0, grad_part(n, 0, h), ob[kind].at[j, h]).wait()
            load(n, h, 2, recv2[kind].at[j, 0], db[kind].at[j, h]).wait()
            place = (lambda a, b: (j, 2 * h + a, b)) if order[1] == low else (lambda a, b: (j, b, 2 * h + a))
            add(acc2[kind], [ob[kind].at[j, h], db[kind].at[j, h], eb[kind].at[j, h]], (2, 4), BF, place)

        def part_of(phase):
            def part(n, k, h):
                j, kind = STREAMS[n]
                return acc2[kind].at[j, k, pl.ds(2 * h, 2)] if phase == 1 else acc1[kind].at[j, k]

            return part

        def arrived(n, phase, slot):
            j, kind = STREAMS[n]
            ref = landing[phase, kind].at[j, {2: slot - 4, 1: slot, 0: slot // 2}[phase]]
            rs_copy(n, phase, slot, ref, moved(pos, 0, 1)).wait_recv()
            return ref

        def phase_2_last(kind):
            for n, h in items[2]:
                if STREAMS[n][1] == kind:
                    arrived(n, 2, neighbours(n, 2)[1][h][3])
                    last2(n, h)
                    if h == 1:
                        rs_start(n, 1, part_of(1))

        def first(phase, kind):
            for n, h in items[phase]:
                if STREAMS[n][1] == kind:
                    slot, block, to, summed, _ = neighbours(n, phase)[1][h]
                    ref = arrived(n, phase, slot)
                    add(ref, [ref, part_of(phase)(n, block, h)], (2,) if phase == 1 else (), BF)
                    rs_copy(n, phase, summed, ref, to).start()

        def last(phase, kind):
            for n, h in items[phase]:
                j, own_kind = STREAMS[n]
                if own_kind == kind:
                    here, halves = neighbours(n, phase)
                    parts = [part_of(phase)(n, here, h), arrived(n, phase, halves[h][4]), arrived(n, phase, halves[h][3])]
                    if phase == 0:
                        add(fin[kind].at[j], parts, (), F32)
                    else:
                        add(acc1[kind], parts, (2,), BF, lambda a: (j, 2 * h + a))
                        if h == 1:
                            rs_start(n, 0, part_of(0))

        phase_2_last(0)
        done = small_start(1)
        phase_2_last(1)
        first(1, 0)
        phase_2_last(2)
        first(1, 1)
        last(1, 0)
        done()
        done = small_start(0)
        first(1, 2)
        last(1, 1)
        first(0, 0)
        last(1, 2)
        first(0, 1)
        last(0, 0)
        for j in range(3):
            fsend[j] = jnp.where(even, fin[0][j, 24:48, :], fin[0][j, 0:24, :])
        swap_f = misc(5, fsend, fgot, device(partner))
        swap_f.start()
        first(0, 2)
        last(0, 1)
        last(0, 2)
        last_tile = done()

        last_e = jnp.concatenate([fin[2][j] for j in range(3)], axis=0)
        gsend[...] = jnp.where(even, last_e[24:48], last_e[0:24])
        swap_g = misc(6, gsend, ggot, device(partner))
        swap_g.start()
        for j in range(3):
            for i, at in enumerate(group_columns(2 * j + parity)):
                lanes = slice(512 * i, 512 * i + 512)
                d_win[:, at] = jnp.where(even, fin[0][j, 0:24, lanes], fin[0][j, 24:48, lanes])
            d_wout[:, 512 * j : 512 * j + 512] = fin[1][j]
        d_small[...] = last_tile
        swap_f.wait()
        swap_g.wait()
        for j in range(3):
            for i, at in enumerate(group_columns(2 * j + 1 - parity)):
                d_win[:, at] = fgot[j, :, 512 * i : 512 * i + 512]
        mine, theirs = jnp.where(even, last_e[0:24], last_e[24:48]), ggot[...]
        d_win[:, 2 * DI : 2 * DI + 2 * N] = jnp.where(even, mine, theirs)
        d_win[:, 2 * DI + 2 * N :] = jnp.where(even, theirs, mine)[:, 0:H]
        for phase in range(3):
            sent(phase)

    shapes = []
    for lead, dtype in (((3, 2, 2, 4), BF),) * 4 + (((3, 4, 4), BF), ((3, 4), BF), ((3, 6, 2), BF), ((3, 3), BF), ((3,), F32)):
        shapes += [V(lead + dims, dtype) for dims in KINDS]
    shapes += [V((3, 24, 1024), F32), V((24, 256), F32)] * 2 + [V((4, 4, 8, 128), F32), V((4, 8, 128), F32)]
    pl.run_scoped(sums, *shapes, pltpu.SemaphoreType.DMA((9, 2, 4)))

    @pl.when(trailing)
    def _():
        for n, (j, kind) in enumerate(STREAMS):
            ref = gath[kind].at[1, j]
            remote(ref, ref, s_sib.at[n], r_sib.at[n], sibling).wait_send()

    @pl.when(leading)
    def _():
        for n, ref in enumerate((us_, os_, dvs)):
            term(n, ref.at[2], ref.at[1]).wait_send()
        for g in (4, 5):
            dterm(g).wait_send()
        term(9, dpes.at[2], dpes.at[1]).wait_send()
        term(10, gs.at[1], gs.at[0]).wait_send()

    ag_sent(1)
    ag_sent(2)


def step(ends, segs, counts, win, taps, bias, pre, gate, wout, dtb, alog, skip):
    vm = pl.BlockSpec(memory_space=pltpu.VMEM)
    any_ = pl.BlockSpec(memory_space=pl.ANY)
    s = jax.ShapeDtypeStruct
    V, S = pltpu.VMEM, pltpu.SemaphoreType.DMA
    large = []
    for lead in ((2, 3, 4, 4, 4), (3, 4, 4, 4), (3, 4, 2, 4)):
        large += [s(lead + dims, BF) for dims in KINDS]
    return pl.pallas_call(
        step_kernel,
        out_shape=[
            s((2, T, D), BF), s((24, 6448), F32), s((48, D), F32), s((8, 128), F32),
        ] + large + [s((3, T, DI), F32)],
        in_specs=[vm, vm, pl.BlockSpec(memory_space=pltpu.SMEM)] + [vm] * 9,
        out_specs=[vm] * 4 + [any_] * 10,
        scratch_shapes=[
            V((3, 24, 1024), BF), V((24, 256), BF), V((2, 4, 4, 4, 8, 128), F32),
            V((2, 8, CC), F32), V((2, 8, 128), F32), V((2, 8, CC), F32), V((2, 8, 128), F32),
            V((3, 4, 4, 8, 128), F32), V((3, 4, 8, 128), F32), V((3, 8, 128), F32),
            V((T, D), BF), V((T, D), BF), V((3, T, D), BF), V((3, T, DI), BF), V((3, T, D), BF), V((14, T, 1024), BF), V((3, 2, T, 256), BF),
            S((9,)), S((9,)), S((9, 3)), S((9, 3, 8)), S((6, 3)), S((6, 3)), S((9,)), S((9,)), S((9, 3)), S((9, 3, 6)), S((11,)), S((11,)), S((9,)),
            pltpu.SemaphoreType.REGULAR, pltpu.SemaphoreType.REGULAR,
        ],
        compiler_params=pltpu.CompilerParams(collective_id=0, has_side_effects=True, vmem_limit_bytes=65280 * 1024),
        name="train_step",
    )(ends, segs, counts, win, taps, bias, pre, gate, wout, dtb, alog, skip)[:4]


def results_kernel(ends, win, wout, tile, ends_out, d_win, d_taps, d_bias, d_pre, d_gate, d_wout, d_dtb, d_alog, d_skip):
    ends_out[...] = ends[...]
    d_win[...] = win[...]
    d_wout[...] = wout[...]
    d_taps[...] = tile[0:4, 0:52]
    d_bias[...] = tile[4:5, 0:52]
    d_pre[...] = tile[5:6, 0:24]
    d_gate[...] = tile[6:7, 0:48]
    d_dtb[...] = tile[7:8, 0:48]
    d_alog[...] = tile[5:6, 64:112]
    d_skip[...] = tile[6:7, 64:112]


def results(ends, win, wout, tile):
    vm = pl.BlockSpec(memory_space=pltpu.VMEM)
    s = jax.ShapeDtypeStruct
    return pl.pallas_call(
        results_kernel,
        out_shape=[
            s((2, T, D), BF), s((24, 6448), F32), s((4, 52), F32), s((1, 52), F32), s((1, 24), F32), s((1, 48), F32), s((48, D), F32),
            s((1, H), F32), s((1, H), F32), s((1, H), F32),
        ],
        in_specs=[vm] * 4,
        out_specs=[vm] * 10,
        name="results",
    )(ends, win, wout, tile)


def body(ends_in, seg_ids, block_counts, in_weight, conv_weight, conv_bias, pre_gain, gate_gain, out_weight, dt_bias, a_log, skip):
    outs = results(*step(
        ends_in[0].reshape(2, T, D), seg_ids, block_counts, in_weight[0], conv_weight[0], conv_bias, pre_gain, gate_gain, out_weight[0], dt_bias, a_log, skip
    ))
    ends_out, d_in, d_taps, d_bias, d_pre, d_gate, d_out, d_dtb, d_alog, d_skip = outs
    return ends_out.reshape(1, 2 * T, D), d_in[None], d_taps[None], d_bias, d_pre, d_gate, d_out[None], d_dtb, d_alog, d_skip


def solution(mesh):
    placed = (
        P("section", "dp", None),
        P("dp", None),
        P("dp"),
        P("section", "dp", None),
        P("section", None, "dp"),
        P("section", "dp"),
        P("section", "dp"),
        P("section", "dp"),
        P("section", "dp", None),
        P("section", None),
        P("section", None),
        P("section", None),
    )
    return jax.shard_map(
        body,
        mesh=mesh,
        in_specs=placed,
        out_specs=(
            P("section", "dp", None),
            P("section", "dp", None),
            P("section", None, "dp"),
            P("section", "dp"),
            P("section", "dp"),
            P("section", "dp"),
            P("section", "dp", None),
            P("section", None),
            P("section", None),
            P("section", None),
        ),
        check_vma=False,
    )
```

```python
import jax
import jax.numpy as jnp
from jax import lax
from jax.experimental import pallas as pl
from jax.experimental.pallas import tpu as pltpu
from jax.sharding import PartitionSpec as P

D = 1536
DI = 3072
N = 128
H = 48
CC = 3328
T = 128
EPSILON = 1e-05
F32 = jnp.float32
BF = jnp.bfloat16
GROUPS = 6
LOG2E = 1.4426950408889634
MESH = pl.DeviceIdType.MESH
KINDS = ((48, 1024), (48, 512), (16, 256))
ORDERS = ((2, 1, 0), (1, 0, 2), (0, 2, 1))
STREAMS = tuple((j, kind) for j in range(3) for kind in range(3))
ALL = (0, 3, 6, 1, 4, 7, 2, 5, 8)
OUT = (1, 4, 7)
REST = (0, 3, 6, 2, 5, 8)


def moved(pos, axis, by):
    out = list(pos)
    out[axis] = lax.rem(pos[axis] + by, 4)
    return tuple(out)


def block_index(order, phase, pos, half, sub=None):
    index = [pos[0], pos[1], pos[2]]
    for a in order[:phase]:
        index[a] = slice(None)
    if phase > 0 and half is not None:
        index[min(order[:phase])] = pl.ds(2 * half, 2) if sub is None else 2 * half + sub
    return tuple(index)


def has_half(kind, phase, half):
    return phase != 0 or half == (0 if kind == 0 else 1)


def dot(a, b, dims=((1,), (0,))):
    return lax.dot_general(a, b, (dims, ((), ())), preferred_element_type=F32)


def sigmoid(v):
    return 1.0 / (1.0 + jnp.exp(-v))


def total(v):
    return jnp.sum(v, axis=0, keepdims=True)


def exact_dot(zeros_ones, wide, dims=((1,), (0,)), flip=False, terms=3):
    out = None
    for _ in range(terms):
        term = wide.astype(BF)
        wide = wide - term.astype(F32)
        part = dot(term, zeros_ones, dims) if flip else dot(zeros_ones, term, dims)
        out = part if out is None else out + part
    return out


def keep_lanes(v, keep):
    return jnp.where(keep, v, jnp.zeros_like(v))


def step_kernel(*refs):
    it = iter(refs)
    take = lambda n: [next(it) for _ in range(n)]
    ends, segs, counts, win, taps_in, bias_in, pre_in, gate_in, wout, dtb_in, alog_in, skip_in = take(12)
    ends_out, d_win, d_wout, d_small = take(4)
    gath, grad, recv2 = take(3), take(3), take(3)
    spill, = take(1)
    wgot, egot, gs, par, hp, gr, hg, sg2, sg1, sg0, swapped, hbuf, us_, os_, dvs, dps, dpes = take(17)
    (s_misc, r_misc, s_ag, r_ag, s_small, r_small, s_sib, r_sib, s_rs, r_rs, s_terms, r_terms, own_sem, go_sem, ready_sem) = take(15)

    section = lax.axis_index("section")
    dp = lax.axis_index("dp")
    pos = (lax.div(dp, 16), lax.rem(lax.div(dp, 4), 4), lax.rem(dp, 4))
    parity = lax.rem(pos[2], 2)
    even = parity == 0
    partner = (pos[0], pos[1], pos[2] + 1 - 2 * parity)
    leading = section == 0

    def device(at, s=None):
        return {"section": section if s is None else s, "dp": at[0] * 16 + at[1] * 4 + at[2]}

    sibling = device(pos, 1 - section)

    def remote(src, dst, s, r, to):
        return pltpu.make_async_remote_copy(src, dst, s, r, device_id=to, device_id_type=MESH)

    def misc(n, src, dst, to):
        return remote(src, dst, s_misc.at[n], r_misc.at[n], to)

    barrier = pltpu.get_barrier_semaphore()
    for axis in range(3):
        for by in (1, 2, 3):
            pl.semaphore_signal(barrier, inc=1, device_id=device(moved(pos, axis, by)), device_id_type=MESH)
    pl.semaphore_signal(barrier, inc=1, device_id=sibling, device_id_type=MESH)

    def group_columns(g):
        return [pl.ds(pl.multiple_of(512 * g + first, 128), 512) for first in (0, DI)]

    def ag_copy(n, phase, slot, src, index, to):
        j, kind = STREAMS[n]
        return remote(src, gath[kind].at[section, j].at[index], s_ag.at[n, phase], r_ag.at[n, phase, slot], device(to))

    def ag_start(n, phase, unit=None):
        j, kind = STREAMS[n]
        order = ORDERS[j]
        right, left = moved(pos, order[phase], 1), moved(pos, order[phase], 3)
        for slot, (h, to) in enumerate(((0, right), (1, left), (1, right), (0, left))):
            if has_half(kind, phase, h):
                index = block_index(order, phase, pos, h)
                src = unit[kind].at[j] if phase == 0 else gath[kind].at[section, j].at[index]
                ag_copy(n, phase, slot, src, index, to).start()

    def ag_pieces(n, phase, at, h):
        order = ORDERS[STREAMS[n][0]]
        if phase < 2:
            return [block_index(order, phase, at, h)]
        return [block_index(order, phase, at, h, q) for q in range(2)]

    def to_sibling(n, index):
        j, kind = STREAMS[n]
        ref = gath[kind].at[section, j].at[index]
        remote(ref, ref, s_sib.at[n], r_sib.at[n], sibling).start()

    def ag_arrived(n, phase, slot, index, share):
        j, kind = STREAMS[n]
        ag_copy(n, phase, slot, gath[kind].at[section, j].at[index], index, moved(pos, 0, 1)).wait_recv()
        if share:
            to_sibling(n, index)

    def ag_forward(phase, share=False, part=ALL):
        for n in part:
            j, kind = STREAMS[n]
            order = ORDERS[j]
            right, left = moved(pos, order[phase], 1), moved(pos, order[phase], 3)
            for slot, h, source, to in ((0, 0, left, right), (1, 1, right, left)):
                if has_half(kind, phase, h):
                    ag_arrived(n, phase, slot, block_index(order, phase, source, h), share)
                    for q, index in enumerate(ag_pieces(n, phase, source, h)):
                        ag_copy(n, phase, 4 + 2 * slot + q, gath[kind].at[section, j].at[index], index, to).start()

    def ag_rest(phase, share=False, part=ALL):
        for n in part:
            j, kind = STREAMS[n]
            order = ORDERS[j]
            right, left = moved(pos, order[phase], 1), moved(pos, order[phase], 3)
            for slot, h, source in ((2, 1, left), (3, 0, right)):
                if has_half(kind, phase, h):
                    ag_arrived(n, phase, slot, block_index(order, phase, source, h), share)
        for q in range(2 if phase == 2 else 1):
            for n in part:
                j, kind = STREAMS[n]
                far = moved(pos, ORDERS[j][phase], 2)
                for slot in (0, 1):
                    if has_half(kind, phase, slot):
                        ag_arrived(n, phase, 4 + 2 * slot + q, ag_pieces(n, phase, far, slot)[q], share)

    def ag_sent(phase):
        for n, (j, kind) in enumerate(STREAMS):
            index = {0: (0, 0, pl.ds(0, 3)), 1: (0, pl.ds(0, 3)), 2: (pl.ds(0, 3),)}[phase]
            ref = gath[kind].at[section, j].at[index]
            remote(ref, ref, s_ag.at[n, phase], r_ag.at[n, phase, 0], sibling).wait_send()

    def small_gather(phase):
        axis = (2, 1, 0)[phase]
        index = tuple(pos[: 3 - phase])
        sent = []
        for by in (1, 2, 3):
            ref = gs.at[section].at[index]
            c = remote(ref, ref, s_small.at[phase, by - 1], r_small.at[phase, by - 1], device(moved(pos, axis, by)))
            c.start()
            sent.append(c)
        return sent

    trailing = jnp.logical_not(leading)
    cotangent_0 = misc(2, ends.at[0], swapped, sibling)
    small_across = misc(3, gs.at[section], gs.at[section], sibling)

    def prologue(wsend, esend, uw, uo, ue, us):
        unit = (uw, uo, ue)
        bc = win[:, 2 * DI : 2 * DI + 2 * N].astype(F32)
        rz = jnp.concatenate([win[:, 2 * DI + 2 * N :].astype(F32), jnp.zeros((24, 2 * N - H), F32)], axis=1)
        for j in range(3):
            for i, at in enumerate(group_columns(2 * j + 1 - parity)):
                wsend[j, :, 512 * i : 512 * i + 512] = win[:, at]
        esend[...] = jnp.where(even, rz, bc).astype(BF)
        us[...] = jnp.zeros((8, 128), F32)
        us[0:4, 0:52] = taps_in[...].astype(F32)
        us[4:5, 0:52] = bias_in[...].astype(F32)
        us[5:6, 0:24] = pre_in[...].astype(F32)
        us[6:7, 0:48] = gate_in[...].astype(F32)
        us[7:8, 0:48] = dtb_in[...].astype(F32)
        us[5:6, 64:112] = alog_in[...].astype(F32)
        us[6:7, 64:112] = skip_in[...].astype(F32)
        gs[section, pos[0], pos[1], pos[2]] = us[...]
        for j in range(3):
            uo[j] = wout[:, 512 * j : 512 * j + 512]

        pl.semaphore_wait(barrier, 10)
        swap_w = misc(0, wsend, wgot, device(partner))
        swap_e = misc(1, esend, egot, device(partner))
        swap_w.start()
        swap_e.start()

        @pl.when(trailing)
        def _():
            cotangent_0.start()


        def first_phase(part):
            copies = []
            for n in part:
                j, kind = STREAMS[n]
                ag_start(n, 0, unit)
                c = pltpu.make_async_copy(unit[kind].at[j], gath[kind].at[section, j].at[pos], own_sem.at[n])
                c.start()
                copies.append(c)
            return copies

        small = small_gather(0)
        own = first_phase(OUT)
        swap_w.wait()
        swap_e.wait()
        for j in range(3):
            for i, at in enumerate(group_columns(2 * j + parity)):
                lanes = slice(512 * i, 512 * i + 512)
                mine, theirs = win[:, at].astype(F32), wgot[j, :, lanes].astype(F32)
                uw[j, :, lanes] = jnp.concatenate([jnp.where(even, mine, theirs), jnp.where(even, theirs, mine)], axis=0).astype(BF)
        mine, theirs = jnp.where(even, bc, rz), egot[...].astype(F32)
        both = jnp.concatenate([jnp.where(even, mine, theirs), jnp.where(even, theirs, mine)], axis=0).astype(BF)
        for j in range(3):
            ue[j] = both[16 * j : 16 * j + 16, :]
        own_rest = first_phase(REST)
        for c in small:
            c.wait()
        small = small_gather(1)
        ag_forward(0, part=OUT)
        for c in own:
            c.wait()
        ag_rest(0, part=OUT)
        for n in OUT:
            ag_start(n, 1)
        ag_forward(0, part=REST)
        for c in small:
            c.wait()
        small = small_gather(2)
        for c in own_rest:
            c.wait()
        ag_rest(0, part=REST)

        @pl.when(leading)
        def _():
            for n in REST:
                ag_start(n, 1)

        for c in small:
            c.wait()
        small_across.start()
        ag_forward(1, part=OUT)
        ag_rest(1, part=OUT)

        @pl.when(leading)
        def _():
            for n in OUT:
                ag_start(n, 2)

        ag_sent(0)

    pl.run_scoped(
        prologue,
        pltpu.VMEM((3, 24, 1024), BF), pltpu.VMEM((24, 256), BF), pltpu.VMEM((3, 48, 1024), BF), pltpu.VMEM((3, 48, 512), BF), pltpu.VMEM((3, 16, 256), BF), pltpu.VMEM((8, 128), F32),
    )

    def own_across():
        for n, (j, kind) in enumerate(STREAMS):
            to_sibling(n, block_index(ORDERS[j], 2, pos, None))

    misc(3, gs.at[1 - section], gs.at[1 - section], sibling).wait()
    for l in range(2):
        hp[l] = gs[l, 0, 0, 0]
        for i in range(64):
            tile = gs.at[l, i // 16, i // 4 % 4, i % 4]
            par[l, 0:5, 52 * i : 52 * i + 52] = tile[0:5, 0:52]
            par[l, 7:8, 24 * i : 24 * i + 24] = tile[5:6, 0:24]
            par[l, 5:6, 48 * i : 48 * i + 48] = tile[6:7, 0:48]
    def from_sibling(l):
        for n, (j, kind) in enumerate(STREAMS):
            ref = gath[kind].at[l, j]
            remote(ref, ref, s_sib.at[n], r_sib.at[n], sibling).wait_recv()

    @pl.when(leading)
    def _():
        ag_forward(1, part=REST)
        ag_rest(1, part=REST)
        for n in REST:
            ag_start(n, 2)
        ag_forward(2)
        pl.semaphore_signal(go_sem, inc=1, device_id=sibling, device_id_type=MESH)
        ag_rest(2)

    @pl.when(trailing)
    def _():
        for n in REST:
            ag_start(n, 1)
        ag_forward(1, part=REST)
        ag_rest(1, part=REST)
        own_across()
        pl.semaphore_wait(go_sem, 1)
        for n in ALL:
            ag_start(n, 2)

    landing = {}

    def rs_copy(n, phase, slot, src, to):
        j, kind = STREAMS[n]
        if phase == 2 and slot >= 4:
            dst = landing[2, kind].at[j, slot - 4]
        elif phase == 2:
            dst = recv2[kind].at[j, slot]
        else:
            dst = landing[phase, kind].at[j, slot if phase == 1 else slot // 2]
        return remote(src, dst, s_rs.at[n, phase], r_rs.at[n, phase, slot], device(to))

    def rs_start(n, phase, part):
        j, kind = STREAMS[n]
        axis = ORDERS[j][phase]
        right, left, far = (moved(pos, axis, by) for by in (1, 3, 2))
        for slot, at, h, to in ((0, far, 0, left), (1, far, 1, right), (2, left, 1, left), (3, right, 0, right)):
            if has_half(kind, phase, h):
                rs_copy(n, phase, slot, part(n, at[axis], h), to).start()

    def grad_part(n, k, h):
        j, kind = STREAMS[n]
        at = list(pos)
        at[ORDERS[j][2]] = k
        return grad[kind].at[(j,) + block_index(ORDERS[j], 2, tuple(at), h)]

    def term(n, src, dst):
        return remote(src, dst, s_terms.at[n], r_terms.at[n], sibling)

    def dterm(g):
        return term(3 + g, dps.at[12 + lax.rem(g, 2)], dps.at[6 + g])

    def layers(wbuf, ebuf, obuf, zbuf, xbuf, ybuf, tbuf, pebuf, masks, coef, allowed, tri, sel, qcol, qrow, dtrow, heads, smat, gbuf, dgacc, rowq, rowx, acc, rbuf, ut, ot, wsem, esem, osem, gsem, psem):
        def copy_w(l, g):
            j, p = lax.div(g, 2), lax.rem(g, 2)
            return [pltpu.make_async_copy(gath[0].at[l, j, :, :, 2 * m + p], wbuf.at[g, :, :, pl.ds(48 * m, 48)], wsem.at[g, m]) for m in range(2)]

        def copy_e(l):
            return [pltpu.make_async_copy(gath[2].at[l, j, :, :, 2 * m + p], ebuf.at[p, :, :, m, j], esem.at[p, m, j]) for p in range(2) for m in range(2) for j in range(3)]

        def copy_o(l, j):
            return [pltpu.make_async_copy(gath[1].at[l, j], obuf.at[j], osem.at[j])]

        def start(copies):
            for c in copies:
                c.start()

        def finish(copies):
            for c in copies:
                c.wait()

        def weights_e(p):
            return ebuf[p].reshape(D, 256)

        def start_all(l):
            start(copy_e(l))
            for g in range(GROUPS):
                start(copy_w(l, jnp.int32(g)))
            for j in range(3):
                start(copy_o(l, j))

        @pl.when(leading)
        def _():
            start_all(0)

        rows = lax.broadcasted_iota(jnp.int32, (T, T), 0)
        cols = lax.broadcasted_iota(jnp.int32, (T, T), 1)
        def set_block(b):
            seg = jnp.where(b == 0, segs[0:1, :], segs[1:2, :]).astype(F32)
            seg_s = jnp.broadcast_to(seg, (T, T))
            seg_t = jnp.transpose(seg_s)
            allowed[...] = jnp.where(rows >= cols, jnp.where(seg_t == seg_s, 1.0, 0.0), 0.0)
            for d in (1, 2, 3):
                masks[d - 1] = jnp.where(rows >= d, jnp.where(pltpu.roll(seg_t, d, 0) == seg_t, 1.0, 0.0), 0.0)
            masks[3] = jnp.where(rows < counts[b], 1.0, 0.0)

        tri[...] = jnp.where(rows >= cols, 1.0, 0.0).astype(BF)
        srow = lax.broadcasted_iota(jnp.int32, (512, T), 0)
        scol = lax.broadcasted_iota(jnp.int32, (512, T), 1)
        sel[...] = jnp.where(lax.div(srow, 64) == scol, 1.0, 0.0).astype(BF)
        low_lanes = cols < 64
        for l in range(2):
            skips = hp[l, 6:7, 64:112]
            skips = jnp.concatenate([skips, jnp.zeros((1, 80), F32)], axis=1)
            skips = jnp.broadcast_to(skips, (8, T))
            for g in range(GROUPS):
                mine = skips if g == 0 else pltpu.roll(skips, T - 8 * g, 1)
                mine = jnp.where(cols[0:8] < 8, mine, 0.0)
                par[l, 6:7, 512 * g : 512 * g + 512] = dot(mine.astype(BF), sel[...], ((1,), (1,)))[0:1]

        def conv(px, taps, bias):
            s1 = pltpu.roll(px, 1, 0) * masks[0]
            s2 = pltpu.roll(px, 2, 0) * masks[1]
            s3 = pltpu.roll(px, 3, 0) * masks[2]
            c = bias + taps[3:4] * px + taps[2:3] * s1 + taps[1:2] * s2 + taps[0:1] * s3
            return c, (s3, s2, s1, px)

        def conv_back(dc, taps):
            out = taps[3:4] * dc
            out = out + taps[2:3] * pltpu.roll(dc * masks[0], T - 1, 0)
            out = out + taps[1:2] * pltpu.roll(dc * masks[1], T - 2, 0)
            return out + taps[0:1] * pltpu.roll(dc * masks[2], T - 3, 0)

        def decay(g, hh):
            gap = jnp.broadcast_to(qcol[g][:, hh : hh + 1], (T, T)) - qrow[g][hh : hh + 1, :]
            return jnp.exp2(jnp.minimum(gap, 0.0)) * dtrow[g][hh : hh + 1, :]

        def rate_bias(l):
            return hp[l, 7:8, :]

        def rate(l):
            tile = pltpu.roll(hp[l], 64, 1)
            return -jnp.exp(jnp.where(cols[0:1] < H, tile[5:6, :], 0.0))

        def tile_at(g, k):
            return pl.ds(pl.multiple_of(512 * g + 128 * k, 128), 128)

        def prepare(s):
            q = heads[s, 1]
            qt = jnp.transpose(q)
            dtt = jnp.transpose(heads[s, 0])
            for g in range(GROUPS):
                qcol[g] = q if g == 0 else pltpu.roll(q, T - 8 * g, 1)
                qrow[g] = qt[8 * g : 8 * g + 8, :]
                dtrow[g] = dtt[8 * g : 8 * g + 8, :]

        def when_first(first, fn):
            if first is True:
                fn()
            else:
                pl.when(first)(fn)

        def forward(l, h, s, z, b, sl, first):
            set_block(b)
            rs = lax.rsqrt(jnp.sum(h * h, axis=1, keepdims=True) * (1.0 / D) + EPSILON)
            rbuf[s, 0] = jnp.broadcast_to(rs, (T, T))
            us_[sl] = (h * rs * par[l, 7:8, 0:D] * masks[3][:, 0:1]).astype(BF)
            when_first(first, lambda: finish(copy_e(l)))
            pebuf[s, :, 0:256] = dot(us_[sl], weights_e(0))
            pebuf[s, :, 256:384] = dot(us_[sl], weights_e(1))[:, 0:128]
            for j in range(2):
                at = slice(DI + 128 * j, DI + 128 * j + 128)
                c, _ = conv(pebuf[s, :, 128 * j : 128 * j + 128], par[l, 0:4, at], par[l, 4:5, at])
                smat[s, j] = (c * sigmoid(c)).astype(BF)
            v = pebuf[s, :, 256:384] + rate_bias(l)
            dt = jnp.maximum(v, 0.0) + jnp.log1p(jnp.exp(-jnp.abs(v)))
            heads[s, 0] = dt
            heads[s, 1] = exact_dot(tri[...], dt * rate(l)) * LOG2E
            gbuf[s] = dot(smat[s, 1], smat[s, 0], ((1,), (1,))) * allowed[...]
            prepare(s)
            acc[:, 0:128] = jnp.zeros((T, T), F32)

            def group(g, carry):
                when_first(first, lambda: finish(copy_w(l, g)))
                wide = pl.ds(pl.multiple_of(512 * g, 128), 512)
                zbuf[z, :, wide] = dot(us_[sl], wbuf[g, :, :, :, 0:512].reshape(D, 512))
                xbuf[z, :, wide] = dot(us_[sl], wbuf[g, :, :, :, 512:1024].reshape(D, 512))
                for k in range(4):
                    at = tile_at(g, k)
                    c, _ = conv(xbuf[z, :, at], par[l, 0:4, at], par[l, 4:5, at])
                    x = c * sigmoid(c)
                    xb = x.astype(BF)
                    both = jnp.concatenate([keep_lanes(xb, low_lanes), keep_lanes(xb, ~low_lanes)], axis=0)
                    w = jnp.concatenate([(gbuf[s] * decay(g, 2 * k + i)).astype(BF) for i in range(2)], axis=1)
                    y = dot(w, both) + par[l, 6:7, at] * x
                    ybuf[z, :, at] = y
                    zz_ = zbuf[z, :, at]
                    e = y * (zz_ * sigmoid(zz_))
                    tbuf[:, at] = e
                    acc[:, 0:128] += e * e
                return carry

            lax.fori_loop(0, GROUPS, group, 0)
            r = lax.rsqrt(jnp.sum(acc[:, 0:128], axis=1, keepdims=True) * (1.0 / DI) + EPSILON)
            rbuf[s, 1] = jnp.broadcast_to(r, (T, T))
            for g in range(GROUPS):
                at = slice(512 * g, 512 * g + 512)
                os_[sl, :, at] = (tbuf[:, at] * r * par[l, 5:6, at]).astype(BF)
            for j in range(3):
                when_first(first, lambda j=j: finish(copy_o(l, j)))
                acc[:, 512 * j : 512 * j + 512] = dot(os_[sl], obuf[j].reshape(DI, 512))
            return h + acc[...]

        def backward(l, h, dh, s, z, b, sl, gi, first):
            set_block(b)
            if l == 1:
                dvs[sl] = dh.astype(BF)

            if l == 1:
                @pl.when(leading)
                def _():
                    for n, ref in enumerate((us_, os_, dvs)):
                        term(n, ref.at[2], ref.at[1]).start()
            else:
                when_first(first, lambda: [finish(copy_o(0, j)) for j in range(3)] and None)
            acc[:, 0:128] = jnp.zeros((T, T), F32)

            def gated_back(zz, carry):
                wide = pl.ds(pl.multiple_of(768 * zz, 128), 768)
                do = None
                for j in range(3):
                    part = dot(dvs[sl, :, 512 * j : 512 * j + 512], obuf[j, zz].reshape(768, 512), ((1,), (1,)))
                    do = part if do is None else do + part
                tbuf[:, wide] = do
                for k in range(6):
                    at = pl.ds(pl.multiple_of(768 * zz + 128 * k, 128), 128)
                    zz_ = zbuf[z, :, at]
                    e = ybuf[z, :, at] * (zz_ * sigmoid(zz_))
                    prod = tbuf[:, at] * e
                    gr[gi, 5:6, at] = total(prod * rbuf[s, 1])
                    acc[:, 0:128] += prod * par[l, 5:6, at]
                return carry

            lax.fori_loop(0, 4, gated_back, 0)
            if l == 1:
                @pl.when(leading)
                def _():
                    for j in range(3):
                        start(copy_o(0, j))
            r = rbuf[s, 1]
            coef[...] = jnp.broadcast_to(jnp.sum(acc[:, 0:128], axis=1, keepdims=True) * (1.0 / DI), (T, T)) * r * r * r
            prepare(s)
            dgacc[...] = jnp.zeros((T, T), F32)
            rowq[...] = jnp.zeros((T, T), F32)
            rowx[...] = jnp.zeros((T, T), F32)
            acc[...] = jnp.zeros((T, D), F32)

            def second(g, carry):
                if l == 0:
                    when_first(first, lambda: finish(copy_w(0, g)))
                    here = 6 * b + g
                else:
                    here = lax.select(leading, 12 + lax.rem(g, 2), g)

                    @pl.when(jnp.logical_and(leading, g >= 2))
                    def _():
                        dterm(g - 2).wait_send()

                sums_q, sums_x = None, None
                for k in range(4):
                    at = tile_at(g, k)
                    zz_ = zbuf[z, :, at]
                    y = ybuf[z, :, at]
                    sz = sigmoid(zz_)
                    silu = zz_ * sz
                    de = rbuf[s, 1] * (tbuf[:, at] * par[l, 5:6, at]) - (y * silu) * coef[...]
                    dyb = (de * silu).astype(BF)
                    dz = de * y * (sz + silu * (1.0 - sz))
                    dps[here, :, 128 * k : 128 * k + 128] = dz.astype(BF)
                    taps = par[l, 0:4, at]
                    c, shifts = conv(xbuf[z, :, at], taps, par[l, 4:5, at])
                    sc = sigmoid(c)
                    x = c * sc
                    xb = x.astype(BF)
                    dyw = dyb.astype(F32)
                    skip = par[l, 6:7, at]
                    xt = jnp.concatenate([keep_lanes(xb, low_lanes), keep_lanes(xb, ~low_lanes)], axis=0)
                    dyt = jnp.concatenate([keep_lanes(dyb, low_lanes), keep_lanes(dyb, ~low_lanes)], axis=0)
                    dw = dot(dyb, xt, ((1,), (1,)))
                    ws, dg = [], None
                    for i in range(2):
                        e = decay(g, 2 * k + i)
                        ws.append((gbuf[s] * e).astype(BF))
                        part = dw[:, 128 * i : 128 * i + 128] * e
                        dg = part if dg is None else dg + part
                    dgacc[...] += dg
                    dx0 = dot(jnp.concatenate(ws, axis=0), dyt, ((0,), (0,)))
                    dx = dx0 + skip * dyw
                    gr[gi, 6:7, at] = total(dyw * x)
                    one = sel[128 * k : 128 * k + 128, :]
                    part = exact_dot(one, dyw * (y - skip * x), flip=True, terms=2)
                    sums_q = part if sums_q is None else sums_q + part
                    part = exact_dot(one, xb.astype(F32) * dx0, flip=True, terms=2)
                    sums_x = part if sums_x is None else sums_x + part
                    dc = dx * (sc + x * (1.0 - sc))
                    for t in range(4):
                        gr[gi, t : t + 1, at] = total(dc * shifts[t])
                    gr[gi, 4:5, at] = total(dc)
                    dps[here, :, 512 + 128 * k : 640 + 128 * k] = conv_back(dc, taps).astype(BF)
                rowq[...] += pltpu.roll(sums_q, 8 * g, 1)
                rowx[...] += pltpu.roll(sums_x, 8 * g, 1)

                if l == 1:
                    @pl.when(leading)
                    def _():
                        dterm(g).start()

                for zz in range(4):
                    acc[:, 384 * zz : 384 * zz + 384] += dot(dps[here], wbuf[g, zz].reshape(384, 1024), ((1,), (1,)))
                if l == 1:
                    @pl.when(leading)
                    def _():
                        start(copy_w(0, g))
                return carry

            lax.fori_loop(0, GROUPS, second, 0)
            dg = (dgacc[...] * allowed[...]).astype(BF)
            d_states = (dot(dg, smat[s, 1], ((0,), (0,))), dot(dg, smat[s, 0]))
            for j in range(2):
                at = slice(DI + 128 * j, DI + 128 * j + 128)
                taps = par[l, 0:4, at]
                c, shifts = conv(pebuf[s, :, 128 * j : 128 * j + 128], taps, par[l, 4:5, at])
                sc = sigmoid(c)
                dc = d_states[j] * (sc + c * sc * (1.0 - sc))
                for t in range(4):
                    gr[gi, t : t + 1, at] = total(dc * shifts[t])
                gr[gi, 4:5, at] = total(dc)
                dpes[sl, 0, :, 128 * j : 128 * j + 128] = conv_back(dc, taps).astype(BF)
            v = pebuf[s, :, 256:384] + rate_bias(l)
            sv = sigmoid(v)
            dt = heads[s, 0]
            back = exact_dot(tri[...], rowq[...] - rowx[...], ((0,), (0,)))
            ratio = jnp.where(v < -15.0, 1.0, sv / jnp.maximum(dt, 1e-30))
            dr = jnp.where(cols < H, rowx[...] * ratio + back * rate(l) * sv, 0.0)
            d_rate = total(jnp.where(cols < H, back * dt, 0.0)) * rate(l)
            dpes[sl, 1, :, 0:128] = dr.astype(BF)
            dpes[sl, 1, :, 128:256] = jnp.zeros((T, T), BF)

            if l == 1:
                @pl.when(leading)
                def _():
                    term(9, dpes.at[2], dpes.at[1]).start()
            else:
                when_first(first, lambda: finish(copy_e(0)))
            du = acc[...]
            for p in range(2):
                du = du + dot(dpes[sl, p], weights_e(p), ((1,), (1,)))
            if l == 1:
                @pl.when(leading)
                def _():
                    start(copy_e(0))

            hn = h * rbuf[s, 0][:, 0:1]
            du = du * masks[3][:, 0:1]
            gr[gi, 7:8, 0:D] = total(du * hn)
            t = du * par[l, 7:8, 0:D]
            mean = jnp.sum(t * hn, axis=1, keepdims=True) * (1.0 / D)
            dh_in = dh + rbuf[s, 0][:, 0:1] * (t - hn * mean)
            hg[gi, 0:1] = total(dr)
            hg[gi, 1:2] = d_rate
            return dh_in

        def small_tiles(l):
            skips = jnp.zeros((8, T), F32)
            for g in range(GROUPS):
                mine = exact_dot(sel[...], jnp.broadcast_to(gr[0, 6:7, 512 * g : 512 * g + 512], (8, 512)), flip=True)
                skips = skips + (mine if g == 0 else pltpu.roll(mine, 8 * g, 1))
            for i in range(64):
                tile = gs.at[l, i // 16, i // 4 % 4, i % 4]
                tile[0:5, 0:52] = gr[0, 0:5, 52 * i : 52 * i + 52]
                tile[5:6, 0:24] = gr[0, 7:8, 24 * i : 24 * i + 24]
                tile[6:7, 0:48] = gr[0, 5:6, 48 * i : 48 * i + 48]
                tile[7:8, 0:128] = hg[0, 0:1]
                tile[5:6, 64:112] = hg[0, 1:2, 0:48]
                tile[6:7, 64:112] = skips[0:1, 0:48]

        def products(l):
            if l == 1:
                for n, ref in enumerate((us_, os_, dvs)):
                    term(n, ref.at[2], ref.at[1]).wait_recv()
                for g in range(GROUPS):
                    dterm(g).wait_recv()
                term(9, dpes.at[2], dpes.at[1]).wait_recv()

            def stacked(ref, *index):
                return jnp.concatenate([ref[(0,) + index], ref[(1,) + index]], axis=0)

            def turn(i, carry):
                at = pl.ds(pl.multiple_of(128 * i, 128), 128)
                ut[at, :] = jnp.transpose(stacked(us_, slice(None), at))
                return carry

            lax.fori_loop(0, D // 128, turn, 0)

            for p in range(2):
                for zz in range(4):
                    de = dot(ut[384 * zz : 384 * zz + 384, :], stacked(dpes, p))
                    ebuf[p, zz] = de.astype(BF).reshape(4, 2, 3, 16, 256)
            for p in range(2):
                for m in range(2):
                    for j in range(3):
                        pltpu.make_async_copy(ebuf.at[p, :, :, m, j], grad[2].at[j, :, :, 2 * m + p], gsem.at[j, 2]).start()

            def wstep(i, carry):
                g, zz = lax.div(i, 4), lax.rem(i, 4)
                u = ut[pl.ds(pl.multiple_of(384 * zz, 128), 384), :]
                for half in range(2):
                    at = slice(512 * half, 512 * half + 512)
                    d = jnp.concatenate([dps[g, :, at], dps[6 + g, :, at]], axis=0)
                    wbuf[g, zz, :, :, at] = dot(u, d).astype(BF).reshape(4, 96, 512)
                j, p = lax.div(g, 2), lax.rem(g, 2)
                for m in range(2):
                    pltpu.make_async_copy(wbuf.at[g, zz, :, pl.ds(48 * m, 48)], grad[0].at[j, zz, :, 2 * m + p], gsem.at[j, 0]).start()
                return carry

            def ostep(zz, carry):
                for i in range(6):
                    at = pl.ds(pl.multiple_of(768 * zz + 128 * i, 128), 128)
                    ot[128 * i : 128 * i + 128, :] = jnp.transpose(stacked(os_, slice(None), at))
                for j in range(3):
                    d = stacked(dvs, slice(None), slice(512 * j, 512 * j + 512))
                    for half in range(2):
                        o = ot[384 * half : 384 * half + 384, :]
                        obuf[j, zz, 2 * half : 2 * half + 2] = dot(o, d).astype(BF).reshape(2, 4, 48, 512)
                    pltpu.make_async_copy(obuf.at[j, zz], grad[1].at[j, zz], gsem.at[j, 1]).start()
                return carry

            def written(j, kind):
                pltpu.make_async_copy(grad[kind].at[j], grad[kind].at[j], gsem.at[j, kind]).wait()
                rs_start(3 * j + kind, 2, grad_part)

            for j in range(3):
                lax.fori_loop(8 * j, 8 * j + 8, wstep, 0)
                if j > 0:
                    written(j - 1, 0)
            lax.fori_loop(0, 4, ostep, 0)
            written(2, 0)
            for kind in (1, 2):
                for j in range(3):
                    written(j, kind)

        middle_1 = misc(7, dvs.at[0], hbuf, sibling)
        out_0 = misc(4, ends_out.at[0], ends_out.at[0], sibling)
        d_middle_1 = misc(8, dvs.at[2], dvs.at[1], sibling)
        sets = [pltpu.make_async_copy(ref.at[0], spill.at[n], psem.at[n]) for n, ref in enumerate((zbuf, xbuf, ybuf))]
        sets_back = [pltpu.make_async_copy(spill.at[n], ref.at[0], psem.at[n]) for n, ref in enumerate((zbuf, xbuf, ybuf))]

        @pl.when(leading)
        def _():
            def block(b, carry):
                out = forward(0, ends[b].astype(F32), b, b, b, b, b == 0).astype(BF)

                @pl.when(b == 0)
                def _():
                    hbuf[...] = out
                    start(sets)

                @pl.when(b == 1)
                def _():
                    dvs[0] = out
                    middle_1.start()

                return carry

            lax.fori_loop(0, 2, block, 0)
            finish(sets)
            cotangent_0.wait_recv()
            from_sibling(1)

        @pl.when(trailing)
        def _():
            ag_forward(2, True)
            ag_rest(2, True)
            cotangent_0.wait_send()
            middle_1.wait_recv()

        start_all(1)
        out = forward(1, hbuf[...].astype(F32), 2, 0, section, lax.select(leading, 2, 0), True).astype(BF)

        @pl.when(leading)
        def _():
            ends_out[0] = out
            out_0.start()

        @pl.when(trailing)
        def _():
            ends_out[1] = out

        cotangent = jnp.where(leading, swapped[...].astype(F32), ends[1].astype(F32))
        d_middle = backward(1, hbuf[...].astype(F32), cotangent, 2, 0, section, lax.select(leading, 2, 0), 0, True).astype(BF)

        @pl.when(trailing)
        def _():
            dvs[2] = d_middle
            d_middle_1.start()
            small_tiles(1)
            products(1)
            d_middle_1.wait_send()
            out_0.wait_recv()

        @pl.when(leading)
        def _():
            start(sets_back)
            middle_1.wait_send()
            dvs[0] = d_middle
            small_tiles(1)
            term(10, gs.at[1], gs.at[0]).start()
            out_0.wait_send()
            d_middle_1.wait_recv()

            def block(i, carry):
                b = 1 - i

                @pl.when(i == 1)
                def _():
                    finish(sets_back)

                ends_out[b] = backward(0, ends[b].astype(F32), dvs[b].astype(F32), b, b, b, b, i, i == 0).astype(BF)
                return carry

            lax.fori_loop(0, 2, block, 0)
            gr[0] += gr[1]
            hg[0] += hg[1]
            small_tiles(0)
            products(0)

    V = pltpu.VMEM
    pl.run_scoped(
        layers,
        V((6, 4, 4, 96, 1024), BF), V((2, 4, 4, 2, 3, 16, 256), BF), V((3, 4, 4, 4, 48, 512), BF),
        V((2, T, DI), F32), V((2, T, DI), F32), V((2, T, DI), F32), V((T, DI), F32), V((3, T, 384), F32),
        V((4, T, T), F32), V((T, T), F32), V((T, T), F32), V((T, T), BF), V((512, T), BF), V((6, T, T), F32), V((6, 8, T), F32), V((6, 8, T), F32),
        V((3, 2, T, T), F32), V((3, 2, T, T), BF), V((3, T, T), F32), V((T, T), F32), V((T, T), F32), V((T, T), F32), V((T, D), F32), V((3, 2, T, T), F32),
        V((D, 256), BF), V((768, 256), BF),
        pltpu.SemaphoreType.DMA((6, 2)), pltpu.SemaphoreType.DMA((2, 2, 3)), pltpu.SemaphoreType.DMA((3,)), pltpu.SemaphoreType.DMA((3, 3)), pltpu.SemaphoreType.DMA((3,)),
    )

    def sums(*bufs):
        it = iter(bufs)
        take = lambda n: [next(it) for _ in range(n)]
        ab, ob, db, eb, acc2, acc1, b1, b0, fin = (take(3) for _ in range(9))
        fsend, gsend, fgot, ggot, sa2, sa1, lsem = it
        for kind in range(3):
            landing[2, kind], landing[1, kind], landing[0, kind] = eb[kind], b1[kind], b0[kind]
        for axis in range(3):
            for by in (1, 3):
                pl.semaphore_signal(ready_sem, inc=1, device_id=device(moved(pos, axis, by)), device_id_type=MESH)

        def load(n, h, which, src, dst):
            return pltpu.make_async_copy(src, dst, lsem.at[n, h, which])

        def add(dst, parts, dims, dtype, place=None):
            if not dims:
                out = parts[0][...].astype(F32)
                for p in parts[1:]:
                    out = out + p[...].astype(F32)
                dst[...] = out.astype(dtype)
                return
            count = dims[0] * (dims[1] if len(dims) > 1 else 1)

            def one(i, carry):
                index = (i,) if len(dims) == 1 else (lax.div(i, dims[1]), lax.rem(i, dims[1]))
                out = parts[0][index].astype(F32)
                for p in parts[1:]:
                    out = out + p[index].astype(F32)
                dst[index if place is None else place(*index)] = out.astype(dtype)
                return carry

            lax.fori_loop(0, count, one, 0)

        def neighbours(n, phase):
            axis = ORDERS[STREAMS[n][0]][phase]
            right, left = moved(pos, axis, 1), moved(pos, axis, 3)
            return pos[axis], {0: (0, left[axis], left, 4, 3), 1: (1, right[axis], right, 5, 2)}

        def sent(phase):
            for n, (j, kind) in enumerate(STREAMS):
                if phase == 2:
                    ref = grad[kind].at[j, pl.ds(0, 3)]
                else:
                    ref = landing[phase, kind].at[j, pl.ds(0, 3 if phase == 0 else 6)]
                remote(ref, ref, s_rs.at[n, phase], r_rs.at[n, phase, 0], sibling).wait_send()

        items = {phase: [(3 * j + kind, h) for kind in range(3) for j in range(3) for h in (0, 1) if has_half(kind, phase, h)] for phase in range(3)}


        def small_start(phase):
            axis = ORDERS[0][phase]
            cur = (sa1, sa2, gs.at[section])[phase]
            got = (sg0, sg1, sg2)[phase]
            copies = []
            for by in (1, 2, 3):
                to = moved(pos, axis, by)
                c = remote(cur.at[to[axis]], got.at[by - 1], s_small.at[3 + phase, by - 1], r_small.at[3 + phase, by - 1], device(to))
                c.start()
                copies.append(c)

            def done():
                for c in copies:
                    c.wait()
                out = cur[pos[axis]] + got[0] + got[1] + got[2]
                if phase == 0:
                    return out
                (sa1, sa2)[phase - 1][...] = out
                return None

            return done

        @pl.when(trailing)
        def _():
            term(10, gs.at[1], gs.at[0]).wait_recv()
            gs[1] += gs[0]

        for n, h in items[2]:
            j, kind = STREAMS[n]
            _, halves = neighbours(n, 2)
            load(n, h, 0, grad_part(n, halves[h][1], h), ob[kind].at[j, h]).start()
        for n, h in items[2]:
            j, kind = STREAMS[n]
            slot = neighbours(n, 2)[1][h][0]
            rs_copy(n, 2, slot, ab[kind].at[j, h], moved(pos, 0, 1)).wait_recv()
            load(n, h, 1, recv2[kind].at[j, slot], ab[kind].at[j, h]).start()
        pl.semaphore_wait(ready_sem, 6)
        done = small_start(2)
        for n, h in items[2]:
            j, kind = STREAMS[n]
            here, halves = neighbours(n, 2)
            _, block, to, slot, _ = halves[h]
            load(n, h, 0, grad_part(n, block, h), ob[kind].at[j, h]).wait()
            load(n, h, 1, recv2[kind].at[j, 0], ab[kind].at[j, h]).wait()
            add(ab[kind].at[j, h], [ab[kind].at[j, h], ob[kind].at[j, h]], (2, 4), BF)
            rs_copy(n, 2, slot, ab[kind].at[j, h], to).start()
            load(n, h, 0, grad_part(n, here, h), ob[kind].at[j, h]).start()
        done()
        for n, h in items[2]:
            j, kind = STREAMS[n]
            slot = neighbours(n, 2)[1][h][4]
            rs_copy(n, 2, slot, ab[kind].at[j, h], moved(pos, 0, 1)).wait_recv()
            load(n, h, 2, recv2[kind].at[j, slot], db[kind].at[j, h]).start()

        def last2(n, h):
            j, kind = STREAMS[n]
            order = ORDERS[j]
            low = min(order[:2])
            load(n, h, 0, grad_part(n, 0, h), ob[kind].at[j, h]).wait()
            load(n, h, 2, recv2[kind].at[j, 0], db[kind].at[j, h]).wait()
            place = (lambda a, b: (j, 2 * h + a, b)) if order[1] == low else (lambda a, b: (j, b, 2 * h + a))
            add(acc2[kind], [ob[kind].at[j, h], db[kind].at[j, h], eb[kind].at[j, h]], (2, 4), BF, place)

        def part_of(phase):
            def part(n, k, h):
                j, kind = STREAMS[n]
                return acc2[kind].at[j, k, pl.ds(2 * h, 2)] if phase == 1 else acc1[kind].at[j, k]

            return part

        def arrived(n, phase, slot):
            j, kind = STREAMS[n]
            ref = landing[phase, kind].at[j, {2: slot - 4, 1: slot, 0: slot // 2}[phase]]
            rs_copy(n, phase, slot, ref, moved(pos, 0, 1)).wait_recv()
            return ref

        def phase_2_last(kind):
            for n, h in items[2]:
                if STREAMS[n][1] == kind:
                    arrived(n, 2, neighbours(n, 2)[1][h][3])
                    last2(n, h)
                    if h == 1:
                        rs_start(n, 1, part_of(1))

        def first(phase, kind):
            for n, h in items[phase]:
                if STREAMS[n][1] == kind:
                    slot, block, to, summed, _ = neighbours(n, phase)[1][h]
                    ref = arrived(n, phase, slot)
                    add(ref, [ref, part_of(phase)(n, block, h)], (2,) if phase == 1 else (), BF)
                    rs_copy(n, phase, summed, ref, to).start()

        def last(phase, kind):
            for n, h in items[phase]:
                j, own_kind = STREAMS[n]
                if own_kind == kind:
                    here, halves = neighbours(n, phase)
                    parts = [part_of(phase)(n, here, h), arrived(n, phase, halves[h][4]), arrived(n, phase, halves[h][3])]
                    if phase == 0:
                        add(fin[kind].at[j], parts, (), F32)
                    else:
                        add(acc1[kind], parts, (2,), BF, lambda a: (j, 2 * h + a))
                        if h == 1:
                            rs_start(n, 0, part_of(0))

        phase_2_last(0)
        done = small_start(1)
        phase_2_last(1)
        first(1, 0)
        phase_2_last(2)
        first(1, 1)
        last(1, 0)
        done()
        done = small_start(0)
        first(1, 2)
        last(1, 1)
        first(0, 0)
        last(1, 2)
        first(0, 1)
        last(0, 0)
        for j in range(3):
            fsend[j] = jnp.where(even, fin[0][j, 24:48, :], fin[0][j, 0:24, :])
        swap_f = misc(5, fsend, fgot, device(partner))
        swap_f.start()
        first(0, 2)
        last(0, 1)
        last(0, 2)
        last_tile = done()

        last_e = jnp.concatenate([fin[2][j] for j in range(3)], axis=0)
        gsend[...] = jnp.where(even, last_e[24:48], last_e[0:24])
        swap_g = misc(6, gsend, ggot, device(partner))
        swap_g.start()
        for j in range(3):
            for i, at in enumerate(group_columns(2 * j + parity)):
                lanes = slice(512 * i, 512 * i + 512)
                d_win[:, at] = jnp.where(even, fin[0][j, 0:24, lanes], fin[0][j, 24:48, lanes])
            d_wout[:, 512 * j : 512 * j + 512] = fin[1][j]
        d_small[...] = last_tile
        swap_f.wait()
        swap_g.wait()
        for j in range(3):
            for i, at in enumerate(group_columns(2 * j + 1 - parity)):
                d_win[:, at] = fgot[j, :, 512 * i : 512 * i + 512]
        mine, theirs = jnp.where(even, last_e[0:24], last_e[24:48]), ggot[...]
        d_win[:, 2 * DI : 2 * DI + 2 * N] = jnp.where(even, mine, theirs)
        d_win[:, 2 * DI + 2 * N :] = jnp.where(even, theirs, mine)[:, 0:H]
        for phase in range(3):
            sent(phase)

    shapes = []
    for lead, dtype in (((3, 2, 2, 4), BF),) * 4 + (((3, 4, 4), BF), ((3, 4), BF), ((3, 6, 2), BF), ((3, 3), BF), ((3,), F32)):
        shapes += [V(lead + dims, dtype) for dims in KINDS]
    shapes += [V((3, 24, 1024), F32), V((24, 256), F32)] * 2 + [V((4, 4, 8, 128), F32), V((4, 8, 128), F32)]
    pl.run_scoped(sums, *shapes, pltpu.SemaphoreType.DMA((9, 2, 4)))

    @pl.when(trailing)
    def _():
        for n, (j, kind) in enumerate(STREAMS):
            ref = gath[kind].at[1, j]
            remote(ref, ref, s_sib.at[n], r_sib.at[n], sibling).wait_send()

    @pl.when(leading)
    def _():
        for n, ref in enumerate((us_, os_, dvs)):
            term(n, ref.at[2], ref.at[1]).wait_send()
        for g in (4, 5):
            dterm(g).wait_send()
        term(9, dpes.at[2], dpes.at[1]).wait_send()
        term(10, gs.at[1], gs.at[0]).wait_send()

    ag_sent(1)
    ag_sent(2)


def step(ends, segs, counts, win, taps, bias, pre, gate, wout, dtb, alog, skip):
    vm = pl.BlockSpec(memory_space=pltpu.VMEM)
    any_ = pl.BlockSpec(memory_space=pl.ANY)
    s = jax.ShapeDtypeStruct
    V, S = pltpu.VMEM, pltpu.SemaphoreType.DMA
    large = []
    for lead in ((2, 3, 4, 4, 4), (3, 4, 4, 4), (3, 4, 2, 4)):
        large += [s(lead + dims, BF) for dims in KINDS]
    return pl.pallas_call(
        step_kernel,
        out_shape=[
            s((2, T, D), BF), s((24, 6448), F32), s((48, D), F32), s((8, 128), F32),
        ] + large + [s((3, T, DI), F32)],
        in_specs=[vm, vm, pl.BlockSpec(memory_space=pltpu.SMEM)] + [vm] * 9,
        out_specs=[vm] * 4 + [any_] * 10,
        scratch_shapes=[
            V((3, 24, 1024), BF), V((24, 256), BF), V((2, 4, 4, 4, 8, 128), F32),
            V((2, 8, CC), F32), V((2, 8, 128), F32), V((2, 8, CC), F32), V((2, 8, 128), F32),
            V((3, 4, 4, 8, 128), F32), V((3, 4, 8, 128), F32), V((3, 8, 128), F32),
            V((T, D), BF), V((T, D), BF), V((3, T, D), BF), V((3, T, DI), BF), V((3, T, D), BF), V((14, T, 1024), BF), V((3, 2, T, 256), BF),
            S((9,)), S((9,)), S((9, 3)), S((9, 3, 8)), S((6, 3)), S((6, 3)), S((9,)), S((9,)), S((9, 3)), S((9, 3, 6)), S((11,)), S((11,)), S((9,)),
            pltpu.SemaphoreType.REGULAR, pltpu.SemaphoreType.REGULAR,
        ],
        compiler_params=pltpu.CompilerParams(collective_id=0, has_side_effects=True, vmem_limit_bytes=65280 * 1024),
        name="train_step",
    )(ends, segs, counts, win, taps, bias, pre, gate, wout, dtb, alog, skip)[:4]


def results_kernel(ends, win, wout, tile, ends_out, d_win, d_taps, d_bias, d_pre, d_gate, d_wout, d_dtb, d_alog, d_skip):
    ends_out[...] = ends[...]
    d_win[...] = win[...]
    d_wout[...] = wout[...]
    d_taps[...] = tile[0:4, 0:52]
    d_bias[...] = tile[4:5, 0:52]
    d_pre[...] = tile[5:6, 0:24]
    d_gate[...] = tile[6:7, 0:48]
    d_dtb[...] = tile[7:8, 0:48]
    d_alog[...] = tile[5:6, 64:112]
    d_skip[...] = tile[6:7, 64:112]


def results(ends, win, wout, tile):
    vm = pl.BlockSpec(memory_space=pltpu.VMEM)
    s = jax.ShapeDtypeStruct
    return pl.pallas_call(
        results_kernel,
        out_shape=[
            s((2, T, D), BF), s((24, 6448), F32), s((4, 52), F32), s((1, 52), F32), s((1, 24), F32), s((1, 48), F32), s((48, D), F32),
            s((1, H), F32), s((1, H), F32), s((1, H), F32),
        ],
        in_specs=[vm] * 4,
        out_specs=[vm] * 10,
        name="results",
    )(ends, win, wout, tile)


def body(ends_in, seg_ids, block_counts, in_weight, conv_weight, conv_bias, pre_gain, gate_gain, out_weight, dt_bias, a_log, skip):
    outs = results(*step(
        ends_in[0].reshape(2, T, D), seg_ids, block_counts, in_weight[0], conv_weight[0], conv_bias, pre_gain, gate_gain, out_weight[0], dt_bias, a_log, skip
    ))
    ends_out, d_in, d_taps, d_bias, d_pre, d_gate, d_out, d_dtb, d_alog, d_skip = outs
    return ends_out.reshape(1, 2 * T, D), d_in[None], d_taps[None], d_bias, d_pre, d_gate, d_out[None], d_dtb, d_alog, d_skip


def solution(mesh):
    placed = (
        P("section", "dp", None),
        P("dp", None),
        P("dp"),
        P("section", "dp", None),
        P("section", None, "dp"),
        P("section", "dp"),
        P("section", "dp"),
        P("section", "dp"),
        P("section", "dp", None),
        P("section", None),
        P("section", None),
        P("section", None),
    )
    return jax.shard_map(
        body,
        mesh=mesh,
        in_specs=placed,
        out_specs=(
            P("section", "dp", None),
            P("section", "dp", None),
            P("section", None, "dp"),
            P("section", "dp"),
            P("section", "dp"),
            P("section", "dp"),
            P("section", "dp", None),
            P("section", None),
            P("section", None),
            P("section", None),
        ),
        check_vma=False,
    )
```
